32 devices in a mesh: head: 4 (over y, core), blk: 8 (over z, x).
Axes of the slice: x: 2, y: 2, z: 4, core: 2. Of those that a mesh axis runs over, the one named last changes fastest.
Arguments:
- layer_input: bfloat16 [8, 1024, 2048], P('blk', 'head'), may hold values from -6 to 6
- lengths: int32 [1, 5], replicated, may hold values from 1 to 4096, 8192 in all within a row
- ln1_gain: bfloat16 [2048], P(('head', 'blk')), may hold values from 0.25 to 1.75
- ln1_bias: bfloat16 [2048], P(('head', 'blk')), may hold values from -3 to 3
- w_qkv: bfloat16 [2048, 6144], P(('head', 'blk')), may hold values from -0.125 to 0.125
- bias_query: bfloat16 [2048], P(('head', 'blk')), may hold values from -3 to 3
- bias_value: bfloat16 [2048], P(('head', 'blk')), may hold values from -3 to 3
- w_out: bfloat16 [2048, 2048], P(('head', 'blk')), may hold values from -0.5 to 0.5
- bias_out: bfloat16 [2048], P(('head', 'blk')), may hold values from -3 to 3
- ln2_gain: bfloat16 [2048], P(('head', 'blk')), may hold values from 0.25 to 1.75
- ln2_bias: bfloat16 [2048], P(('head', 'blk')), may hold values from -3 to 3
- w_up: bfloat16 [2048, 8192], P(('head', 'blk')), may hold values from -0.125 to 0.125
- bias_up: bfloat16 [8192], P(('head', 'blk')), may hold values from -3 to 3
- w_down: bfloat16 [8192, 2048], P(('head', 'blk')), may hold values from -0.0625 to 0.0625
- bias_down: bfloat16 [2048], P(('head', 'blk')), may hold values from -3 to 3
- cotangent: bfloat16 [8, 1024, 2048], P('blk', 'head'), may hold values from -6 to 6
Outputs:
- layer_out: bfloat16 [8, 1024, 2048], P('blk', 'head')
- grad_input: float32 [8, 1024, 2048], P('blk', 'head')
- grad_ln1_gain: float32 [2048], P(('head', 'blk'))
- grad_ln1_bias: float32 [2048], P(('head', 'blk'))
- grad_w_qkv: float32 [2048, 6144], P(('head', 'blk'))
- grad_bias_query: float32 [2048], P(('head', 'blk'))
- grad_bias_value: float32 [2048], P(('head', 'blk'))
- grad_w_out: float32 [2048, 2048], P(('head', 'blk'))
- grad_bias_out: float32 [2048], P(('head', 'blk'))
- grad_ln2_gain: float32 [2048], P(('head', 'blk'))
- grad_ln2_bias: float32 [2048], P(('head', 'blk'))
- grad_w_up: float32 [2048, 8192], P(('head', 'blk'))
- grad_bias_up: float32 [8192], P(('head', 'blk'))
- grad_w_down: float32 [8192, 2048], P(('head', 'blk'))
- grad_bias_down: float32 [2048], P(('head', 'blk'))
The draws below stay inside these ranges and needn't reach their ends.
Inputs may be any that keep to these rules, and one draw needn't show every extreme that they name: Row s holds the lengths of sequence s's 4 documents in order, then the length of its padding run; each row sums to 8192.
All inputs are finite; a program needn't handle non-finite values.
Results may differ from the reference program's by a relative error of at most 0.018.
Values may be sent and summed in bfloat16 or wider, within the bound.
No kernel may reach another device: no remote copies, remote signals or barrier semaphores. Data moves between devices by JAX's collectives and lax.ppermute only.
A program may use at most 640 MiB of HBM per device.

```python
import math
import jax
import jax.numpy as jnp
import numpy as np
from jax import lax

D = 2048
HEADS = 16
HEAD_DIM = 128
FF = 8192
WINDOW = 1024
SEQ_LEN = 8192
DOCS = 4
BLOCK = 1024
SEQS = 1
DOC_SLOTS = 5
MOST_DOC = 4096
N_BLK = 8


def spiked(drawn, own_key, source, target, parts, factor):
    def block_of(axis_at):
        return (jnp.arange(drawn.shape[axis_at]) // (drawn.shape[axis_at] // parts)).reshape((-1,) + (1,) * (drawn.ndim - 1 - axis_at))

    first = jax.random.permutation(own_key, parts)[block_of(target)]
    other_side = (block_of(target) + parts // 2) % parts
    return jnp.where((block_of(source) == first) | (block_of(source) == other_side), factor * drawn, drawn)


def block_levels(key, shape, split, smallest, high):
    factor_of = 1.0
    for position, parts in split:
        draws = jax.random.uniform(jax.random.fold_in(jax.random.fold_in(key, 6), position), (parts,), jnp.float32, smallest / len(split), high / len(split))
        factor_of = factor_of * jnp.repeat(jnp.exp(draws), shape[position] // parts).reshape((-1,) + (1,) * (len(shape) - 1 - position))
    return factor_of


def profile(number_of, total, reach, lean):
    loads = [(1 << 20) // math.isqrt(standing ** lean) + 1 for standing in range(2, number_of + 1)]
    surplus, holding = total - reach - (number_of - 1), [1] * (number_of - 1)
    while surplus > 0:
        candidates = [i for i in range(number_of - 1) if holding[i] < reach]
        mass, budget = sum([loads[i] for i in candidates]), surplus
        for i in candidates:
            extra = min(reach - holding[i], max(1, budget * loads[i] // mass), surplus)
            holding[i] = holding[i] + extra
            surplus = surplus - extra
    return np.array([reach] + holding)


def ragged_sizes(stream_key, amount, total, reach, slope):
    if amount == 2:
        one = jax.random.randint(stream_key, (), max(1, total - reach), min(reach, total - 1) + 1)
        return jnp.stack([one, total - one])
    sizes = jnp.asarray(profile(amount, total, reach, slope), jnp.int32)
    twos = (amount - 1) // 2
    source_of, sink = sizes[1:1 + 2 * twos:2], sizes[2:2 + 2 * twos:2]
    room = jnp.minimum(source_of - 1, reach - sink)
    moved = jax.random.randint(jax.random.fold_in(stream_key, 1), (twos,), 0, 1 << 20) % (room + 1)
    sizes = sizes.at[1:1 + 2 * twos:2].set(source_of - moved).at[2:2 + 2 * twos:2].set(sink + moved)
    return sizes[jax.random.permutation(jax.random.fold_in(stream_key, 2), amount)]


def noise(rng, shape, width, limit, cuts=(), kind=jnp.bfloat16):
    array = jax.random.normal(rng, shape, jnp.float32) * width
    if len(cuts) > 0:
        array = block_levels(rng, shape, cuts, -0.22, 0.18) * array
    return jnp.clip(array, min=-limit, max=limit).astype(kind)


def noise_with(rng, dims, spread, reach, split, heavy, kind=jnp.bfloat16):
    entries = spread * jax.random.normal(rng, dims, jnp.float32)
    if split:
        entries = entries * block_levels(rng, dims, split, -0.22, 0.18)
    return jnp.clip(spiked(entries, jax.random.fold_in(rng, 3), *heavy), -reach, reach).astype(kind)


def setup_inputs(seed: int = 0) -> dict:
    splits = jax.random.split(jax.random.key(seed), 17)
    return {
        "layer_input": noise(splits[0], (N_BLK, BLOCK, D), 1.0, 6.0, ((0, 8), (1, 4))),
        "lengths": jax.vmap(lambda own: ragged_sizes(own, DOC_SLOTS, SEQ_LEN, MOST_DOC, 2))(jax.random.split(splits[1], SEQS)).reshape((SEQS, DOC_SLOTS)).astype(jnp.int32),
        "ln1_gain": jnp.clip(1.0 + 0.15 * jax.random.normal(splits[2], (D,), jnp.float32), 0.25, 1.75).astype(jnp.bfloat16),
        "ln1_bias": noise(splits[3], (D,), 0.5, 3.0, ((0, 32),)),
        "w_qkv": noise(splits[4], (D, 3 * D), D ** -0.5, 0.125, ((0, 32),)),
        "bias_query": noise(splits[5], (D,), 0.5, 3.0, ((0, 32),)),
        "bias_value": noise(splits[6], (D,), 0.5, 3.0, ((0, 32),)),
        "w_out": noise(splits[7], (D, D), HEAD_DIM ** -0.5, 0.5, ((0, 32),)),
        "bias_out": noise(splits[8], (D,), 0.5, 3.0, ((0, 32),)),
        "ln2_gain": jnp.clip(1.0 + 0.15 * jax.random.normal(splits[9], (D,), jnp.float32), 0.25, 1.75).astype(jnp.bfloat16),
        "ln2_bias": noise(splits[10], (D,), 0.5, 3.0, ((0, 32),)),
        "w_up": noise(splits[11], (D, FF), D ** -0.5, 0.125, ((0, 32),)),
        "bias_up": noise(splits[12], (FF,), 0.5, 3.0, ((0, 32),)),
        "w_down": noise(splits[13], (FF, D), FF ** -0.5, 0.0625, ((0, 32),)),
        "bias_down": noise(splits[14], (D,), 0.5, 3.0, ((0, 32),)),
        "cotangent": noise_with(splits[15], (N_BLK, BLOCK, D), 1.0, 6.0, ((0, 8), (1, 4)), (0, 2, 8, 2.0)),
    }


EPS = 1e-05
NEG = -1e+30

@jax.custom_vjp
def low(v):
    return lax.optimization_barrier(v.astype(jnp.bfloat16)).astype(jnp.float32)

@jax.custom_vjp
def low_back(v):
    return v

def low_keep(v):
    return (low(v), None)

def low_pass(kept, grad):
    return (grad,)

def back_keep(v):
    return (v, None)

def back_low(kept, grad):
    return (low(grad),)
low.defvjp(low_keep, low_pass)
low_back.defvjp(back_keep, back_low)

def matmul(left, right):
    return jnp.dot(left, right, precision=lax.Precision.HIGHEST)

def normalize(values):
    center = values - lax.optimization_barrier(jnp.mean(values, axis=-1, keepdims=True))
    return center * lax.rsqrt(lax.optimization_barrier(jnp.mean(center * center, axis=-1, keepdims=True)) + EPS)

def gelu_tanh(values):
    return 0.5 * values * (1.0 + jnp.tanh(0.7978845608028654 * (values + 0.044715 * values * values * values)))

def attention(query, key_all, value_all, documents):
    length = query.shape[0]
    query_rows = min(512, length)
    padding = jnp.zeros((WINDOW, HEADS, HEAD_DIM), jnp.float32)
    keys_pad = jnp.concatenate([padding, key_all], axis=0)
    values_pad = jnp.concatenate([padding, value_all], axis=0)
    docs_pad = jnp.concatenate([jnp.full((WINDOW,), -1, jnp.int32), documents.astype(jnp.int32)])
    slopes = 2.0 ** (-8.0 * (jnp.arange(HEADS).astype(jnp.float32) + 1.0) / HEADS)
    scale = HEAD_DIM ** (-0.5)

    def one_block(offset):
        span = WINDOW + query_rows
        q_block = lax.dynamic_slice_in_dim(query, offset, query_rows, 0)
        k_block = lax.dynamic_slice_in_dim(keys_pad, offset, span, 0)
        v_block = lax.dynamic_slice_in_dim(values_pad, offset, span, 0)
        q_pos = offset + jnp.arange(query_rows, dtype=jnp.int32)
        k_pos = offset - WINDOW + jnp.arange(span, dtype=jnp.int32)
        q_doc = lax.dynamic_slice_in_dim(documents.astype(jnp.int32), offset, query_rows, 0)
        k_doc = lax.dynamic_slice_in_dim(docs_pad, offset, span, 0)
        scores = jnp.einsum('qhd,khd->hqk', q_block, k_block, precision=lax.Precision.HIGHEST) * scale
        distance = (k_pos[None, :] - q_pos[:, None]).astype(jnp.float32)
        scores = low_back(scores + slopes[:, None, None] * distance[None])
        allowed = (k_pos[None, :] <= q_pos[:, None]) & (q_pos[:, None] - k_pos[None, :] < WINDOW)
        allowed = allowed & (k_pos[None, :] >= 0) & (k_doc[None, :] == q_doc[:, None])
        probs = low(jax.nn.softmax(jnp.where(allowed[None], scores, NEG), axis=-1))
        return jnp.einsum('hqk,khd->qhd', probs, v_block, precision=lax.Precision.HIGHEST)
    offsets = jnp.arange(length // query_rows, dtype=jnp.int32) * query_rows
    blocks = lax.map(jax.checkpoint(one_block), offsets)
    return blocks.reshape(length, HEADS, HEAD_DIM)

def block_layer(inputs, params, documents, valid):
    ln1_gain, ln1_bias, w_qkv, bias_query, bias_value, w_out, bias_out, ln2_gain, ln2_bias, w_up, bias_up, w_down, bias_down = params
    length = inputs.shape[0]
    normed = low(normalize(inputs) * ln1_gain + ln1_bias)
    projected = matmul(normed, w_qkv)
    query = low_back(low(projected[:, :D] + bias_query)).reshape(length, HEADS, HEAD_DIM)
    key_all = low_back(low(projected[:, D:2 * D])).reshape(length, HEADS, HEAD_DIM)
    value_all = low_back(low(projected[:, 2 * D:] + bias_value)).reshape(length, HEADS, HEAD_DIM)
    context = attention(query, key_all, value_all, documents) * valid[:, None, None]
    context = low_back(low(context)).reshape(length, D)
    middle = inputs + low_back(matmul(context, w_out) + bias_out)
    normed_mid = low(normalize(middle) * ln2_gain + ln2_bias)
    up_pre = low_back(matmul(normed_mid, w_up) + bias_up)
    active = low(gelu_tanh(up_pre))
    return middle + low_back(matmul(active, w_down) + bias_down)

def reference(layer_input, lengths, ln1_gain, ln1_bias, w_qkv, bias_query, bias_value, w_out, bias_out, ln2_gain, ln2_bias, w_up, bias_up, w_down, bias_down, cotangent):
    params = (ln1_gain.astype(jnp.float32), ln1_bias.astype(jnp.float32), w_qkv.astype(jnp.float32), bias_query.astype(jnp.float32), bias_value.astype(jnp.float32), w_out.astype(jnp.float32), bias_out.astype(jnp.float32), ln2_gain.astype(jnp.float32), ln2_bias.astype(jnp.float32), w_up.astype(jnp.float32), bias_up.astype(jnp.float32), w_down.astype(jnp.float32), bias_down.astype(jnp.float32))
    inputs = layer_input.reshape(SEQS, SEQ_LEN, D).astype(jnp.float32)
    cotan_all = cotangent.reshape(SEQS, SEQ_LEN, D).astype(jnp.float32)
    positions = jnp.arange(SEQ_LEN, dtype=jnp.int32)

    def per_sequence(summed, items):
        seq_in, seq_cot, seq_lengths = items
        doc_ends = jnp.cumsum(seq_lengths.astype(jnp.int32)).astype(jnp.int32)
        documents = lax.optimization_barrier(jnp.sum((doc_ends[None, :] <= positions[:, None]).astype(jnp.int32), axis=1)).astype(jnp.int32)
        valid = (documents < DOCS).astype(jnp.float32)
        output, pullback = jax.vjp(lambda a, b: block_layer(a, b, documents, valid), seq_in, params)
        grad_in, grad_params = pullback(seq_cot)
        summed = jax.tree.map(lambda a, b: a + b, summed, grad_params)
        return (summed, (output.astype(jnp.bfloat16), grad_in))
    zeros = jax.tree.map(jnp.zeros_like, params)
    grads, (outputs, grad_inputs) = lax.scan(per_sequence, zeros, (inputs, cotan_all, lengths))
    return (outputs.reshape(N_BLK, BLOCK, D), grad_inputs.reshape(N_BLK, BLOCK, D), grads[0], grads[1], grads[2], grads[3], grads[4], grads[5], grads[6], grads[7], grads[8], grads[9], grads[10], grads[11], grads[12])
```

```python
import jax
import jax.numpy as jnp
from jax import lax
from jax.experimental import pallas as pl
from jax.experimental.pallas import tpu as pltpu
from jax.sharding import PartitionSpec as P

D = 2048
HEADS = 16
HEAD_DIM = 128
FF = 8192
TOK_DEV = 256
WINDOW = 1024
SEQ_LEN = 8192
DOCS = 4

EPS = 1e-05
NEG = -1e30
BF = jnp.bfloat16
F32 = jnp.float32
ROWS = (((0,), (0,)), ((), ()))
COLS = (((1,), (1,)), ((), ()))

TILE = 256
HALO = WINDOW // TILE
SPAN = WINDOW + TILE
VMEM = 48 * 1024 * 1024


def normalize(values):
    center = values - jnp.mean(values, axis=-1, keepdims=True)
    inv_scale = lax.rsqrt(jnp.mean(center * center, axis=-1, keepdims=True) + EPS)
    return (center * inv_scale, inv_scale)


def norm_back(d_hat, normed, inv_scale):
    return inv_scale * (
        d_hat
        - jnp.mean(d_hat, axis=-1, keepdims=True)
        - normed * jnp.mean(d_hat * normed, axis=-1, keepdims=True)
    )


def gelu_tanh(values):
    return (
        0.5
        * values
        * (1.0 + jnp.tanh(0.7978845608028654 * (values + 0.044715 * values * values * values)))
    )


def fill_tiles(buffer, halo_ref, own_ref, halo_slots, slots, tiles):
    for tile in range(HALO):
        buffer[tile * TILE : (tile + 1) * TILE, :] = halo_ref[halo_slots[tile]]
    for tile in range(tiles):
        buffer[(HALO + tile) * TILE : (HALO + tile + 1) * TILE, :] = own_ref[slots[tile]]


def fill_bias(bias, slope):
    key = lax.broadcasted_iota(jnp.int32, (SPAN, TILE), 0)
    query = lax.broadcasted_iota(jnp.int32, (SPAN, TILE), 1)
    rel = key - WINDOW - query
    bias[...] = jnp.where((rel <= 0) & (rel > -WINDOW), slope * rel.astype(F32), NEG)


def masked_scores(q, keys, bias, low_row):
    scores = lax.dot_general(keys, q, COLS, preferred_element_type=F32)
    scores = scores * HEAD_DIM ** (-0.5) + bias
    key = lax.broadcasted_iota(jnp.int32, (SPAN, TILE), 0)
    return jnp.where(key >= low_row, scores, NEG)


def attn_fwd_kernel(
    slots, halo_slots, slopes, q_ref, k_ref, v_ref, hk_ref, hv_ref, low_ref, valid_ref, ctx_ref, lse_ref, kbuf, vbuf, bias
):
    head = pl.program_id(0)
    tile = pl.program_id(1)

    @pl.when(tile == 0)
    def _():
        fill_tiles(kbuf, hk_ref, k_ref, halo_slots, slots, k_ref.shape[0])
        fill_tiles(vbuf, hv_ref, v_ref, halo_slots, slots, k_ref.shape[0])
        fill_bias(bias, slopes[head])

    start = pl.multiple_of(tile * TILE, TILE)
    scores = masked_scores(q_ref[0], kbuf[pl.ds(start, SPAN), :], bias[...], low_ref[0])
    highest = jnp.max(scores, axis=0, keepdims=True)
    expo = jnp.exp(scores - highest)
    summed = jnp.sum(expo, axis=0, keepdims=True)
    lse_ref[0, 0] = highest + jnp.log(summed)
    context = lax.dot_general(
        vbuf[pl.ds(start, SPAN), :], expo.astype(BF), ROWS, preferred_element_type=F32
    )
    context = context * (valid_ref[0] / summed)
    ctx_ref[0] = context.T.astype(BF)


def attn_bwd_kernel(
    slots,
    halo_slots,
    slopes,
    q_ref,
    k_ref,
    v_ref,
    hk_ref,
    hv_ref,
    low_ref,
    dctx_ref,
    lse_ref,
    dq_ref,
    dk_ref,
    dv_ref,
    dhk_ref,
    dhv_ref,
    kbuf,
    vbuf,
    bias,
    dkbuf,
    dvbuf,
):
    head = pl.program_id(0)
    tile = pl.program_id(1)
    tiles = k_ref.shape[0]

    @pl.when(tile == 0)
    def _():
        fill_tiles(kbuf, hk_ref, k_ref, halo_slots, slots, tiles)
        fill_tiles(vbuf, hv_ref, v_ref, halo_slots, slots, tiles)
        fill_bias(bias, slopes[head])
        dkbuf[...] = jnp.zeros_like(dkbuf)
        dvbuf[...] = jnp.zeros_like(dvbuf)

    start = pl.multiple_of(tile * TILE, TILE)
    rows = pl.ds(start, SPAN)
    q = q_ref[0]
    d_ctx = dctx_ref[0]
    keys = kbuf[rows, :]
    scores = masked_scores(q, keys, bias[...], low_ref[0])
    probs = jnp.exp(scores - lse_ref[0, 0])
    d_probs = lax.dot_general(vbuf[rows, :], d_ctx, COLS, preferred_element_type=F32)
    delta = jnp.sum(probs * d_probs, axis=0, keepdims=True)
    d_scores = (probs * (d_probs - delta)).astype(BF)
    scale = HEAD_DIM ** (-0.5)
    d_query = lax.dot_general(d_scores, keys, ROWS, preferred_element_type=F32)
    dq_ref[0] = (d_query * scale).astype(BF)
    dkbuf[rows, :] += jnp.dot(d_scores, q, preferred_element_type=F32)
    dvbuf[rows, :] += jnp.dot(probs.astype(BF), d_ctx, preferred_element_type=F32)

    @pl.when(tile == tiles - 1)
    def _():
        for at in range(HALO):
            piece = slice(at * TILE, (at + 1) * TILE)
            dhk_ref[halo_slots[at]] = (dkbuf[piece, :] * scale).astype(BF)
            dhv_ref[halo_slots[at]] = dvbuf[piece, :].astype(BF)
        for at in range(tiles):
            piece = slice((HALO + at) * TILE, (HALO + at + 1) * TILE)
            dk_ref[slots[at]] = dkbuf[piece, :] * scale
            dv_ref[slots[at]] = dvbuf[piece, :]


def attention_specs(heads, tiles):
    block = (1, TILE, HEAD_DIM)
    whole = (tiles, TILE, HEAD_DIM)
    halo = (HALO, TILE, HEAD_DIM)
    row = (1, 1, TILE)
    q_spec = pl.BlockSpec(block, lambda h, t, s, hs, sl: (s[t], 0, h))
    k_spec = pl.BlockSpec(whole, lambda h, t, s, hs, sl: (0, 0, heads + h))
    v_spec = pl.BlockSpec(whole, lambda h, t, s, hs, sl: (0, 0, 2 * heads + h))
    hk_spec = pl.BlockSpec(halo, lambda h, t, s, hs, sl: (0, 0, h))
    hv_spec = pl.BlockSpec(halo, lambda h, t, s, hs, sl: (0, 0, heads + h))
    row_spec = pl.BlockSpec(row, lambda h, t, s, hs, sl: (t, 0, 0))
    lse_spec = pl.BlockSpec((1, 1, 1, TILE), lambda h, t, s, hs, sl: (h, t, 0, 0))
    own_spec = pl.BlockSpec(whole, lambda h, t, s, hs, sl: (0, 0, h))
    return q_spec, k_spec, v_spec, hk_spec, hv_spec, row_spec, lse_spec, own_spec


def attn_forward(scalars, qkv, halo, low, valid, heads):
    tiles = qkv.shape[0]
    q_s, k_s, v_s, hk_s, hv_s, row_s, lse_s, own_s = attention_specs(heads, tiles)
    length = (HALO + tiles) * TILE
    work = heads * tiles * SPAN * TILE
    return pl.pallas_call(
        attn_fwd_kernel,
        grid_spec=pltpu.PrefetchScalarGridSpec(
            num_scalar_prefetch=3,
            grid=(heads, tiles),
            in_specs=[q_s, k_s, v_s, hk_s, hv_s, row_s, row_s],
            out_specs=[q_s, lse_s],
            scratch_shapes=[
                pltpu.VMEM((length, HEAD_DIM), BF),
                pltpu.VMEM((length, HEAD_DIM), BF),
                pltpu.VMEM((SPAN, TILE), F32),
            ],
        ),
        out_shape=[
            jax.ShapeDtypeStruct((tiles, TILE, heads * HEAD_DIM), BF),
            jax.ShapeDtypeStruct((heads, tiles, 1, TILE), F32),
        ],
        compiler_params=pltpu.CompilerParams(vmem_limit_bytes=VMEM),
        cost_estimate=pl.CostEstimate(
            flops=8 * work * HEAD_DIM, bytes_accessed=8 << 20, transcendentals=work
        ),
    )(*scalars, qkv, qkv, qkv, halo, halo, low, valid)


def attn_backward(scalars, qkv, halo, low, d_ctx, lse, heads):
    tiles = qkv.shape[0]
    q_s, k_s, v_s, hk_s, hv_s, row_s, lse_s, own_s = attention_specs(heads, tiles)
    length = (HALO + tiles) * TILE
    work = heads * tiles * SPAN * TILE
    width = heads * HEAD_DIM
    return pl.pallas_call(
        attn_bwd_kernel,
        grid_spec=pltpu.PrefetchScalarGridSpec(
            num_scalar_prefetch=3,
            grid=(heads, tiles),
            in_specs=[q_s, k_s, v_s, hk_s, hv_s, row_s, q_s, lse_s],
            out_specs=[q_s, own_s, own_s, hk_s, hk_s],
            scratch_shapes=[
                pltpu.VMEM((length, HEAD_DIM), BF),
                pltpu.VMEM((length, HEAD_DIM), BF),
                pltpu.VMEM((SPAN, TILE), F32),
                pltpu.VMEM((length, HEAD_DIM), F32),
                pltpu.VMEM((length, HEAD_DIM), F32),
            ],
        ),
        out_shape=[
            jax.ShapeDtypeStruct((tiles, TILE, width), BF),
            jax.ShapeDtypeStruct((tiles, TILE, width), F32),
            jax.ShapeDtypeStruct((tiles, TILE, width), F32),
            jax.ShapeDtypeStruct((HALO, TILE, width), BF),
            jax.ShapeDtypeStruct((HALO, TILE, width), BF),
        ],
        compiler_params=pltpu.CompilerParams(vmem_limit_bytes=VMEM),
        cost_estimate=pl.CostEstimate(
            flops=20 * work * HEAD_DIM, bytes_accessed=16 << 20, transcendentals=work
        ),
    )(*scalars, qkv, qkv, qkv, halo, halo, low, d_ctx, lse)


def shards(
    layer_input,
    lengths,
    ln1_gain,
    ln1_bias,
    w_qkv,
    bias_query,
    bias_value,
    w_out,
    bias_out,
    ln2_gain,
    ln2_bias,
    w_up,
    bias_up,
    w_down,
    bias_down,
    cotangent,
):
    nh = lax.axis_size("head")
    nb = lax.axis_size("blk")
    nx = 2
    nz = nb // nx
    members = nx * nh
    rows = D // (nh * nb)
    ff_rows = FF // (nh * nb)
    ff_own = nz * ff_rows
    heads = HEADS // members
    width = heads * HEAD_DIM
    head_at = lax.axis_index("head")
    blk_at = lax.axis_index("blk")
    x_at = lax.rem(blk_at, nx)
    z_at = lax.div(blk_at, nx)
    both = ("head", "blk")
    plane = [[h * nb + z * nx + x for x in range(nx) for h in range(nh)] for z in range(nz)]
    column = [[z * nx + x for z in range(nz)] for x in range(nx)]

    def to_core(t):
        return lax.ppermute(t, "head", [(h, h ^ 1) for h in range(nh)])

    def to_y(t):
        return lax.ppermute(t, "head", [(h, h ^ 2) for h in range(nh)])

    def to_x(t):
        return lax.ppermute(t, "blk", [(b, b ^ 1) for b in range(nb)])

    def to_diag(t):
        return lax.ppermute(
            t, both, [(h * nb + b, (h ^ 2) * nb + (b ^ 1)) for h in range(nh) for b in range(nb)]
        )

    def gather_plane(own):
        same = [own, to_y(own), to_x(own), to_diag(own)]
        return jnp.concatenate(same + [to_core(t) for t in same], axis=0)

    def scatter_plane(part):
        half = part.shape[0] // 2
        kept = (part[:half].astype(F32) + to_core(part[half:]).astype(F32)).astype(BF)
        kept = kept.reshape(4, half // 4, part.shape[1])
        return (
            kept[0].astype(F32)
            + to_y(kept[1]).astype(F32)
            + to_x(kept[2]).astype(F32)
            + to_diag(kept[3]).astype(F32)
        )

    def plane_a2a(t):
        return lax.all_to_all(
            t, both, split_axis=0, concat_axis=0, tiled=True, axis_index_groups=plane
        )

    def gather_z(t):
        return lax.all_gather(t, "blk", axis=0, tiled=False, axis_index_groups=column)

    def scatter_z(t):
        return lax.psum_scatter(
            t, "blk", scatter_dimension=0, tiled=False, axis_index_groups=column
        )

    me = x_at * nh + head_at
    slots, halo_slots = [], []
    for tile in range(members):
        diff = jnp.bitwise_xor(me, tile)
        slots.append((diff & 1) * 4 + ((diff >> 2) & 1) * 2 + ((diff >> 1) & 1))
    for tile in range(HALO):
        diff = jnp.bitwise_xor(head_at, tile)
        halo_slots.append((diff & 1) * 2 + ((diff >> 1) & 1))
    slots = jnp.stack(slots).astype(jnp.int32)
    halo_slots = jnp.stack(halo_slots).astype(jnp.int32)
    head_ids = (head_at * nx + x_at) * heads + jnp.arange(heads, dtype=jnp.int32)
    slopes = 2.0 ** (-8.0 * (head_ids.astype(F32) + 1.0) / HEADS)
    scalars = (slots, halo_slots, slopes)
    group_tokens = members * TOK_DEV
    local = jnp.arange(group_tokens, dtype=jnp.int32)
    first = z_at * group_tokens
    positions = first + local
    sequence = lax.div(positions, SEQ_LEN)
    within = positions - sequence * SEQ_LEN
    row_lengths = jnp.take(lengths, sequence, axis=0)
    ends = jnp.cumsum(row_lengths, axis=1)
    past = ends <= within[:, None]
    valid = (jnp.sum(past.astype(jnp.int32), axis=1) < DOCS).astype(F32)
    doc_start = sequence * SEQ_LEN + jnp.sum(jnp.where(past, row_lengths, 0), axis=1)
    low = doc_start - first + WINDOW - lax.div(local, TILE) * TILE
    low = low.reshape(members, 1, TILE)
    valid_tiles = valid.reshape(members, 1, TILE)

    out_z = gather_z(w_out)
    qkv_sent = w_qkv.reshape(rows, 3, nh, nx, width).transpose(3, 2, 0, 1, 4)
    qkv_col = plane_a2a(qkv_sent.reshape(members, rows, 3 * width))
    up_sent = w_up.reshape(rows, nh, nz, nx, ff_rows).transpose(3, 1, 0, 2, 4)
    up_col = plane_a2a(up_sent.reshape(members, rows, ff_own))
    qkv_z = gather_z(qkv_col)
    up_z = gather_z(up_col)
    down_w = gather_z(w_down).reshape(ff_own, D)

    def true_rows(t):
        return t.reshape(nz, nx, nh, rows, -1).transpose(2, 0, 1, 3, 4).reshape(D, -1)

    def sent_rows(t):
        return t.reshape(nh, nz, nx, rows, -1).transpose(1, 2, 0, 3, 4).reshape(nz, members, rows, -1)

    qkv_w = true_rows(qkv_z)
    up_w = true_rows(up_z)
    half_z = nz // 2
    halves = out_z.reshape(2, half_z, rows, D)
    mine = jnp.where(x_at == 0, halves[0], halves[1])
    theirs = to_x(jnp.where(x_at == 0, halves[1], halves[0]))
    low_half = jnp.where(x_at == 0, mine, theirs)
    high_half = jnp.where(x_at == 0, theirs, mine)
    out_w = jnp.stack([low_half, high_half], axis=1).reshape(width, D)

    small = jnp.concatenate(
        [ln1_gain, ln1_bias, bias_query, bias_value, bias_out, ln2_gain, ln2_bias, bias_down, bias_up]
    )
    small_z = gather_z(small)
    bias_u = small_z[:, 8 * rows :].reshape(ff_own).astype(F32)
    small_all = lax.all_gather(
        small_z[:, : 8 * rows], both, axis=0, tiled=False, axis_index_groups=plane
    )
    vectors = (
        small_all.reshape(nx, nh, nz, 8, rows).transpose(3, 1, 2, 0, 4).reshape(8, D).astype(F32)
    )
    gain_one, shift_one, bias_q, bias_v, bias_o, gain_two, shift_two, bias_d = vectors
    own_cols = (head_at * nx + x_at) * width
    bias_qkv = jnp.concatenate(
        [
            lax.dynamic_slice_in_dim(bias_q, own_cols, width),
            jnp.zeros((width,), F32),
            lax.dynamic_slice_in_dim(bias_v, own_cols, width),
        ]
    )

    x_own = layer_input.reshape(TOK_DEV, D)
    cot_own = cotangent.reshape(TOK_DEV, D)
    x_all = gather_plane(x_own)
    ln1 = (normalize(x_all.astype(F32))[0] * gain_one + shift_one).astype(BF)
    rows_in = x_own.astype(F32)
    normed_in, inv_in = normalize(rows_in)
    qkv = (jnp.dot(ln1, qkv_w, preferred_element_type=F32) + bias_qkv).astype(BF)
    qkv = qkv.reshape(members, TILE, 3 * width)
    kv = qkv[:, :, width:].reshape(2, 2, 2, TILE, 2 * width)
    kv = jnp.where(x_at == 0, kv[:, 1], kv[:, 0]).reshape(HALO, TILE, 2 * width)
    halo = lax.ppermute(kv, "blk", [(b, b + nx) for b in range(nb - nx)])
    ctx, lse = attn_forward(scalars, qkv, halo, low, valid_tiles, heads)
    ctx = ctx.reshape(group_tokens, width)
    attn_part = jnp.dot(ctx, out_w, preferred_element_type=F32).astype(BF)
    middle = rows_in + (scatter_plane(attn_part) + bias_o)
    normed_mid, inv_mid = normalize(middle)
    ln2_own = (normed_mid * gain_two + shift_two).astype(BF)
    ln2 = gather_plane(ln2_own)
    up_pre = jnp.dot(ln2, up_w, preferred_element_type=F32) + bias_u
    active = gelu_tanh(up_pre).astype(BF)
    down_part = jnp.dot(active, down_w, preferred_element_type=F32).astype(BF)
    output = (middle + (scatter_plane(down_part) + bias_d)).astype(BF)

    cot = gather_plane(cot_own)
    cot_full = cot_own.astype(F32)
    g_down = lax.dot_general(active, cot, ROWS, preferred_element_type=F32).astype(BF)
    grad_w_down = scatter_z(g_down.reshape(nz, ff_rows, D)).astype(F32)
    d_act = lax.dot_general(cot, down_w, COLS, preferred_element_type=F32)
    d_up_full = jax.vjp(gelu_tanh, up_pre)[1](d_act)[0]
    d_up = d_up_full.astype(BF)
    g_up = lax.dot_general(ln2, d_up, ROWS, preferred_element_type=F32).astype(BF)
    g_up = plane_a2a(scatter_z(sent_rows(g_up)))
    grad_w_up = (
        g_up.reshape(nx, nh, rows, nz, ff_rows).transpose(2, 1, 3, 0, 4).reshape(rows, FF)
    ).astype(F32)
    grad_b_up = jnp.sum(d_up.astype(F32), axis=0)
    d_ln2 = scatter_plane(
        lax.dot_general(d_up, up_w, COLS, preferred_element_type=F32).astype(BF)
    )
    d_middle = cot_full + norm_back(d_ln2 * gain_two, normed_mid, inv_mid)
    d_attn_own = d_middle.astype(BF)
    d_attn = gather_plane(d_attn_own)
    g_out = lax.dot_general(ctx, d_attn, ROWS, preferred_element_type=F32).astype(BF)
    g_out = g_out.reshape(half_z, nx, rows, D)
    g_mine = jnp.where(x_at == 0, g_out[:, 0], g_out[:, 1])
    g_theirs = to_x(jnp.where(x_at == 0, g_out[:, 1], g_out[:, 0]))
    g_out = jnp.concatenate(
        [jnp.where(x_at == 0, g_mine, g_theirs), jnp.where(x_at == 0, g_theirs, g_mine)], axis=0
    )
    grad_w_out = scatter_z(g_out).astype(F32)
    valid_slot = jnp.zeros((members, TILE), F32).at[slots].set(valid.reshape(members, TILE))
    d_ctx = lax.dot_general(d_attn, out_w, COLS, preferred_element_type=F32)
    d_ctx = (d_ctx * valid_slot.reshape(group_tokens, 1)).astype(BF)
    d_q, d_k, d_v, d_hk, d_hv = attn_backward(
        scalars, qkv, halo, low, d_ctx.reshape(members, TILE, width), lse, heads
    )
    back = lax.ppermute(
        jnp.concatenate([d_hk, d_hv], axis=-1), "blk", [(b + nx, b) for b in range(nb - nx)]
    ).astype(F32)
    back = back.reshape(2, 1, 2, TILE, 2 * width)
    second = (jnp.arange(2) != x_at).reshape(1, 2, 1, 1, 1)
    d_kv = jnp.concatenate([d_k, d_v], axis=-1).reshape(2, 2, 2, TILE, 2 * width)
    d_kv = (d_kv + jnp.where(second, back, 0.0)).astype(BF).reshape(group_tokens, 2 * width)
    d_q = d_q.reshape(group_tokens, width)
    d_proj = jnp.concatenate([d_q, d_kv], axis=1)
    g_qkv = lax.dot_general(ln1, d_proj, ROWS, preferred_element_type=F32).astype(BF)
    g_qkv = plane_a2a(scatter_z(sent_rows(g_qkv)))
    grad_w_qkv = (
        g_qkv.reshape(nx, nh, rows, 3, width).transpose(2, 3, 1, 0, 4).reshape(rows, 3 * D)
    ).astype(F32)
    d_ln1 = scatter_plane(
        lax.dot_general(d_proj, qkv_w, COLS, preferred_element_type=F32).astype(BF)
    )
    grad_input = d_middle + norm_back(d_ln1 * gain_one, normed_in, inv_in)

    def placed(t):
        return lax.dynamic_update_slice_in_dim(jnp.zeros((D,), F32), t, own_cols, 0)

    sums = jnp.stack(
        [
            jnp.sum(d_ln1 * normed_in, axis=0),
            jnp.sum(d_ln1, axis=0),
            placed(jnp.sum(d_q.astype(F32), axis=0)),
            placed(jnp.sum(d_kv[:, width:].astype(F32), axis=0)),
            jnp.sum(d_attn_own.astype(F32), axis=0),
            jnp.sum(d_ln2 * normed_mid, axis=0),
            jnp.sum(d_ln2, axis=0),
            jnp.sum(cot_full, axis=0),
        ]
    )
    sums = sums.reshape(8, nh, nz, nx, rows).transpose(3, 1, 2, 0, 4)
    sums = jnp.sum(plane_a2a(sums.reshape(members, nz, 8 * rows)), axis=0)
    sums = jnp.concatenate([sums, grad_b_up.reshape(nz, ff_rows)], axis=1)
    sums = jnp.sum(
        lax.all_to_all(
            sums, "blk", split_axis=0, concat_axis=0, tiled=True, axis_index_groups=column
        ),
        axis=0,
    )
    vec = sums[: 8 * rows].reshape(8, rows)
    return (
        output.reshape(1, TOK_DEV, D),
        grad_input.reshape(1, TOK_DEV, D),
        vec[0],
        vec[1],
        grad_w_qkv,
        vec[2],
        vec[3],
        grad_w_out,
        vec[4],
        vec[5],
        vec[6],
        grad_w_up,
        sums[8 * rows :],
        grad_w_down,
        vec[7],
    )


def solution(mesh):
    split = P(("head", "blk"))
    wide = P(("head", "blk"), None)
    tokens = P("blk", "head", None)
    return jax.shard_map(
        shards,
        mesh=mesh,
        in_specs=(
            tokens, P(), split, split, wide, split, split, wide, split, split, split, wide, split, wide, split, tokens,
        ),
        out_specs=(
            tokens, tokens, split, split, wide, split, split, wide, split, split, split, wide, split, wide, split,
        ),
        check_vma=False,
    )
```

```python
import functools

import jax
import jax.numpy as jnp
from jax import lax
from jax.experimental import pallas as pl
from jax.experimental.pallas import tpu as pltpu
from jax.sharding import PartitionSpec as P

D = 2048
HEADS = 16
HEAD_DIM = 128
FF = 8192
TOK_DEV = 256
WINDOW = 1024
SEQ_LEN = 8192
DOCS = 4

EPS = 1e-05
NEG = -1e30
BF = jnp.bfloat16
F32 = jnp.float32
ROWS = (((0,), (0,)), ((), ()))
COLS = (((1,), (1,)), ((), ()))

TILE = 256
HALO = WINDOW // TILE
SPAN = WINDOW + TILE
VMEM = 48 * 1024 * 1024
F = dict(x1=0, cot=0, cotk=1, cotctx=0, cotb=0, gd_lo=1, gd_hi=1, gu_lo=1, gu_hi=1, rsd=1, rsu=4, rso=0, df_lo=0, df_hi=2, lo_lo=1, lo_hi=3, go_lo=0, go_hi=1, gkv=1, hsplit=0, gq=0, agd=1, upc=0)
COST = dict(qkv_fwd=0, out_fwd=3, up_fwd=0, down_back=0, collect=0, down_grad=0, up_grad=0, down_fwd=0, ctx_back=20, out_grad=0, qkv_grad=8, qkv_back=0, attn_fwd_low=1, attn_fwd_high=0, attn_bwd_low=20, attn_bwd_high=0, qkv_split=8, up_split=1, up_join=0, qkv_join=0)


def cost_of(name):
    flops = int(COST[name] * 1e9)
    return pl.CostEstimate(flops=flops, bytes_accessed=4096, transcendentals=0)


def normalize(values):
    center = values - jnp.mean(values, axis=-1, keepdims=True)
    inv_scale = lax.rsqrt(jnp.mean(center * center, axis=-1, keepdims=True) + EPS)
    return (center * inv_scale, inv_scale)


def norm_back(d_hat, normed, inv_scale):
    return inv_scale * (
        d_hat
        - jnp.mean(d_hat, axis=-1, keepdims=True)
        - normed * jnp.mean(d_hat * normed, axis=-1, keepdims=True)
    )


def gelu_tanh(values):
    return (
        0.5
        * values
        * (1.0 + jnp.tanh(0.7978845608028654 * (values + 0.044715 * values * values * values)))
    )


def fill_tiles(buffer, halo_ref, own_ref, halo_slots, slots):
    if halo_ref is None:
        sources = [(own_ref, slots, tile) for tile in range(own_ref.shape[0])]
    else:
        sources = [(halo_ref, halo_slots, tile) for tile in range(HALO)]
        sources += [(own_ref, slots, tile) for tile in range(own_ref.shape[0] - HALO)]
    for at, (ref, order, tile) in enumerate(sources):
        buffer[at * TILE : (at + 1) * TILE, :] = ref[order[tile]]


def fill_bias(bias, slope):
    key = lax.broadcasted_iota(jnp.int32, (SPAN, TILE), 0)
    query = lax.broadcasted_iota(jnp.int32, (SPAN, TILE), 1)
    rel = key - WINDOW - query
    bias[...] = jnp.where((rel <= 0) & (rel > -WINDOW), slope * rel.astype(F32), NEG)


def masked_scores(q, keys, bias, low_row):
    scores = lax.dot_general(keys, q, COLS, preferred_element_type=F32)
    scores = scores * HEAD_DIM ** (-0.5) + bias
    key = lax.broadcasted_iota(jnp.int32, (SPAN, TILE), 0)
    return jnp.where(key >= low_row, scores, NEG)


def attn_fwd_kernel(first, slots, halo_slots, slopes, q_ref, k_ref, v_ref, *refs):
    hk_ref, hv_ref, refs = (refs[0], refs[1], refs[3:]) if first else (None, None, refs)
    low_ref, valid_ref, ctx_ref, lse_ref, kbuf, vbuf, bias = refs
    head = pl.program_id(0)
    tile = pl.program_id(1)

    @pl.when(tile == 0)
    def _():
        fill_tiles(kbuf, hk_ref, k_ref, halo_slots, slots)
        fill_tiles(vbuf, hv_ref, v_ref, halo_slots, slots)
        fill_bias(bias, slopes[head])

    start = pl.multiple_of(tile * TILE, TILE)
    scores = masked_scores(q_ref[0], kbuf[pl.ds(start, SPAN), :], bias[...], low_ref[0])
    highest = jnp.max(scores, axis=0, keepdims=True)
    expo = jnp.exp(scores - highest)
    summed = jnp.sum(expo, axis=0, keepdims=True)
    lse_ref[0, 0] = highest + jnp.log(summed)
    context = lax.dot_general(
        vbuf[pl.ds(start, SPAN), :], expo.astype(BF), ROWS, preferred_element_type=F32
    )
    context = context * (valid_ref[0] / summed)
    ctx_ref[0] = context.T.astype(BF)


def attn_bwd_kernel(first, slots, halo_slots, slopes, q_ref, k_ref, v_ref, *refs):
    hk_ref, hv_ref, refs = (refs[0], refs[1], refs[2:]) if first else (None, None, refs)
    low_ref, dctx_ref, lse_ref = refs[:3]
    if first:
        dq_ref, dhk_ref, dhv_ref, dk_ref, dv_ref = refs[3:8]
    else:
        dk_in, dv_in, _, dq_ref, dk_ref, dv_ref = refs[3:9]
    kbuf, vbuf, bias, dkbuf, dvbuf = refs[-5:]
    head = pl.program_id(0)
    tile = pl.program_id(1)
    tiles = k_ref.shape[0]
    own = tiles - HALO
    kept = own * TILE

    @pl.when(tile == 0)
    def _():
        fill_tiles(kbuf, hk_ref, k_ref, halo_slots, slots)
        fill_tiles(vbuf, hv_ref, v_ref, halo_slots, slots)
        fill_bias(bias, slopes[head])
        if first:
            dkbuf[...] = jnp.zeros_like(dkbuf)
            dvbuf[...] = jnp.zeros_like(dvbuf)
        else:
            for buffer, start in ((dkbuf, dk_in), (dvbuf, dv_in)):
                buffer[:kept, :] = start[0]
                buffer[kept:, :] = jnp.zeros((buffer.shape[0] - kept, HEAD_DIM), F32)

    start = pl.multiple_of(tile * TILE, TILE)
    rows = pl.ds(start, SPAN)
    q = q_ref[0]
    d_ctx = dctx_ref[0]
    keys = kbuf[rows, :]
    scores = masked_scores(q, keys, bias[...], low_ref[0])
    probs = jnp.exp(scores - lse_ref[0, 0])
    d_probs = lax.dot_general(vbuf[rows, :], d_ctx, COLS, preferred_element_type=F32)
    delta = jnp.sum(probs * d_probs, axis=0, keepdims=True)
    d_scores = (probs * (d_probs - delta)).astype(BF)
    scale = HEAD_DIM ** (-0.5)
    d_query = lax.dot_general(d_scores, keys, ROWS, preferred_element_type=F32)
    dq_ref[0] = (d_query * scale).astype(BF)
    dkbuf[rows, :] += jnp.dot(d_scores, q, preferred_element_type=F32)
    dvbuf[rows, :] += jnp.dot(probs.astype(BF), d_ctx, preferred_element_type=F32)

    @pl.when(tile == pl.num_programs(1) - 1)
    def _():
        if first:
            for at in range(HALO):
                piece = slice(at * TILE, (at + 1) * TILE)
                dhk_ref[halo_slots[at]] = (dkbuf[piece, :] * scale).astype(BF)
                dhv_ref[halo_slots[at]] = dvbuf[piece, :].astype(BF)
            dk_ref[0] = dkbuf[HALO * TILE :, :]
            dv_ref[0] = dvbuf[HALO * TILE :, :]
        else:
            for at in range(tiles):
                piece = slice(at * TILE, (at + 1) * TILE)
                dk_ref[slots[at]] = dkbuf[piece, :] * scale
                dv_ref[slots[at]] = dvbuf[piece, :]


def attention_call(kernel, first, scalars, qkv, halo, rows, heads, grads):
    tiles = qkv.shape[0]
    queries = HALO if first else tiles - HALO
    base = 0 if first else HALO
    width = heads * HEAD_DIM
    block = (1, TILE, HEAD_DIM)
    whole = (tiles, TILE, HEAD_DIM)
    edge = (HALO, TILE, HEAD_DIM)
    q_s = pl.BlockSpec(block, lambda h, t, s, hs, sl: (s[t + base], 0, h))
    own_s = pl.BlockSpec(whole, lambda h, t, s, hs, sl: (0, 0, h))
    k_s = pl.BlockSpec(whole, lambda h, t, s, hs, sl: (0, 0, heads + h))
    v_s = pl.BlockSpec(whole, lambda h, t, s, hs, sl: (0, 0, 2 * heads + h))
    hk_s = pl.BlockSpec(edge, lambda h, t, s, hs, sl: (0, 0, h))
    hv_s = pl.BlockSpec(edge, lambda h, t, s, hs, sl: (0, 0, heads + h))
    row_s = pl.BlockSpec((1, 1, TILE), lambda h, t, s, hs, sl: (t + base, 0, 0))
    lse_s = pl.BlockSpec((1, 1, 1, TILE), lambda h, t, s, hs, sl: (h, t, 0, 0))
    part_s = pl.BlockSpec(
        (1, (tiles - HALO) * TILE, HEAD_DIM), lambda h, t, s, hs, sl: (h, 0, 0)
    )
    any_s = pl.BlockSpec(memory_space=pl.ANY)
    out = jax.ShapeDtypeStruct
    in_specs, args = [q_s, k_s, v_s], [qkv, qkv, qkv]
    if first:
        in_specs += [hk_s, hv_s]
        args += [halo, halo]
    forward = kernel is attn_fwd_kernel
    aliases = {}
    length = tiles * TILE
    scratch = [
        pltpu.VMEM((length, HEAD_DIM), BF),
        pltpu.VMEM((length, HEAD_DIM), BF),
        pltpu.VMEM((SPAN, TILE), F32),
    ]
    part = (heads, (tiles - HALO) * TILE, HEAD_DIM)
    if forward:
        if first:
            aliases = {3 + len(args): 0}
            in_specs += [any_s]
            args += [grads]
        in_specs += [row_s, row_s]
        out_specs = [q_s, lse_s]
        shapes = [out((tiles, TILE, width), BF), out((heads, queries, 1, TILE), F32)]
    else:
        in_specs += [row_s, q_s, lse_s]
        scratch += [pltpu.VMEM((length, HEAD_DIM), F32), pltpu.VMEM((length, HEAD_DIM), F32)]
        if first:
            out_specs = [q_s, hk_s, hk_s, part_s, part_s]
            shapes = [out((tiles, TILE, width), BF)] + [out((HALO, TILE, width), BF)] * 2
            shapes += [out(part, F32)] * 2
        else:
            in_specs += [part_s, part_s, any_s]
            aliases = {3 + len(args) + len(rows): 0}
            out_specs = [q_s, own_s, own_s]
            shapes = [out((tiles, TILE, width), BF)] + [out((tiles, TILE, width), F32)] * 2
            rows = list(rows) + [grads]
    return pl.pallas_call(
        functools.partial(kernel, first),
        grid_spec=pltpu.PrefetchScalarGridSpec(
            num_scalar_prefetch=3,
            grid=(heads, queries),
            in_specs=in_specs,
            out_specs=out_specs,
            scratch_shapes=scratch,
        ),
        out_shape=shapes,
        input_output_aliases=aliases,
        compiler_params=pltpu.CompilerParams(vmem_limit_bytes=VMEM),
        cost_estimate=cost_of(("attn_fwd" if forward else "attn_bwd") + ("_low" if first else "_high")),
        name=("attn_fwd" if forward else "attn_bwd") + ("_low" if first else "_high"),
    )(*scalars, *args, *rows)


def column_rows(z_count, x_count, h_count, rows):
    return [
        ((z, x * h_count + h), ((h * z_count + z) * x_count + x) * rows)
        for z in range(z_count)
        for x in range(x_count)
        for h in range(h_count)
    ]


def token_kernel(pieces, weights, extras, outs, body, keep=False, name=None):
    count = len(pieces)
    wide, kind = pieces[0][0].shape[1], pieces[0][0].dtype
    n_w, n_e, n_o = len(weights), len(extras), len(outs)
    places = []
    out_shapes = []
    for cols, dtype, apart in list(outs) + ([(wide, kind, False)] if keep else []):
        places.append(len(out_shapes))
        shape = jax.ShapeDtypeStruct((TILE if apart else count * TILE, cols), dtype)
        out_shapes += [shape] * (count if apart else 1)
    n_out = len(out_shapes)

    def kernel(*refs):
        tile_refs = refs[:count]
        w_refs = refs[count : count + n_w]
        e_refs = refs[count + n_w : count + n_w + n_e]
        refs = refs[count + n_w + n_e :]
        o_refs = refs[:n_out]
        refs = refs[n_out:]
        x_buf, w_bufs, o_bufs = refs[0], refs[1 : 1 + n_w], refs[1 + n_w : 1 + n_w + n_o]
        x_sem, w_sem, o_sem = refs[1 + n_w + n_o :]
        for at in range(n_w):
            _, moves, rows, cols = weights[at]
            for lead, row in moves:
                if isinstance(lead, int):
                    source = w_refs[at].at[lead : lead + rows]
                else:
                    source = w_refs[at].at[lead + (slice(None), slice(0, cols))]
                pltpu.make_async_copy(
                    source,
                    w_bufs[at].at[row : row + rows],
                    w_sem.at[at],
                ).start()
        for at in range(count):
            row = pieces[at][1]
            pltpu.make_async_copy(
                tile_refs[at].at[row : row + TILE],
                x_buf.at[at * TILE : (at + 1) * TILE],
                x_sem.at[at],
            ).start()
        for at in range(n_w):
            pltpu.make_async_copy(w_bufs[at], w_bufs[at], w_sem.at[at]).wait()

        def rows_of(at):
            return pl.ds(pl.multiple_of(at * TILE, TILE), TILE)

        bufs = list(o_bufs) + ([x_buf] if keep else [])

        def step(at, carry):
            rows = rows_of(at)
            pltpu.make_async_copy(x_buf.at[rows], x_buf.at[rows], x_sem.at[at]).wait()
            found = body(x_buf[rows, :], rows, w_bufs, e_refs)
            for i in range(n_o):
                o_bufs[i][rows, :] = found[i]
            for i in range(len(bufs)):
                if i < n_o and outs[i][2]:
                    for own in range(count):

                        @pl.when(at == own)
                        def _():
                            pltpu.make_async_copy(
                                bufs[i].at[rows], o_refs[places[i] + own], o_sem.at[i, at]
                            ).start()

                else:
                    pltpu.make_async_copy(
                        bufs[i].at[rows], o_refs[places[i]].at[rows], o_sem.at[i, at]
                    ).start()
            return carry

        lax.fori_loop(0, count, step, 0)

        def finish(at, carry):
            rows = rows_of(at)
            for i in range(len(bufs)):
                pltpu.make_async_copy(bufs[i].at[rows], bufs[i].at[rows], o_sem.at[i, at]).wait()
            return carry

        lax.fori_loop(0, count, finish, 0)

    any_spec = pl.BlockSpec(memory_space=pl.ANY)
    w_shapes = [(len(moves) * rows, cols) for _, moves, rows, cols in weights]
    return pl.pallas_call(
        kernel,
        in_specs=[any_spec] * (count + n_w) + [pl.BlockSpec(memory_space=pltpu.VMEM)] * n_e,
        out_specs=[any_spec] * n_out,
        out_shape=out_shapes,
        scratch_shapes=[
            pltpu.VMEM((count * TILE, wide), kind),
            *[pltpu.VMEM(shape, BF) for shape in w_shapes],
            *[pltpu.VMEM((count * TILE, c), t) for c, t, _ in outs],
            pltpu.SemaphoreType.DMA((count,)),
            pltpu.SemaphoreType.DMA((max(n_w, 1),)),
            pltpu.SemaphoreType.DMA((n_o + 1, count)),
        ],
        compiler_params=pltpu.CompilerParams(vmem_limit_bytes=VMEM),
        cost_estimate=cost_of(name),
        name=name,
    )(*[p[0] for p in pieces], *[w[0] for w in weights], *extras)


def tokens_product(left, right, name):
    tokens, cols = left.shape
    wide = right.shape[1]
    block = min(256, cols)

    def kernel(a_ref, b_ref, o_ref):
        o_ref[...] = lax.dot_general(
            a_ref[...], b_ref[...], ROWS, preferred_element_type=F32
        ).astype(BF)

    return pl.pallas_call(
        kernel,
        grid=(cols // block,),
        in_specs=[
            pl.BlockSpec((tokens, block), lambda i: (0, i)),
            pl.BlockSpec((tokens, wide), lambda i: (0, 0)),
        ],
        out_specs=pl.BlockSpec((block, wide), lambda i: (i, 0)),
        out_shape=jax.ShapeDtypeStruct((cols, wide), BF),
        compiler_params=pltpu.CompilerParams(vmem_limit_bytes=VMEM),
        cost_estimate=cost_of(name),
        name=name,
    )(left, right)


def rows_kernel(array, shape, dtype, moves, name):
    def kernel(a_ref, o_ref):
        for a_lead, a_col, o_lead, o_col, cols in moves:
            source, target = slice(a_col, a_col + cols), slice(o_col, o_col + cols)
            found = a_ref[:, source] if a_lead is None else a_ref[a_lead, :, source]
            if o_lead is None:
                o_ref[:, target] = found.astype(dtype)
            else:
                o_ref[o_lead, :, target] = found.astype(dtype)

    return pl.pallas_call(
        kernel,
        in_specs=[pl.BlockSpec(memory_space=pltpu.VMEM)],
        out_specs=pl.BlockSpec(memory_space=pltpu.VMEM),
        out_shape=jax.ShapeDtypeStruct(shape, dtype),
        compiler_params=pltpu.CompilerParams(vmem_limit_bytes=VMEM),
        cost_estimate=cost_of(name),
        name=name,
    )(array)


def shards(
    layer_input,
    lengths,
    ln1_gain,
    ln1_bias,
    w_qkv,
    bias_query,
    bias_value,
    w_out,
    bias_out,
    ln2_gain,
    ln2_bias,
    w_up,
    bias_up,
    w_down,
    bias_down,
    cotangent,
):
    nh = lax.axis_size("head")
    nb = lax.axis_size("blk")
    nx = 2
    nz = nb // nx
    members = nx * nh
    rows = D // (nh * nb)
    ff_rows = FF // (nh * nb)
    ff_own = nz * ff_rows
    heads = HEADS // members
    width = heads * HEAD_DIM
    head_at = lax.axis_index("head")
    blk_at = lax.axis_index("blk")
    x_at = lax.rem(blk_at, nx)
    z_at = lax.div(blk_at, nx)
    both = ("head", "blk")
    plane = [[h * nb + z * nx + x for x in range(nx) for h in range(nh)] for z in range(nz)]
    column = [[z * nx + x for z in range(nz)] for x in range(nx)]

    def to_core(t):
        return lax.ppermute(t, "head", [(h, h ^ 1) for h in range(nh)])

    def to_y(t):
        return lax.ppermute(t, "head", [(h, h ^ 2) for h in range(nh)])

    def to_x(t):
        return lax.ppermute(t, "blk", [(b, b ^ 1) for b in range(nb)])

    def up_z(t, sources):
        pairs = [(z * nx + x, (z + 1) * nx + x) for z in sources for x in range(nx)]
        return lax.ppermute(t, "blk", pairs)

    def down_z(t, sources):
        pairs = [(z * nx + x, (z - 1) * nx + x) for z in sources for x in range(nx)]
        return lax.ppermute(t, "blk", pairs)

    def to_diag(t):
        return lax.ppermute(
            t, both, [(h * nb + b, (h ^ 2) * nb + (b ^ 1)) for h in range(nh) for b in range(nb)]
        )

    def gather_plane(own):
        same = [own, to_y(own), to_x(own), to_diag(own)]
        return same + [to_core(t) for t in same]

    def scatter_start(mine, other):
        kept = [mine[at].astype(F32) + to_core(other[at]).astype(F32) for at in (3, 1, 2, 0)]
        sent = tuple(t.astype(BF) for t in kept[:3])
        return lax.optimization_barrier(sent), kept[3]

    def scatter_end(sent, kept):
        arrived = to_diag(sent[0]), to_y(sent[1]), to_x(sent[2])
        return kept + sum(t.astype(F32) for t in arrived)

    def plane_a2a(t):
        return lax.all_to_all(
            t, both, split_axis=0, concat_axis=0, tiled=True, axis_index_groups=plane
        )

    def column_a2a(t):
        return lax.all_to_all(
            t, "blk", split_axis=0, concat_axis=0, tiled=True, axis_index_groups=column
        )

    def gather_z(t):
        return lax.all_gather(t, "blk", axis=0, tiled=False, axis_index_groups=column)

    def scatter_z(t):
        return lax.psum_scatter(
            t, "blk", scatter_dimension=0, tiled=False, axis_index_groups=column
        )

    me = x_at * nh + head_at
    slots, halo_slots = [], []
    for tile in range(members):
        diff = jnp.bitwise_xor(me, tile)
        slots.append((diff & 1) * 4 + ((diff >> 2) & 1) * 2 + ((diff >> 1) & 1))
    for tile in range(HALO):
        diff = jnp.bitwise_xor(head_at, tile)
        halo_slots.append((diff & 1) * 2 + ((diff >> 1) & 1))
    slots = jnp.stack(slots).astype(jnp.int32)
    halo_slots = jnp.stack(halo_slots).astype(jnp.int32)
    head_ids = (head_at * nx + x_at) * heads + jnp.arange(heads, dtype=jnp.int32)
    slopes = 2.0 ** (-8.0 * (head_ids.astype(F32) + 1.0) / HEADS)
    scalars = (slots, halo_slots, slopes)
    group_tokens = members * TOK_DEV
    local = jnp.arange(group_tokens, dtype=jnp.int32)
    first = z_at * group_tokens

    def document_at(places):
        positions = first + places
        sequence = lax.div(positions, SEQ_LEN)
        within = positions - sequence * SEQ_LEN
        picked = sequence[:, None] == jnp.arange(lengths.shape[0], dtype=jnp.int32)[None, :]
        row_lengths = jnp.sum(jnp.where(picked[:, :, None], lengths[None, :, :], 0), axis=1)
        ends = jnp.cumsum(row_lengths, axis=1)
        past = ends <= within[:, None]
        valid = (jnp.sum(past.astype(jnp.int32), axis=1) < DOCS).astype(F32)
        return valid, sequence * SEQ_LEN + jnp.sum(jnp.where(past, row_lengths, 0), axis=1)

    valid, doc_start = document_at(local)
    slot = jnp.arange(members, dtype=jnp.int32)
    slot_diff = ((slot >> 1) & 1) * 4 + (slot & 1) * 2 + (slot >> 2)
    slot_tile = jnp.bitwise_xor(me, slot_diff)
    slot_places = (slot_tile[:, None] * TILE + jnp.arange(TILE, dtype=jnp.int32)[None]).reshape(-1)
    valid_slot = document_at(slot_places)[0].reshape(group_tokens, 1)
    low = doc_start - first + WINDOW - lax.div(local, TILE) * TILE
    low = low.reshape(members, 1, TILE)
    valid_tiles = valid.reshape(members, 1, TILE)

    def after(t, *others):
        return lax.optimization_barrier((t,) + others)[0]

    def pin(flag, t, *others):
        return after(t, *others) if flag else t

    x_own = layer_input.reshape(TOK_DEV, D)
    cot_own = cotangent.reshape(TOK_DEV, D)

    small = jnp.concatenate(
        [ln1_gain, ln1_bias, bias_query, bias_value, bias_out, ln2_gain, ln2_bias, bias_down, bias_up]
    )
    small = plane_a2a(jnp.broadcast_to(small, (members,) + small.shape))
    small_all = column_a2a(jnp.broadcast_to(small, (nz,) + small.shape))
    bias_u = lax.dynamic_index_in_dim(small_all, me, 1, keepdims=False)[:, 8 * rows :]
    bias_u = bias_u.reshape(ff_own).astype(F32)
    small_all = small_all[:, :, : 8 * rows]
    vectors = (
        small_all.reshape(nz, nx, nh, 8, rows).transpose(3, 2, 0, 1, 4).reshape(8, D).astype(F32)
    )
    gain_one, shift_one, bias_q, bias_v, bias_o, gain_two, shift_two, bias_d = vectors
    own_cols = (head_at * nx + x_at) * width
    bias_qkv = jnp.concatenate(
        [
            lax.dynamic_slice_in_dim(bias_q, own_cols, width),
            jnp.zeros((width,), F32),
            lax.dynamic_slice_in_dim(bias_v, own_cols, width),
        ]
    )

    near = [(x, h) for x in range(nx) for h in range(nh)]
    qkv_moves = [
        (None, p * D + (h * nx + x) * width, at, p * width, width)
        for at, (x, h) in enumerate(near)
        for p in range(3)
    ]
    up_moves = [
        (None, ((h * nz + z) * nx + x) * ff_rows, at, z * ff_rows, ff_rows)
        for at, (x, h) in enumerate(near)
        for z in range(nz)
    ]
    qkv_col = plane_a2a(
        rows_kernel(w_qkv, (members, rows, 3 * width), BF, qkv_moves, "qkv_split")
    )
    up_col = plane_a2a(
        after(rows_kernel(w_up, (members, rows, ff_own), BF, up_moves, "up_split"), qkv_col)
    )
    out_cols = w_out.reshape(rows, members, D // members).transpose(1, 0, 2)
    first_z = gather_z(jnp.concatenate([qkv_col, out_cols], axis=2))
    up_z = gather_z(after(up_col, first_z))
    down_w = gather_z(pin(F['agd'], w_down, up_z)).reshape(ff_own, D)

    def sent_rows(t):
        return t.reshape(nh, nz, nx, rows, -1).transpose(1, 2, 0, 3, 4).reshape(nz, members, rows, -1)

    order = column_rows(nz, nx, nh, rows)
    half_z = nz // 2
    halves = first_z[:, :, :, 3 * width :].transpose(0, 2, 1, 3).reshape(2, half_z, rows, D)
    mine = jnp.where(x_at == 0, halves[0], halves[1])
    theirs = to_x(jnp.where(x_at == 0, halves[1], halves[0]))
    low_half = jnp.where(x_at == 0, mine, theirs)
    high_half = jnp.where(x_at == 0, theirs, mine)
    out_w = jnp.stack([low_half, high_half], axis=1).reshape(width, D)

    rows_in = x_own.astype(F32)
    normed_in, inv_in = normalize(rows_in)

    def whole(arrays):
        return [(t, 0) for t in arrays]

    def in_plane(array, weights, body, name):
        def side(at):
            first = at * members // 2
            return token_kernel(
                [(array, (first + i) * TILE) for i in range(members // 2)],
                [weights],
                [],
                [(D, BF, True)],
                body,
                name=name,
            )

        other = side(1)
        return scatter_start(side(0), other)

    def times(x, at, w, e):
        return (jnp.dot(x, w[0][...], preferred_element_type=F32).astype(BF),)

    def times_t(x, at, w, e):
        return (lax.dot_general(x, w[0][...], COLS, preferred_element_type=F32).astype(BF),)

    def qkv_body(x, at, w, e):
        normed = normalize(x.astype(F32))[0]
        lowered = (normed * e[0][...] + e[1][...]).astype(BF)
        return (jnp.dot(lowered, w[0][...], preferred_element_type=F32) + e[2][...]).astype(BF), lowered

    x_tiles = gather_plane(pin(F['x1'], x_own, small))
    if F['cot'] == 0:
        cot_tiles = gather_plane(after(cot_own, *x_tiles[:4]))
    if F['cot'] == 3:
        cot_tiles = gather_plane(cot_own)
    if F['cotk'] and F['cot'] in (0, 3):
        x_tiles = list(after(tuple(x_tiles), *cot_tiles[:4]))
    x_tiles = list(pin(F['upc'], tuple(x_tiles), up_col))
    qkv, ln1 = token_kernel(
        whole(x_tiles),
        [(first_z, order, rows, 3 * width)],
        [
            gain_one.reshape(1, D),
            shift_one.reshape(1, D),
            bias_qkv.reshape(1, -1),
        ],
        [(3 * width, BF, False), (D, BF, False)],
        qkv_body,
        name="qkv_fwd",
    )
    qkv = qkv.reshape(members, TILE, 3 * width)
    kv = qkv[:, :, width:].reshape(2, 2, 2, TILE, 2 * width)
    kv = jnp.where(x_at == 0, kv[:, 1], kv[:, 0]).reshape(HALO, TILE, 2 * width)
    halo = lax.ppermute(kv, "blk", [(b, b + nx) for b in range(nb - nx)])
    if F["cot"] in (1, 2):
        cot_tiles = gather_plane(after(cot_own, qkv if F["cot"] == 1 else halo))
    halo = pin(F["cotb"], halo, *cot_tiles[:4])
    ctx, lse_high = attention_call(
        attn_fwd_kernel, False, scalars, qkv, None, [low, valid_tiles], heads, None
    )
    ctx, lse_low = attention_call(
        attn_fwd_kernel, True, scalars, qkv, halo, [low, valid_tiles], heads, ctx
    )
    ctx = ctx.reshape(group_tokens, width)
    ctx = pin(F['cotctx'], ctx, *cot_tiles[:4])
    half = group_tokens // 2
    attn_sent, attn_kept = in_plane(ctx, (out_w, [(0, 0)], width, D), times, "out_fwd")
    attn_sum = scatter_end(attn_sent, attn_kept)
    middle = rows_in + (attn_sum + bias_o)
    normed_mid, inv_mid = normalize(middle)
    ln2_own = (normed_mid * gain_two + shift_two).astype(BF)

    def up_body(x, at, w, e):
        v = jnp.dot(x, w[0][...], preferred_element_type=F32) + e[0][...]
        squared = v * v
        t = jnp.tanh(v * (0.7978845608028654 + 0.7978845608028654 * 0.044715 * squared))
        half_up = 0.5 + 0.5 * t
        slope = half_up + (0.5 * v) * (1.0 - t * t) * (
            0.7978845608028654 + 3.0 * 0.7978845608028654 * 0.044715 * squared
        )
        return (v * half_up).astype(BF), slope.astype(BF)

    active, up_slope, ln2 = token_kernel(
        whole(gather_plane(ln2_own)),
        [(up_z, order, rows, ff_own)],
        [bias_u.reshape(1, ff_own)],
        [(ff_own, BF, False), (ff_own, BF, False)],
        up_body,
        keep=True,
        name="up_fwd",
    )

    cot_full = cot_own.astype(F32)
    def down_body(x, at, w, e):
        d_act = lax.dot_general(x, w[0][...], COLS, preferred_element_type=F32)
        d_pre = (d_act * w[2][at, :].astype(F32)).astype(BF)
        part = lax.dot_general(d_pre, w[1][...], COLS, preferred_element_type=F32)
        return d_pre, part.astype(BF)

    def down_back(side):
        return token_kernel(
            whole(cot_tiles[side * members // 2 : (side + 1) * members // 2]),
            [
                (down_w, [(0, 0)], ff_own, D),
                (up_z, order, rows, ff_own),
                (up_slope, [(side * half, 0)], half, ff_own),
            ],
            [],
            [(ff_own, BF, False), (D, BF, True)],
            down_body,
            name="down_back",
        )

    d_up_other, *ln2_other = down_back(1)
    d_up_mine, *ln2_mine = down_back(0)
    ln2_sent, ln2_kept = scatter_start(ln2_mine, ln2_other)
    d_ln2 = scatter_end(ln2_sent, ln2_kept)
    cot = token_kernel(
        whole(pin(F['gd_lo'], tuple(cot_tiles), *ln2_sent)), [], [], [], lambda *_: (), keep=True, name="collect"
    )[0]
    g_down = tokens_product(active, cot, "down_grad")
    grad_w_down = scatter_z(g_down.reshape(nz, ff_rows, D)).astype(F32)
    d_up = jnp.concatenate([d_up_mine, d_up_other], axis=0)
    g_up = tokens_product(ln2, pin(F['gu_lo'], d_up, g_down), "up_grad")
    d_ln2 = pin(F["gu_hi"] == 1, d_ln2, g_up)
    d_ln2 = pin(F["gd_hi"] == 1, d_ln2, g_down)
    up_part = g_up
    up_sum = scatter_z(sent_rows(g_up))
    g_up = plane_a2a(up_sum)
    grad_w_up = rows_kernel(
        g_up, (rows, FF), F32, [(m[2], m[3], m[0], m[1], m[4]) for m in up_moves], "up_join"
    )
    grad_b_up = jnp.sum(d_up.astype(F32), axis=0)
    d_middle = cot_full + norm_back(d_ln2 * gain_two, normed_mid, inv_mid)
    d_attn_own = d_middle.astype(BF)
    down_sent, down_kept = in_plane(
        pin(F['df_lo'] == 1, pin(F['df_lo'] == 2, active, *ln2_sent), d_attn_own), (down_w, [(0, 0)], ff_own, D), times, "down_fwd"
    )

    d_attn_tiles = gather_plane(d_attn_own)
    d_attn_tiles = list(pin(F['df_hi'] == 1, pin(F['rsd'] == 1, pin(F['gd_hi'] == 2, pin(F['gu_hi'] == 2, tuple(d_attn_tiles), up_part), g_down), grad_w_down), *down_sent))

    def ctx_body(x, at, w, e):
        found = lax.dot_general(x, w[0][...], COLS, preferred_element_type=F32)
        return ((found * e[0][at, :]).astype(BF),)

    d_ctx, d_attn = token_kernel(
        whole(d_attn_tiles),
        [(out_w, [(0, 0)], width, D)],
        [valid_slot],
        [(width, BF, False)],
        ctx_body,
        keep=True,
        name="ctx_back",
    )
    down_sent = pin(F['lo_lo'], down_sent, *d_attn_tiles)
    down_sum = scatter_end(down_sent, down_kept)
    output = (middle + (down_sum + bias_d)).astype(BF)
    d_ctx = d_ctx.reshape(members, TILE, width)
    d_q, d_hk, d_hv, d_k, d_v = attention_call(
        attn_bwd_kernel, True, scalars, qkv, halo, [low, d_ctx, lse_low], heads, None
    )
    def step_back(t):
        return lax.ppermute(t, "blk", [(b + nx, b) for b in range(nb - nx)])

    if F["hsplit"]:
        back = jnp.concatenate([step_back(d_hk), step_back(d_hv)], axis=-1).astype(F32)
    else:
        back = step_back(jnp.concatenate([d_hk, d_hv], axis=-1)).astype(F32)
    g_out = tokens_product(ctx, pin(F['go_lo'], d_attn, d_hk), "out_grad")
    g_out_part = g_out
    g_out = pin(F["lo_hi"] == 4, g_out, output)
    g_out = g_out.reshape(half_z, nx, rows, D)
    g_mine = jnp.where(x_at == 0, g_out[:, 0], g_out[:, 1])
    g_theirs = to_x(jnp.where(x_at == 0, g_out[:, 1], g_out[:, 0]))
    g_out = jnp.concatenate(
        [jnp.where(x_at == 0, g_mine, g_theirs), jnp.where(x_at == 0, g_theirs, g_mine)], axis=0
    )
    grad_w_out = scatter_z(g_out).astype(F32)
    d_q = pin(F["go_hi"], d_q, g_out_part)
    d_q = pin(F["lo_hi"] == 1, d_q, output)
    d_q = pin(F["df_hi"] == 2, d_q, *down_sent)
    d_q = pin(F["rsd"] == 2, d_q, grad_w_down)
    d_q = pin(F["rsu"] == 2, d_q, up_sum)
    d_q, d_k, d_v = attention_call(
        attn_bwd_kernel, False, scalars, qkv, None, [low, d_ctx, lse_high, d_k, d_v], heads, d_q
    )
    back = back.reshape(2, 1, 2, TILE, 2 * width)
    second = (jnp.arange(2) != x_at).reshape(1, 2, 1, 1, 1)
    d_kv = jnp.concatenate([d_k, d_v], axis=-1).reshape(2, 2, 2, TILE, 2 * width)
    d_kv = pin(F['gkv'], d_kv, g_out)
    d_kv = pin(F['lo_hi'] == 2, d_kv, output)
    d_kv = (d_kv + jnp.where(second, back, 0.0)).astype(BF).reshape(group_tokens, 2 * width)
    d_q = d_q.reshape(group_tokens, width)
    d_proj = jnp.concatenate([d_q, d_kv], axis=1)
    g_qkv_part = tokens_product(ln1, pin(F['rsd'] == 3, pin(F['rsu'] == 3, d_proj, up_sum), grad_w_down), "qkv_grad")
    g_qkv = plane_a2a(scatter_z(sent_rows(g_qkv_part)))
    grad_w_qkv = rows_kernel(
        g_qkv, (rows, 3 * D), F32, [(m[2], m[3], m[0], m[1], m[4]) for m in qkv_moves], "qkv_join"
    )
    d_proj = pin(F['gq'], d_proj, g_qkv_part)
    d_proj = pin(F['lo_hi'] == 3, d_proj, output)
    d_proj = pin(F['rsd'] == 4, d_proj, grad_w_down)
    d_proj = pin(F['rsu'] == 4, d_proj, up_sum)
    d_proj = pin(F['rso'] == 4, d_proj, grad_w_out)
    d_ln1 = scatter_end(*in_plane(d_proj, (first_z, order, rows, 3 * width), times_t, "qkv_back"))
    grad_input = d_middle + norm_back(d_ln1 * gain_one, normed_in, inv_in)

    def placed(t):
        return lax.dynamic_update_slice_in_dim(jnp.zeros((D,), F32), t, own_cols, 0)

    sums = jnp.stack(
        [
            jnp.sum(d_ln1 * normed_in, axis=0),
            jnp.sum(d_ln1, axis=0),
            placed(jnp.sum(d_q.astype(F32), axis=0)),
            placed(jnp.sum(d_kv[:, width:].astype(F32), axis=0)),
            jnp.sum(d_attn_own.astype(F32), axis=0),
            jnp.sum(d_ln2 * normed_mid, axis=0),
            jnp.sum(d_ln2, axis=0),
            jnp.sum(cot_full, axis=0),
        ]
    )
    sums = sums.reshape(8, nh, nz, nx, rows).transpose(3, 1, 2, 0, 4)
    sums = jnp.sum(plane_a2a(sums.reshape(members, nz, 8 * rows)), axis=0)
    sums = jnp.concatenate([sums, grad_b_up.reshape(nz, ff_rows)], axis=1)
    sums = jnp.sum(
        column_a2a(sums),
        axis=0,
    )
    vec = sums[: 8 * rows].reshape(8, rows)
    return (
        output.reshape(1, TOK_DEV, D),
        grad_input.reshape(1, TOK_DEV, D),
        vec[0],
        vec[1],
        grad_w_qkv,
        vec[2],
        vec[3],
        grad_w_out,
        vec[4],
        vec[5],
        vec[6],
        grad_w_up,
        sums[8 * rows :],
        grad_w_down,
        vec[7],
    )


def solution(mesh):
    split = P(("head", "blk"))
    wide = P(("head", "blk"), None)
    tokens = P("blk", "head", None)
    return jax.shard_map(
        shards,
        mesh=mesh,
        in_specs=(
            tokens, P(), split, split, wide, split, split, wide, split, split, split, wide, split, wide, split, tokens,
        ),
        out_specs=(
            tokens, tokens, split, split, wide, split, split, wide, split, split, split, wide, split, wide, split,
        ),
        check_vma=False,
    )
```

```python
import functools

import jax
import jax.numpy as jnp
from jax import lax
from jax.experimental import pallas as pl
from jax.experimental.pallas import tpu as pltpu
from jax.sharding import PartitionSpec as P

D = 2048
HEADS = 16
HEAD_DIM = 128
FF = 8192
TOK_DEV = 256
WINDOW = 1024
SEQ_LEN = 8192
DOCS = 4

EPS = 1e-05
NEG = -1e30
BF = jnp.bfloat16
F32 = jnp.float32
ROWS = (((0,), (0,)), ((), ()))
COLS = (((1,), (1,)), ((), ()))

TILE = 256
HALO = WINDOW // TILE
SPAN = WINDOW + TILE
VMEM = 48 * 1024 * 1024
F = dict(x1=0, cot=1, cotk=1, cotctx=1, cotb=0, gd_lo=1, gd_hi=2, gu_lo=1, gu_hi=0, rsd=1, rsu=4, rso=0, df_lo=0, df_hi=2, lo_lo=1, lo_hi=3, go_lo=0, go_hi=0, gkv=1, hsplit=1, gq=0, agd=1, upc=1, g2x=0, g2c=1, g2l=1, g2a=0, s2a=1, s2l=0, s2o=0, s2i=1, suml=0, split=0, gqr=0, upj=0, gdp=1, colp=0, uph=0, outh=0, arr=0)
COST = dict(qkv_fwd=20, out_fwd=3, up_fwd=0, down_back=0, collect=20, down_grad=20, up_grad=0, down_fwd=0, ctx_back=20, out_grad=0, qkv_grad=8, qkv_back=20, attn_fwd_low=1, attn_fwd_high=20, attn_bwd_low=20, attn_bwd_high=8, qkv_split=8, up_split=3, up_join=3, qkv_join=0, join_grads=0)


def cost_of(name):
    flops = int(COST[name] * 1e9)
    return pl.CostEstimate(flops=flops, bytes_accessed=4096, transcendentals=0)


def normalize(values):
    center = values - jnp.mean(values, axis=-1, keepdims=True)
    inv_scale = lax.rsqrt(jnp.mean(center * center, axis=-1, keepdims=True) + EPS)
    return (center * inv_scale, inv_scale)


def norm_back(d_hat, normed, inv_scale):
    return inv_scale * (
        d_hat
        - jnp.mean(d_hat, axis=-1, keepdims=True)
        - normed * jnp.mean(d_hat * normed, axis=-1, keepdims=True)
    )


def gelu_tanh(values):
    return (
        0.5
        * values
        * (1.0 + jnp.tanh(0.7978845608028654 * (values + 0.044715 * values * values * values)))
    )


def fill_tiles(buffer, halo_ref, own_ref, halo_slots, slots):
    if halo_ref is None:
        sources = [(own_ref, slots, tile) for tile in range(own_ref.shape[0])]
    else:
        sources = [(halo_ref, halo_slots, tile) for tile in range(HALO)]
        sources += [(own_ref, slots, tile) for tile in range(own_ref.shape[0] - HALO)]
    for at, (ref, order, tile) in enumerate(sources):
        buffer[at * TILE : (at + 1) * TILE, :] = ref[order[tile]]


def fill_bias(bias, slope):
    key = lax.broadcasted_iota(jnp.int32, (SPAN, TILE), 0)
    query = lax.broadcasted_iota(jnp.int32, (SPAN, TILE), 1)
    rel = key - WINDOW - query
    bias[...] = jnp.where((rel <= 0) & (rel > -WINDOW), slope * rel.astype(F32), NEG)


def masked_scores(q, keys, bias, low_row):
    scores = lax.dot_general(keys, q, COLS, preferred_element_type=F32)
    scores = scores * HEAD_DIM ** (-0.5) + bias
    key = lax.broadcasted_iota(jnp.int32, (SPAN, TILE), 0)
    return jnp.where(key >= low_row, scores, NEG)


def attn_fwd_kernel(first, slots, halo_slots, slopes, q_ref, k_ref, v_ref, *refs):
    hk_ref, hv_ref, refs = (refs[0], refs[1], refs[3:]) if first else (None, None, refs)
    low_ref, valid_ref, ctx_ref, lse_ref, kbuf, vbuf, bias = refs
    head = pl.program_id(0)
    tile = pl.program_id(1)

    @pl.when(tile == 0)
    def _():
        fill_tiles(kbuf, hk_ref, k_ref, halo_slots, slots)
        fill_tiles(vbuf, hv_ref, v_ref, halo_slots, slots)
        fill_bias(bias, slopes[head])

    start = pl.multiple_of(tile * TILE, TILE)
    scores = masked_scores(q_ref[0], kbuf[pl.ds(start, SPAN), :], bias[...], low_ref[0])
    highest = jnp.max(scores, axis=0, keepdims=True)
    expo = jnp.exp(scores - highest)
    summed = jnp.sum(expo, axis=0, keepdims=True)
    lse_ref[0, 0] = highest + jnp.log(summed)
    context = lax.dot_general(
        vbuf[pl.ds(start, SPAN), :], expo.astype(BF), ROWS, preferred_element_type=F32
    )
    context = context * (valid_ref[0] / summed)
    ctx_ref[0] = context.T.astype(BF)


def attn_bwd_kernel(first, slots, halo_slots, slopes, q_ref, k_ref, v_ref, *refs):
    hk_ref, hv_ref, refs = (refs[0], refs[1], refs[2:]) if first else (None, None, refs)
    low_ref, dctx_ref, lse_ref = refs[:3]
    if first:
        dq_ref, dhk_ref, dhv_ref, dk_ref, dv_ref = refs[3:8]
    else:
        dk_in, dv_in, _, dq_ref, dk_ref, dv_ref = refs[3:9]
    kbuf, vbuf, bias, dkbuf, dvbuf = refs[-5:]
    head = pl.program_id(0)
    tile = pl.program_id(1)
    tiles = k_ref.shape[0]
    own = tiles - HALO
    kept = own * TILE

    @pl.when(tile == 0)
    def _():
        fill_tiles(kbuf, hk_ref, k_ref, halo_slots, slots)
        fill_tiles(vbuf, hv_ref, v_ref, halo_slots, slots)
        fill_bias(bias, slopes[head])
        if first:
            dkbuf[...] = jnp.zeros_like(dkbuf)
            dvbuf[...] = jnp.zeros_like(dvbuf)
        else:
            for buffer, start in ((dkbuf, dk_in), (dvbuf, dv_in)):
                buffer[:kept, :] = start[0]
                buffer[kept:, :] = jnp.zeros((buffer.shape[0] - kept, HEAD_DIM), F32)

    start = pl.multiple_of(tile * TILE, TILE)
    rows = pl.ds(start, SPAN)
    q = q_ref[0]
    d_ctx = dctx_ref[0]
    keys = kbuf[rows, :]
    scores = masked_scores(q, keys, bias[...], low_ref[0])
    probs = jnp.exp(scores - lse_ref[0, 0])
    d_probs = lax.dot_general(vbuf[rows, :], d_ctx, COLS, preferred_element_type=F32)
    delta = jnp.sum(probs * d_probs, axis=0, keepdims=True)
    d_scores = (probs * (d_probs - delta)).astype(BF)
    scale = HEAD_DIM ** (-0.5)
    d_query = lax.dot_general(d_scores, keys, ROWS, preferred_element_type=F32)
    dq_ref[0] = (d_query * scale).astype(BF)
    dkbuf[rows, :] += jnp.dot(d_scores, q, preferred_element_type=F32)
    dvbuf[rows, :] += jnp.dot(probs.astype(BF), d_ctx, preferred_element_type=F32)

    @pl.when(tile == pl.num_programs(1) - 1)
    def _():
        if first:
            for at in range(HALO):
                piece = slice(at * TILE, (at + 1) * TILE)
                dhk_ref[halo_slots[at]] = (dkbuf[piece, :] * scale).astype(BF)
                dhv_ref[halo_slots[at]] = dvbuf[piece, :].astype(BF)
            dk_ref[0] = dkbuf[HALO * TILE :, :]
            dv_ref[0] = dvbuf[HALO * TILE :, :]
        else:
            for at in range(tiles):
                piece = slice(at * TILE, (at + 1) * TILE)
                dk_ref[slots[at]] = dkbuf[piece, :] * scale
                dv_ref[slots[at]] = dvbuf[piece, :]


def attention_call(kernel, first, scalars, qkv, halo, rows, heads, grads):
    tiles = qkv.shape[0]
    queries = HALO if first else tiles - HALO
    base = 0 if first else HALO
    width = heads * HEAD_DIM
    block = (1, TILE, HEAD_DIM)
    whole = (tiles, TILE, HEAD_DIM)
    edge = (HALO, TILE, HEAD_DIM)
    q_s = pl.BlockSpec(block, lambda h, t, s, hs, sl: (s[t + base], 0, h))
    own_s = pl.BlockSpec(whole, lambda h, t, s, hs, sl: (0, 0, h))
    k_s = pl.BlockSpec(whole, lambda h, t, s, hs, sl: (0, 0, heads + h))
    v_s = pl.BlockSpec(whole, lambda h, t, s, hs, sl: (0, 0, 2 * heads + h))
    hk_s = pl.BlockSpec(edge, lambda h, t, s, hs, sl: (0, 0, h))
    hv_s = pl.BlockSpec(edge, lambda h, t, s, hs, sl: (0, 0, heads + h))
    row_s = pl.BlockSpec((1, 1, TILE), lambda h, t, s, hs, sl: (t + base, 0, 0))
    lse_s = pl.BlockSpec((1, 1, 1, TILE), lambda h, t, s, hs, sl: (h, t, 0, 0))
    part_s = pl.BlockSpec(
        (1, (tiles - HALO) * TILE, HEAD_DIM), lambda h, t, s, hs, sl: (h, 0, 0)
    )
    any_s = pl.BlockSpec(memory_space=pl.ANY)
    out = jax.ShapeDtypeStruct
    in_specs, args = [q_s, k_s, v_s], [qkv, qkv, qkv]
    if first:
        in_specs += [hk_s, hv_s]
        args += [halo, halo]
    forward = kernel is attn_fwd_kernel
    aliases = {}
    length = tiles * TILE
    scratch = [
        pltpu.VMEM((length, HEAD_DIM), BF),
        pltpu.VMEM((length, HEAD_DIM), BF),
        pltpu.VMEM((SPAN, TILE), F32),
    ]
    part = (heads, (tiles - HALO) * TILE, HEAD_DIM)
    if forward:
        if first:
            aliases = {3 + len(args): 0}
            in_specs += [any_s]
            args += [grads]
        in_specs += [row_s, row_s]
        out_specs = [q_s, lse_s]
        shapes = [out((tiles, TILE, width), BF), out((heads, queries, 1, TILE), F32)]
    else:
        in_specs += [row_s, q_s, lse_s]
        scratch += [pltpu.VMEM((length, HEAD_DIM), F32), pltpu.VMEM((length, HEAD_DIM), F32)]
        if first:
            out_specs = [q_s, hk_s, hk_s, part_s, part_s]
            shapes = [out((tiles, TILE, width), BF)] + [out((HALO, TILE, width), BF)] * 2
            shapes += [out(part, F32)] * 2
        else:
            in_specs += [part_s, part_s, any_s]
            aliases = {3 + len(args) + len(rows): 0}
            out_specs = [q_s, own_s, own_s]
            shapes = [out((tiles, TILE, width), BF)] + [out((tiles, TILE, width), F32)] * 2
            rows = list(rows) + [grads]
    return pl.pallas_call(
        functools.partial(kernel, first),
        grid_spec=pltpu.PrefetchScalarGridSpec(
            num_scalar_prefetch=3,
            grid=(heads, queries),
            in_specs=in_specs,
            out_specs=out_specs,
            scratch_shapes=scratch,
        ),
        out_shape=shapes,
        input_output_aliases=aliases,
        compiler_params=pltpu.CompilerParams(vmem_limit_bytes=VMEM),
        cost_estimate=cost_of(("attn_fwd" if forward else "attn_bwd") + ("_low" if first else "_high")),
        name=("attn_fwd" if forward else "attn_bwd") + ("_low" if first else "_high"),
    )(*scalars, *args, *rows)


def column_rows(z_count, x_count, h_count, rows):
    return [
        ((z, x * h_count + h), ((h * z_count + z) * x_count + x) * rows)
        for z in range(z_count)
        for x in range(x_count)
        for h in range(h_count)
    ]


def token_kernel(pieces, weights, extras, outs, body, keep=False, name=None):
    count = len(pieces)
    wide, kind = pieces[0][0][0].shape[1], pieces[0][0][0].dtype
    parts = [
        (at * TILE + i * (TILE // len(arrays)), TILE // len(arrays), row, at)
        for at, (arrays, row) in enumerate(pieces)
        for i in range(len(arrays))
    ]
    n_t = len(parts)
    n_w, n_e, n_o = len(weights), len(extras), len(outs)
    places = []
    out_shapes = []
    for cols, dtype, apart in list(outs) + ([(wide, kind, False)] if keep else []):
        places.append(len(out_shapes))
        shape = jax.ShapeDtypeStruct((TILE if apart else count * TILE, cols), dtype)
        out_shapes += [shape] * (count if apart else 1)
    n_out = len(out_shapes)

    def kernel(*refs):
        tile_refs = refs[:n_t]
        w_refs = refs[n_t : n_t + n_w]
        e_refs = refs[n_t + n_w : n_t + n_w + n_e]
        refs = refs[n_t + n_w + n_e :]
        o_refs = refs[:n_out]
        refs = refs[n_out:]
        x_buf, w_bufs, o_bufs = refs[0], refs[1 : 1 + n_w], refs[1 + n_w : 1 + n_w + n_o]
        x_sem, w_sem, o_sem = refs[1 + n_w + n_o :]
        for at in range(n_w):
            _, moves, rows, cols = weights[at]
            for lead, row in moves:
                if isinstance(lead, int):
                    source = w_refs[at].at[lead : lead + rows]
                else:
                    source = w_refs[at].at[lead + (slice(None), slice(0, cols))]
                pltpu.make_async_copy(
                    source,
                    w_bufs[at].at[row : row + rows],
                    w_sem.at[at],
                ).start()
        for i, (place, size, row, at) in enumerate(parts):
            pltpu.make_async_copy(
                tile_refs[i].at[row : row + size], x_buf.at[place : place + size], x_sem.at[at]
            ).start()
        for at in range(n_w):
            pltpu.make_async_copy(w_bufs[at], w_bufs[at], w_sem.at[at]).wait()

        def rows_of(at):
            return pl.ds(pl.multiple_of(at * TILE, TILE), TILE)

        bufs = list(o_bufs) + ([x_buf] if keep else [])

        def step(at, carry):
            rows = rows_of(at)
            pltpu.make_async_copy(x_buf.at[rows], x_buf.at[rows], x_sem.at[at]).wait()
            found = body(x_buf[rows, :], rows, w_bufs, e_refs)
            for i in range(n_o):
                o_bufs[i][rows, :] = found[i]
            for i in range(len(bufs)):
                if i < n_o and outs[i][2]:
                    for own in range(count):

                        @pl.when(at == own)
                        def _():
                            pltpu.make_async_copy(
                                bufs[i].at[rows], o_refs[places[i] + own], o_sem.at[i, at]
                            ).start()

                else:
                    pltpu.make_async_copy(
                        bufs[i].at[rows], o_refs[places[i]].at[rows], o_sem.at[i, at]
                    ).start()
            return carry

        lax.fori_loop(0, count, step, 0)

        def finish(at, carry):
            rows = rows_of(at)
            for i in range(len(bufs)):
                pltpu.make_async_copy(bufs[i].at[rows], bufs[i].at[rows], o_sem.at[i, at]).wait()
            return carry

        lax.fori_loop(0, count, finish, 0)

    any_spec = pl.BlockSpec(memory_space=pltpu.HBM)
    w_shapes = [(len(moves) * rows, cols) for _, moves, rows, cols in weights]
    return pl.pallas_call(
        kernel,
        in_specs=[any_spec] * (n_t + n_w) + [pl.BlockSpec(memory_space=pltpu.VMEM)] * n_e,
        out_specs=[any_spec] * n_out,
        out_shape=out_shapes,
        scratch_shapes=[
            pltpu.VMEM((count * TILE, wide), kind),
            *[pltpu.VMEM(shape, BF) for shape in w_shapes],
            *[pltpu.VMEM((count * TILE, c), t) for c, t, _ in outs],
            pltpu.SemaphoreType.DMA((count,)),
            pltpu.SemaphoreType.DMA((max(n_w, 1),)),
            pltpu.SemaphoreType.DMA((n_o + 1, count)),
        ],
        compiler_params=pltpu.CompilerParams(vmem_limit_bytes=VMEM),
        cost_estimate=cost_of(name),
        name=name,
    )(*[t for p in pieces for t in p[0]], *[w[0] for w in weights], *extras)


def tokens_product(left, right, name, order=None):
    tokens, cols = left.shape
    wide = right.shape[1]
    if order is None:
        block = min(256, cols)
        shape, out_block, place = (cols, wide), (block, wide), lambda i: (i, 0)
    else:
        z_count, x_count, h_count, rows = order
        block = cols // h_count
        shape = (z_count, x_count, h_count, rows, wide)
        out_block, place = (z_count, x_count, 1, rows, wide), lambda i: (0, 0, i, 0, 0)

    def kernel(a_ref, b_ref, o_ref):
        found = lax.dot_general(a_ref[...], b_ref[...], ROWS, preferred_element_type=F32)
        if order is None:
            o_ref[...] = found.astype(BF)
        else:
            for z in range(z_count):
                for x in range(x_count):
                    start = (z * x_count + x) * rows
                    o_ref[z, x, 0] = found[start : start + rows].astype(BF)

    return pl.pallas_call(
        kernel,
        grid=(cols // block,),
        in_specs=[
            pl.BlockSpec((tokens, block), lambda i: (0, i)),
            pl.BlockSpec((tokens, wide), lambda i: (0, 0)),
        ],
        out_specs=pl.BlockSpec(out_block, place),
        out_shape=jax.ShapeDtypeStruct(shape, BF),
        compiler_params=pltpu.CompilerParams(vmem_limit_bytes=VMEM),
        cost_estimate=cost_of(name),
        name=name,
    )(left, right)


def join_grads(x_row, d_q, d_k, d_v, back):
    tiles, _, width = d_q.shape

    def kernel(x_ref, q_ref, k_ref, v_ref, bk_ref, bv_ref, o_ref):
        second = ((pl.program_id(0) >> 1) & 1) != x_ref[0]
        o_ref[0, :, :width] = q_ref[0]
        for at, (own, back) in enumerate(((k_ref, bk_ref), (v_ref, bv_ref))):
            added = own[0] + jnp.where(second, back[0].astype(F32), 0.0)
            o_ref[0, :, (1 + at) * width : (2 + at) * width] = added.astype(BF)

    tile = pl.BlockSpec((1, TILE, width), lambda i, x: (i, 0, 0))
    edge_k = pl.BlockSpec((1, TILE, width), lambda i, x: ((i >> 2) * 2 + (i & 1), 0, 0))
    edge_v = pl.BlockSpec((1, TILE, width), lambda i, x: ((i >> 2) * 2 + (i & 1), 0, 1))
    return pl.pallas_call(
        kernel,
        grid_spec=pltpu.PrefetchScalarGridSpec(
            num_scalar_prefetch=1,
            grid=(tiles,),
            in_specs=[tile, tile, tile, edge_k, edge_v],
            out_specs=pl.BlockSpec((1, TILE, 3 * width), lambda i, x: (i, 0, 0)),
        ),
        out_shape=jax.ShapeDtypeStruct((tiles, TILE, 3 * width), BF),
        compiler_params=pltpu.CompilerParams(vmem_limit_bytes=VMEM),
        cost_estimate=cost_of("join_grads"),
        name="join_grads",
    )(x_row, d_q, d_k, d_v, back, back)


def rows_kernel(array, shape, dtype, moves, name):
    def kernel(a_ref, o_ref):
        for a_lead, a_col, o_lead, o_col, cols in moves:
            source, target = slice(a_col, a_col + cols), slice(o_col, o_col + cols)
            found = a_ref[:, source] if a_lead is None else a_ref[a_lead, :, source]
            if o_lead is None:
                o_ref[:, target] = found.astype(dtype)
            else:
                o_ref[o_lead, :, target] = found.astype(dtype)

    return pl.pallas_call(
        kernel,
        in_specs=[pl.BlockSpec(memory_space=pltpu.VMEM)],
        out_specs=pl.BlockSpec(memory_space=pltpu.VMEM),
        out_shape=jax.ShapeDtypeStruct(shape, dtype),
        compiler_params=pltpu.CompilerParams(vmem_limit_bytes=VMEM),
        cost_estimate=cost_of(name),
        name=name,
    )(array)


def shards(
    layer_input,
    lengths,
    ln1_gain,
    ln1_bias,
    w_qkv,
    bias_query,
    bias_value,
    w_out,
    bias_out,
    ln2_gain,
    ln2_bias,
    w_up,
    bias_up,
    w_down,
    bias_down,
    cotangent,
):
    nh = lax.axis_size("head")
    nb = lax.axis_size("blk")
    nx = 2
    nz = nb // nx
    members = nx * nh
    rows = D // (nh * nb)
    ff_rows = FF // (nh * nb)
    ff_own = nz * ff_rows
    heads = HEADS // members
    width = heads * HEAD_DIM
    head_at = lax.axis_index("head")
    blk_at = lax.axis_index("blk")
    x_at = lax.rem(blk_at, nx)
    z_at = lax.div(blk_at, nx)
    both = ("head", "blk")
    plane = [[h * nb + z * nx + x for x in range(nx) for h in range(nh)] for z in range(nz)]
    column = [[z * nx + x for z in range(nz)] for x in range(nx)]

    def to_core(t):
        return lax.ppermute(t, "head", [(h, h ^ 1) for h in range(nh)])

    def to_y(t):
        return lax.ppermute(t, "head", [(h, h ^ 2) for h in range(nh)])

    def to_x(t):
        return lax.ppermute(t, "blk", [(b, b ^ 1) for b in range(nb)])

    def up_z(t, sources):
        pairs = [(z * nx + x, (z + 1) * nx + x) for z in sources for x in range(nx)]
        return lax.ppermute(t, "blk", pairs)

    def down_z(t, sources):
        pairs = [(z * nx + x, (z - 1) * nx + x) for z in sources for x in range(nx)]
        return lax.ppermute(t, "blk", pairs)

    def to_diag(t):
        return lax.ppermute(
            t, both, [(h * nb + b, (h ^ 2) * nb + (b ^ 1)) for h in range(nh) for b in range(nb)]
        )

    half_tile = TOK_DEV // 2

    def gather_plane(own, relay):
        if relay:
            top, bottom = own[:half_tile], own[half_tile:]
            x_top, y_bottom = to_x(top), to_y(bottom)
            x_bottom, y_top = to_x(bottom), to_y(top)
            diag = (to_y(x_top), to_x(y_bottom))
            same = [(own,), (y_top, y_bottom), (x_top, x_bottom), diag]
        else:
            same = [(own,), (to_y(own),), (to_x(own),), (to_diag(own),)]
        return same + [tuple(to_core(t) for t in arrays) for arrays in same]

    def scatter_start(mine, other, relay):
        swapped = [to_core(other[at]) for at in (3, 1, 2, 0)]
        halves = (slice(0, half_tile), slice(half_tile, TOK_DEV)) if relay else (slice(None),)
        sent = tuple(
            tuple((mine[at][h].astype(F32) + t[h].astype(F32)).astype(BF) for h in halves)
            for at, t in zip((3, 1, 2), swapped)
        )
        return lax.optimization_barrier(sent), mine[0].astype(F32) + swapped[3].astype(F32)

    def scatter_move(sent):
        if len(sent[0]) == 1:
            return to_diag(sent[0][0]), to_y(sent[1][0]), to_x(sent[2][0])

        def added(a, b):
            return (a.astype(F32) + b.astype(F32)).astype(BF)

        diag, y_part, x_part = sent
        from_x, from_y = to_x(diag[0]), to_y(diag[1])
        x_top, y_bottom = to_x(x_part[0]), to_y(y_part[1])
        y_top, x_bottom = to_y(added(y_part[0], from_x)), to_x(added(x_part[1], from_y))
        return x_top, y_top, x_bottom, y_bottom

    def scatter_sum(arrived, kept):
        if len(arrived) == 3:
            return kept + sum(t.astype(F32) for t in arrived)
        top = kept[:half_tile] + arrived[0].astype(F32) + arrived[1].astype(F32)
        bottom = kept[half_tile:] + arrived[2].astype(F32) + arrived[3].astype(F32)
        return jnp.concatenate([top, bottom], axis=0)

    def scatter_end(sent, kept):
        return scatter_sum(scatter_move(sent), kept)

    def plane_a2a(t):
        return lax.all_to_all(
            t, both, split_axis=0, concat_axis=0, tiled=True, axis_index_groups=plane
        )

    def column_a2a(t):
        return lax.all_to_all(
            t, "blk", split_axis=0, concat_axis=0, tiled=True, axis_index_groups=column
        )

    def gather_z(t):
        return lax.all_gather(t, "blk", axis=0, tiled=False, axis_index_groups=column)

    def scatter_z(t):
        return lax.psum_scatter(
            t, "blk", scatter_dimension=0, tiled=False, axis_index_groups=column
        )

    me = x_at * nh + head_at
    slots, halo_slots = [], []
    for tile in range(members):
        diff = jnp.bitwise_xor(me, tile)
        slots.append((diff & 1) * 4 + ((diff >> 2) & 1) * 2 + ((diff >> 1) & 1))
    for tile in range(HALO):
        diff = jnp.bitwise_xor(head_at, tile)
        halo_slots.append((diff & 1) * 2 + ((diff >> 1) & 1))
    slots = jnp.stack(slots).astype(jnp.int32)
    halo_slots = jnp.stack(halo_slots).astype(jnp.int32)
    head_ids = (head_at * nx + x_at) * heads + jnp.arange(heads, dtype=jnp.int32)
    slopes = 2.0 ** (-8.0 * (head_ids.astype(F32) + 1.0) / HEADS)
    scalars = (slots, halo_slots, slopes)
    group_tokens = members * TOK_DEV
    local = jnp.arange(group_tokens, dtype=jnp.int32)
    first = z_at * group_tokens

    def document_at(places):
        positions = first + places
        sequence = lax.div(positions, SEQ_LEN)
        within = positions - sequence * SEQ_LEN
        picked = sequence[:, None] == jnp.arange(lengths.shape[0], dtype=jnp.int32)[None, :]
        row_lengths = jnp.sum(jnp.where(picked[:, :, None], lengths[None, :, :], 0), axis=1)
        ends = jnp.cumsum(row_lengths, axis=1)
        past = ends <= within[:, None]
        valid = (jnp.sum(past.astype(jnp.int32), axis=1) < DOCS).astype(F32)
        return valid, sequence * SEQ_LEN + jnp.sum(jnp.where(past, row_lengths, 0), axis=1)

    valid, doc_start = document_at(local)
    slot = jnp.arange(members, dtype=jnp.int32)
    slot_diff = ((slot >> 1) & 1) * 4 + (slot & 1) * 2 + (slot >> 2)
    slot_tile = jnp.bitwise_xor(me, slot_diff)
    slot_places = (slot_tile[:, None] * TILE + jnp.arange(TILE, dtype=jnp.int32)[None]).reshape(-1)
    valid_slot = document_at(slot_places)[0].reshape(group_tokens, 1)
    low = doc_start - first + WINDOW - lax.div(local, TILE) * TILE
    low = low.reshape(members, 1, TILE)
    valid_tiles = valid.reshape(members, 1, TILE)

    def after(t, *others):
        return lax.optimization_barrier((t,) + others)[0]

    def pin(flag, t, *others):
        return after(t, *others) if flag else t

    x_own = layer_input.reshape(TOK_DEV, D)
    cot_own = cotangent.reshape(TOK_DEV, D)

    small = jnp.concatenate(
        [ln1_gain, ln1_bias, bias_query, bias_value, bias_out, ln2_gain, ln2_bias, bias_down, bias_up]
    )
    small = plane_a2a(jnp.broadcast_to(small, (members,) + small.shape))
    small_all = column_a2a(jnp.broadcast_to(small, (nz,) + small.shape))
    bias_u = lax.dynamic_index_in_dim(small_all, me, 1, keepdims=False)[:, 8 * rows :]
    bias_u = bias_u.reshape(ff_own).astype(F32)
    small_all = small_all[:, :, : 8 * rows]
    vectors = (
        small_all.reshape(nz, nx, nh, 8, rows).transpose(3, 2, 0, 1, 4).reshape(8, D).astype(F32)
    )
    gain_one, shift_one, bias_q, bias_v, bias_o, gain_two, shift_two, bias_d = vectors
    own_cols = (head_at * nx + x_at) * width
    bias_qkv = jnp.concatenate(
        [
            lax.dynamic_slice_in_dim(bias_q, own_cols, width),
            jnp.zeros((width,), F32),
            lax.dynamic_slice_in_dim(bias_v, own_cols, width),
        ]
    )

    near = [(x, h) for x in range(nx) for h in range(nh)]
    qkv_moves = [
        (None, p * D + (h * nx + x) * width, at, p * width, width)
        for at, (x, h) in enumerate(near)
        for p in range(3)
    ]
    up_moves = [
        (None, ((h * nz + z) * nx + x) * ff_rows, at, z * ff_rows, ff_rows)
        for at, (x, h) in enumerate(near)
        for z in range(nz)
    ]
    qkv_col = plane_a2a(
        rows_kernel(w_qkv, (members, rows, 3 * width), BF, qkv_moves, "qkv_split")
    )
    up_col = plane_a2a(
        after(rows_kernel(w_up, (members, rows, ff_own), BF, up_moves, "up_split"), qkv_col)
    )
    out_cols = w_out.reshape(rows, members, D // members).transpose(1, 0, 2)
    if F["split"]:
        first_z = gather_z(qkv_col)
        out_z = gather_z(after(w_out, first_z))
        up_after = out_z
    else:
        first_z = gather_z(jnp.concatenate([qkv_col, out_cols], axis=2))
        up_after = first_z
    if not F["uph"]:
        up_z = gather_z(after(up_col, up_after))
        down_w = gather_z(pin(F["agd"], w_down, up_z)).reshape(ff_own, D)

    by_z = (nz, nx, nh, rows)

    order = column_rows(nz, nx, nh, rows)
    half_z = nz // 2
    if F["split"]:
        halves = out_z.reshape(2, half_z, rows, D)
    else:
        halves = first_z[:, :, :, 3 * width :].transpose(0, 2, 1, 3).reshape(2, half_z, rows, D)
    mine = jnp.where(x_at == 0, halves[0], halves[1])
    theirs = to_x(jnp.where(x_at == 0, halves[1], halves[0]))
    low_half = jnp.where(x_at == 0, mine, theirs)
    high_half = jnp.where(x_at == 0, theirs, mine)
    out_w = jnp.stack([low_half, high_half], axis=1).reshape(width, D)

    rows_in = x_own.astype(F32)
    normed_in, inv_in = normalize(rows_in)

    def whole(arrays):
        return [(t, 0) for t in arrays]

    def in_plane(array, weights, body, name, relay):
        def side(at):
            first = at * members // 2
            return token_kernel(
                [((array,), (first + i) * TILE) for i in range(members // 2)],
                [weights],
                [],
                [(D, BF, True)],
                body,
                name=name,
            )

        other = side(1)
        return scatter_start(side(0), other, relay)

    def times(x, at, w, e):
        return (jnp.dot(x, w[0][...], preferred_element_type=F32).astype(BF),)

    def times_t(x, at, w, e):
        return (lax.dot_general(x, w[0][...], COLS, preferred_element_type=F32).astype(BF),)

    def qkv_body(x, at, w, e):
        normed = normalize(x.astype(F32))[0]
        lowered = (normed * e[0][...] + e[1][...]).astype(BF)
        return (jnp.dot(lowered, w[0][...], preferred_element_type=F32) + e[2][...]).astype(BF), lowered

    x_tiles = gather_plane(pin(F['x1'], x_own, small), F['g2x'])
    if F['cot'] == 0:
        cot_tiles = gather_plane(after(cot_own, *x_tiles[:4]), F['g2c'])
    if F['cot'] == 3:
        cot_tiles = gather_plane(cot_own, F['g2c'])
    if F['cotk'] and F['cot'] in (0, 3):
        x_tiles = list(after(tuple(x_tiles), *(cot_tiles if F['cotk'] == 2 else cot_tiles[:4])))
    x_tiles = list(pin(F['upc'], tuple(x_tiles), up_col))
    qkv, ln1 = token_kernel(
        whole(x_tiles),
        [(first_z, order, rows, 3 * width)],
        [
            gain_one.reshape(1, D),
            shift_one.reshape(1, D),
            bias_qkv.reshape(1, -1),
        ],
        [(3 * width, BF, False), (D, BF, False)],
        qkv_body,
        name="qkv_fwd",
    )
    qkv = qkv.reshape(members, TILE, 3 * width)
    kv = qkv[:, :, width:].reshape(2, 2, 2, TILE, 2 * width)
    kv = jnp.where(x_at == 0, kv[:, 1], kv[:, 0]).reshape(HALO, TILE, 2 * width)
    halo = lax.ppermute(kv, "blk", [(b, b + nx) for b in range(nb - nx)])
    if F["cot"] in (1, 2):
        cot_tiles = gather_plane(after(cot_own, qkv if F["cot"] == 1 else halo), F["g2c"])
    halo = pin(F["cotb"], halo, *cot_tiles[:4])
    if F["uph"]:
        up_z = gather_z(after(up_col, up_after, halo))
        down_w = gather_z(pin(F["agd"], w_down, up_z)).reshape(ff_own, D)
    ctx, lse_high = attention_call(
        attn_fwd_kernel, False, scalars, qkv, None, [low, valid_tiles], heads, None
    )
    ctx, lse_low = attention_call(
        attn_fwd_kernel, True, scalars, qkv, halo, [low, valid_tiles], heads, ctx
    )
    ctx = ctx.reshape(group_tokens, width)
    ctx = pin(F['cotctx'], ctx, *cot_tiles[:4])
    half = group_tokens // 2
    attn_sent, attn_kept = in_plane(ctx, (out_w, [(0, 0)], width, D), times, "out_fwd", F["s2a"])

    def collected(tiles):
        kept = token_kernel(whole(tiles), [], [], [], lambda *_: (), keep=True, name="collect")
        return kept[0]

    if F["gdp"]:
        cot = collected(pin(F["colp"], tuple(cot_tiles), *attn_sent))
    attn_sum = scatter_end(attn_sent, attn_kept)
    if F["gdp"] and F["colp"]:
        attn_sum = after(attn_sum, cot)
    middle = rows_in + (attn_sum + bias_o)
    normed_mid, inv_mid = normalize(middle)
    ln2_own = (normed_mid * gain_two + shift_two).astype(BF)

    def up_body(x, at, w, e):
        v = jnp.dot(x, w[0][...], preferred_element_type=F32) + e[0][...]
        squared = v * v
        t = jnp.tanh(v * (0.7978845608028654 + 0.7978845608028654 * 0.044715 * squared))
        half_up = 0.5 + 0.5 * t
        slope = half_up + (0.5 * v) * (1.0 - t * t) * (
            0.7978845608028654 + 3.0 * 0.7978845608028654 * 0.044715 * squared
        )
        return (v * half_up).astype(BF), slope.astype(BF)

    active, up_slope, ln2 = token_kernel(
        whole(gather_plane(ln2_own, F['g2l'])),
        [(up_z, order, rows, ff_own)],
        [bias_u.reshape(1, ff_own)],
        [(ff_own, BF, False), (ff_own, BF, False)],
        up_body,
        keep=True,
        name="up_fwd",
    )

    cot_full = cot_own.astype(F32)
    def down_body(x, at, w, e):
        d_act = lax.dot_general(x, w[0][...], COLS, preferred_element_type=F32)
        d_pre = (d_act * w[2][at, :].astype(F32)).astype(BF)
        part = lax.dot_general(d_pre, w[1][...], COLS, preferred_element_type=F32)
        return d_pre, part.astype(BF)

    def down_back(side):
        return token_kernel(
            whole(cot_tiles[side * members // 2 : (side + 1) * members // 2]),
            [
                (down_w, [(0, 0)], ff_own, D),
                (up_z, order, rows, ff_own),
                (up_slope, [(side * half, 0)], half, ff_own),
            ],
            [],
            [(ff_own, BF, False), (D, BF, True)],
            down_body,
            name="down_back",
        )

    if F["gdp"]:
        g_down = tokens_product(active, cot, "down_grad")
        up_slope = after(up_slope, g_down)
    d_up_other, *ln2_other = down_back(1)
    d_up_mine, *ln2_mine = down_back(0)
    ln2_sent, ln2_kept = scatter_start(ln2_mine, ln2_other, F['s2l'])
    d_ln2 = scatter_end(ln2_sent, ln2_kept)
    if not F["gdp"]:
        cot = collected(pin(F["gd_lo"], tuple(cot_tiles), *ln2_sent))
        g_down = tokens_product(active, cot, "down_grad")
    grad_w_down = scatter_z(g_down.reshape(nz, ff_rows, D)).astype(F32)
    d_up = jnp.concatenate([d_up_mine, d_up_other], axis=0)
    if F["gu_lo"] != 2:
        d_up = pin(F["gu_lo"] == 3, pin(F["gu_lo"] == 1, d_up, g_down), *ln2_sent)
        g_up = tokens_product(ln2, d_up, "up_grad", by_z)
        d_ln2 = pin(F["gu_hi"] == 1, d_ln2, g_up)
    d_ln2 = pin(F["gd_hi"] == 1, d_ln2, g_down)
    d_middle = cot_full + norm_back(d_ln2 * gain_two, normed_mid, inv_mid)
    d_attn_own = d_middle.astype(BF)
    if F["gu_lo"] == 2:
        g_up = tokens_product(ln2, after(d_up, d_attn_own), "up_grad", by_z)
    up_part = g_up
    up_sum = scatter_z(g_up.reshape(nz, members, rows, ff_own))
    g_up = plane_a2a(up_sum)
    grad_w_up = rows_kernel(
        g_up, (rows, FF), F32, [(m[2], m[3], m[0], m[1], m[4]) for m in up_moves], "up_join"
    )
    grad_b_up = jnp.sum(d_up.astype(F32), axis=0)
    down_sent, down_kept = in_plane(
        pin(F['df_lo'] == 1, pin(F['df_lo'] == 2, active, *ln2_sent), d_attn_own), (down_w, [(0, 0)], ff_own, D), times, "down_fwd", F["s2o"]
    )

    d_attn_tiles = gather_plane(d_attn_own, F['g2a'])
    d_attn_tiles = list(pin(F['df_hi'] == 1, pin(F['rsd'] == 1, pin(F['gd_hi'] == 2, pin(F['gu_hi'] == 2, tuple(d_attn_tiles), up_part), g_down), grad_w_down), *down_sent))

    def ctx_body(x, at, w, e):
        found = lax.dot_general(x, w[0][...], COLS, preferred_element_type=F32)
        return ((found * e[0][at, :]).astype(BF),)

    d_ctx, d_attn = token_kernel(
        whole(d_attn_tiles),
        [(out_w, [(0, 0)], width, D)],
        [valid_slot],
        [(width, BF, False)],
        ctx_body,
        keep=True,
        name="ctx_back",
    )
    down_sent = pin(F['lo_lo'], down_sent, *d_attn_tiles)
    down_moved = scatter_move(down_sent)
    down_sum = scatter_sum(down_moved, down_kept)
    output = (middle + (down_sum + bias_d)).astype(BF)
    d_ctx = d_ctx.reshape(members, TILE, width)
    d_q, d_hk, d_hv, d_k, d_v = attention_call(
        attn_bwd_kernel, True, scalars, qkv, halo, [low, d_ctx, lse_low], heads, None
    )
    def step_back(t):
        return lax.ppermute(t, "blk", [(b + nx, b) for b in range(nb - nx)])

    back = step_back(jnp.concatenate([d_hk, d_hv], axis=-1))
    g_out = tokens_product(ctx, pin(F['go_lo'], d_attn, d_hk), "out_grad")
    g_out_part = g_out
    g_out = pin(F["lo_hi"] == 4, g_out, output)
    g_out = g_out.reshape(half_z, nx, rows, D)
    g_mine = jnp.where(x_at == 0, g_out[:, 0], g_out[:, 1])
    g_theirs = to_x(jnp.where(x_at == 0, g_out[:, 1], g_out[:, 0]))
    g_out = jnp.concatenate(
        [jnp.where(x_at == 0, g_mine, g_theirs), jnp.where(x_at == 0, g_theirs, g_mine)], axis=0
    )
    grad_w_out = scatter_z(pin(F['outh'], g_out, back)).astype(F32)
    d_q = pin(F["go_hi"], d_q, g_out_part)
    d_q = pin(F["lo_hi"] == 1, d_q, output)
    d_q = pin(F["df_hi"] == 2, d_q, *down_sent)
    d_q = pin(F["rsd"] == 2, d_q, grad_w_down)
    d_q = pin(F["rsu"] == 2, d_q, up_sum)
    d_q, d_k, d_v = attention_call(
        attn_bwd_kernel, False, scalars, qkv, None, [low, d_ctx, lse_high, d_k, d_v], heads, d_q
    )
    d_k = pin(F["gkv"], d_k, g_out)
    d_k = pin(F["lo_hi"] == 2, d_k, output)
    x_row = x_at.reshape(1).astype(jnp.int32)
    d_proj = join_grads(x_row, d_q, d_k, d_v, back).reshape(group_tokens, 3 * width)
    d_proj = pin(F["rso"] == 2, d_proj, grad_w_out)
    d_full = pin(F["rso"] == 3, d_proj, grad_w_out)
    d_full = pin(F["rsd"] == 3, pin(F["rsu"] == 3, d_full, up_sum), grad_w_down)
    d_back = pin(F["lo_hi"] == 3, d_proj, *(down_moved if F["arr"] else (output,)))
    d_back = pin(F["rsd"] == 4, d_back, grad_w_down)
    d_back = pin(F["rsu"] == 4, d_back, up_sum)
    d_back = pin(F["rso"] == 4, d_back, grad_w_out)
    d_back = pin(F["upj"], d_back, grad_w_up)
    qkv_weight = (first_z, order, rows, 3 * width)
    if F["gqr"]:
        ln1_sent, ln1_kept = in_plane(d_back, qkv_weight, times_t, "qkv_back", F["s2i"])
        d_full = after(d_full, *ln1_sent)
    g_qkv_part = tokens_product(ln1, d_full, "qkv_grad", by_z)
    if not F["gqr"]:
        d_back = pin(F["gq"], d_back, g_qkv_part)
        ln1_sent, ln1_kept = in_plane(d_back, qkv_weight, times_t, "qkv_back", F["s2i"])
    g_qkv = plane_a2a(scatter_z(g_qkv_part.reshape(nz, members, rows, 3 * width)))
    grad_w_qkv = rows_kernel(
        g_qkv, (rows, 3 * D), F32, [(m[2], m[3], m[0], m[1], m[4]) for m in qkv_moves], "qkv_join"
    )
    d_ln1 = scatter_end(ln1_sent, ln1_kept)
    grad_input = d_middle + norm_back(d_ln1 * gain_one, normed_in, inv_in)

    def placed(t):
        return lax.dynamic_update_slice_in_dim(jnp.zeros((D,), F32), t, own_cols, 0)

    sums = jnp.stack(
        [
            jnp.sum(d_ln1 * normed_in, axis=0),
            jnp.sum(d_ln1, axis=0),
            placed(jnp.sum(d_proj[:, :width].astype(F32), axis=0)),
            placed(jnp.sum(d_proj[:, 2 * width :].astype(F32), axis=0)),
            jnp.sum(d_attn_own.astype(F32), axis=0),
            jnp.sum(d_ln2 * normed_mid, axis=0),
            jnp.sum(d_ln2, axis=0),
            jnp.sum(cot_full, axis=0),
        ]
    )
    sums = sums.reshape(8, nh, nz, nx, rows).transpose(3, 1, 2, 0, 4)
    sums = pin(F["suml"] == 1, sums, g_qkv)
    sums = jnp.sum(plane_a2a(sums.reshape(members, nz, 8 * rows)), axis=0)
    sums = jnp.concatenate([sums, grad_b_up.reshape(nz, ff_rows)], axis=1)
    sums = jnp.sum(
        column_a2a(pin(F["suml"] == 2, sums, grad_w_qkv)),
        axis=0,
    )
    vec = sums[: 8 * rows].reshape(8, rows)
    return (
        output.reshape(1, TOK_DEV, D),
        grad_input.reshape(1, TOK_DEV, D),
        vec[0],
        vec[1],
        grad_w_qkv,
        vec[2],
        vec[3],
        grad_w_out,
        vec[4],
        vec[5],
        vec[6],
        grad_w_up,
        sums[8 * rows :],
        grad_w_down,
        vec[7],
    )


def solution(mesh):
    split = P(("head", "blk"))
    wide = P(("head", "blk"), None)
    tokens = P("blk", "head", None)
    return jax.shard_map(
        shards,
        mesh=mesh,
        in_specs=(
            tokens, P(), split, split, wide, split, split, wide, split, split, split, wide, split, wide, split, tokens,
        ),
        out_specs=(
            tokens, tokens, split, split, wide, split, split, wide, split, split, split, wide, split, wide, split,
        ),
        check_vma=False,
    )
```

```python
import functools

import jax
import jax.numpy as jnp
from jax import lax
from jax.experimental import pallas as pl
from jax.experimental.pallas import tpu as pltpu
from jax.sharding import PartitionSpec as P

D = 2048
HEADS = 16
HEAD_DIM = 128
FF = 8192
TOK_DEV = 256
WINDOW = 1024
SEQ_LEN = 8192
DOCS = 4

EPS = 1e-05
NEG = -1e30
BF = jnp.bfloat16
F32 = jnp.float32
ROWS = (((0,), (0,)), ((), ()))
COLS = (((1,), (1,)), ((), ()))

TILE = 256
HALO = WINDOW // TILE
SPAN = WINDOW + TILE
VMEM = 48 * 1024 * 1024
F = dict(x1=0, cot=1, cotk=1, cotctx=1, cotb=0, gd_lo=1, gd_hi=2, gu_lo=1, gu_hi=0, rsd=1, rsu=4, rso=0, df_lo=0, df_hi=2, lo_lo=1, lo_hi=3, go_lo=1, go_hi=0, gkv=1, hsplit=1, gq=0, agd=1, upc=1, g2x=0, g2c=1, g2l=1, g2a=0, s2a=1, s2l=0, s2o=0, s2i=1, suml=2, split=0, gqr=0, upj=1, gdp=1, colp=0, uph=0, outh=0, arr=0)
COST = dict(qkv_fwd=20, out_fwd=3, up_fwd=0, down_back=0, collect=20, down_grad=20, up_grad=1, down_fwd=0, ctx_back=20, out_grad=0, qkv_grad=8, qkv_back=20, attn_fwd_low=1, attn_fwd_high=20, attn_bwd_low=20, attn_bwd_high=8, qkv_split=8, up_split=3, up_join=3, qkv_join=0, join_grads=0)


def cost_of(name):
    flops = int(COST[name] * 1e9)
    return pl.CostEstimate(flops=flops, bytes_accessed=4096, transcendentals=0)


def normalize(values):
    center = values - jnp.mean(values, axis=-1, keepdims=True)
    inv_scale = lax.rsqrt(jnp.mean(center * center, axis=-1, keepdims=True) + EPS)
    return (center * inv_scale, inv_scale)


def norm_back(d_hat, normed, inv_scale):
    return inv_scale * (
        d_hat
        - jnp.mean(d_hat, axis=-1, keepdims=True)
        - normed * jnp.mean(d_hat * normed, axis=-1, keepdims=True)
    )


def gelu_tanh(values):
    return (
        0.5
        * values
        * (1.0 + jnp.tanh(0.7978845608028654 * (values + 0.044715 * values * values * values)))
    )


def fill_tiles(buffer, halo_ref, own_ref, halo_slots, slots):
    if halo_ref is None:
        sources = [(own_ref, slots, tile) for tile in range(own_ref.shape[0])]
    else:
        sources = [(halo_ref, halo_slots, tile) for tile in range(HALO)]
        sources += [(own_ref, slots, tile) for tile in range(own_ref.shape[0] - HALO)]
    for at, (ref, order, tile) in enumerate(sources):
        buffer[at * TILE : (at + 1) * TILE, :] = ref[order[tile]]


def fill_bias(bias, slope):
    key = lax.broadcasted_iota(jnp.int32, (SPAN, TILE), 0)
    query = lax.broadcasted_iota(jnp.int32, (SPAN, TILE), 1)
    rel = key - WINDOW - query
    bias[...] = jnp.where((rel <= 0) & (rel > -WINDOW), slope * rel.astype(F32), NEG)


def masked_scores(q, keys, bias, low_row):
    scores = lax.dot_general(keys, q, COLS, preferred_element_type=F32)
    scores = scores * HEAD_DIM ** (-0.5) + bias
    key = lax.broadcasted_iota(jnp.int32, (SPAN, TILE), 0)
    return jnp.where(key >= low_row, scores, NEG)


def attn_fwd_kernel(first, slots, halo_slots, slopes, q_ref, k_ref, v_ref, *refs):
    hk_ref, hv_ref, refs = (refs[0], refs[1], refs[3:]) if first else (None, None, refs)
    low_ref, valid_ref, ctx_ref, lse_ref, kbuf, vbuf, bias = refs
    head = pl.program_id(0)
    tile = pl.program_id(1)

    @pl.when(tile == 0)
    def _():
        fill_tiles(kbuf, hk_ref, k_ref, halo_slots, slots)
        fill_tiles(vbuf, hv_ref, v_ref, halo_slots, slots)
        fill_bias(bias, slopes[head])

    start = pl.multiple_of(tile * TILE, TILE)
    scores = masked_scores(q_ref[0], kbuf[pl.ds(start, SPAN), :], bias[...], low_ref[0])
    highest = jnp.max(scores, axis=0, keepdims=True)
    expo = jnp.exp(scores - highest)
    summed = jnp.sum(expo, axis=0, keepdims=True)
    lse_ref[0, 0] = highest + jnp.log(summed)
    context = lax.dot_general(
        vbuf[pl.ds(start, SPAN), :], expo.astype(BF), ROWS, preferred_element_type=F32
    )
    context = context * (valid_ref[0] / summed)
    ctx_ref[0] = context.T.astype(BF)


def attn_bwd_kernel(first, slots, halo_slots, slopes, q_ref, k_ref, v_ref, *refs):
    hk_ref, hv_ref, refs = (refs[0], refs[1], refs[2:]) if first else (None, None, refs)
    low_ref, dctx_ref, lse_ref = refs[:3]
    if first:
        dq_ref, dhk_ref, dhv_ref, dk_ref, dv_ref = refs[3:8]
    else:
        dk_in, dv_in, _, dq_ref, dk_ref, dv_ref = refs[3:9]
    kbuf, vbuf, bias, dkbuf, dvbuf = refs[-5:]
    head = pl.program_id(0)
    tile = pl.program_id(1)
    tiles = k_ref.shape[0]
    own = tiles - HALO
    kept = own * TILE

    @pl.when(tile == 0)
    def _():
        fill_tiles(kbuf, hk_ref, k_ref, halo_slots, slots)
        fill_tiles(vbuf, hv_ref, v_ref, halo_slots, slots)
        fill_bias(bias, slopes[head])
        if first:
            dkbuf[...] = jnp.zeros_like(dkbuf)
            dvbuf[...] = jnp.zeros_like(dvbuf)
        else:
            for buffer, start in ((dkbuf, dk_in), (dvbuf, dv_in)):
                buffer[:kept, :] = start[0]
                buffer[kept:, :] = jnp.zeros((buffer.shape[0] - kept, HEAD_DIM), F32)

    start = pl.multiple_of(tile * TILE, TILE)
    rows = pl.ds(start, SPAN)
    q = q_ref[0]
    d_ctx = dctx_ref[0]
    keys = kbuf[rows, :]
    scores = masked_scores(q, keys, bias[...], low_ref[0])
    probs = jnp.exp(scores - lse_ref[0, 0])
    d_probs = lax.dot_general(vbuf[rows, :], d_ctx, COLS, preferred_element_type=F32)
    delta = jnp.sum(probs * d_probs, axis=0, keepdims=True)
    d_scores = (probs * (d_probs - delta)).astype(BF)
    scale = HEAD_DIM ** (-0.5)
    d_query = lax.dot_general(d_scores, keys, ROWS, preferred_element_type=F32)
    dq_ref[0] = (d_query * scale).astype(BF)
    dkbuf[rows, :] += jnp.dot(d_scores, q, preferred_element_type=F32)
    dvbuf[rows, :] += jnp.dot(probs.astype(BF), d_ctx, preferred_element_type=F32)

    @pl.when(tile == pl.num_programs(1) - 1)
    def _():
        if first:
            for at in range(HALO):
                piece = slice(at * TILE, (at + 1) * TILE)
                dhk_ref[halo_slots[at]] = (dkbuf[piece, :] * scale).astype(BF)
                dhv_ref[halo_slots[at]] = dvbuf[piece, :].astype(BF)
            dk_ref[0] = dkbuf[HALO * TILE :, :]
            dv_ref[0] = dvbuf[HALO * TILE :, :]
        else:
            for at in range(tiles):
                piece = slice(at * TILE, (at + 1) * TILE)
                dk_ref[slots[at]] = dkbuf[piece, :] * scale
                dv_ref[slots[at]] = dvbuf[piece, :]


def attention_call(kernel, first, scalars, qkv, halo, rows, heads, grads):
    tiles = qkv.shape[0]
    queries = HALO if first else tiles - HALO
    base = 0 if first else HALO
    width = heads * HEAD_DIM
    block = (1, TILE, HEAD_DIM)
    whole = (tiles, TILE, HEAD_DIM)
    edge = (HALO, TILE, HEAD_DIM)
    q_s = pl.BlockSpec(block, lambda h, t, s, hs, sl: (s[t + base], 0, h))
    own_s = pl.BlockSpec(whole, lambda h, t, s, hs, sl: (0, 0, h))
    k_s = pl.BlockSpec(whole, lambda h, t, s, hs, sl: (0, 0, heads + h))
    v_s = pl.BlockSpec(whole, lambda h, t, s, hs, sl: (0, 0, 2 * heads + h))
    hk_s = pl.BlockSpec(edge, lambda h, t, s, hs, sl: (0, 0, h))
    hv_s = pl.BlockSpec(edge, lambda h, t, s, hs, sl: (0, 0, heads + h))
    row_s = pl.BlockSpec((1, 1, TILE), lambda h, t, s, hs, sl: (t + base, 0, 0))
    lse_s = pl.BlockSpec((1, 1, 1, TILE), lambda h, t, s, hs, sl: (h, t, 0, 0))
    part_s = pl.BlockSpec(
        (1, (tiles - HALO) * TILE, HEAD_DIM), lambda h, t, s, hs, sl: (h, 0, 0)
    )
    any_s = pl.BlockSpec(memory_space=pl.ANY)
    out = jax.ShapeDtypeStruct
    in_specs, args = [q_s, k_s, v_s], [qkv, qkv, qkv]
    if first:
        in_specs += [hk_s, hv_s]
        args += [halo, halo]
    forward = kernel is attn_fwd_kernel
    aliases = {}
    length = tiles * TILE
    scratch = [
        pltpu.VMEM((length, HEAD_DIM), BF),
        pltpu.VMEM((length, HEAD_DIM), BF),
        pltpu.VMEM((SPAN, TILE), F32),
    ]
    part = (heads, (tiles - HALO) * TILE, HEAD_DIM)
    if forward:
        if first:
            aliases = {3 + len(args): 0}
            in_specs += [any_s]
            args += [grads]
        in_specs += [row_s, row_s]
        out_specs = [q_s, lse_s]
        shapes = [out((tiles, TILE, width), BF), out((heads, queries, 1, TILE), F32)]
    else:
        in_specs += [row_s, q_s, lse_s]
        scratch += [pltpu.VMEM((length, HEAD_DIM), F32), pltpu.VMEM((length, HEAD_DIM), F32)]
        if first:
            out_specs = [q_s, hk_s, hk_s, part_s, part_s]
            shapes = [out((tiles, TILE, width), BF)] + [out((HALO, TILE, width), BF)] * 2
            shapes += [out(part, F32)] * 2
        else:
            in_specs += [part_s, part_s, any_s]
            aliases = {3 + len(args) + len(rows): 0}
            out_specs = [q_s, own_s, own_s]
            shapes = [out((tiles, TILE, width), BF)] + [out((tiles, TILE, width), F32)] * 2
            rows = list(rows) + [grads]
    return pl.pallas_call(
        functools.partial(kernel, first),
        grid_spec=pltpu.PrefetchScalarGridSpec(
            num_scalar_prefetch=3,
            grid=(heads, queries),
            in_specs=in_specs,
            out_specs=out_specs,
            scratch_shapes=scratch,
        ),
        out_shape=shapes,
        input_output_aliases=aliases,
        compiler_params=pltpu.CompilerParams(vmem_limit_bytes=VMEM),
        cost_estimate=cost_of(("attn_fwd" if forward else "attn_bwd") + ("_low" if first else "_high")),
        name=("attn_fwd" if forward else "attn_bwd") + ("_low" if first else "_high"),
    )(*scalars, *args, *rows)


def column_rows(z_count, x_count, h_count, rows):
    return [
        ((z, x * h_count + h), ((h * z_count + z) * x_count + x) * rows)
        for z in range(z_count)
        for x in range(x_count)
        for h in range(h_count)
    ]


def token_kernel(pieces, weights, extras, outs, body, keep=False, name=None):
    count = len(pieces)
    wide, kind = pieces[0][0][0].shape[1], pieces[0][0][0].dtype
    parts = [
        (at * TILE + i * (TILE // len(arrays)), TILE // len(arrays), row, at)
        for at, (arrays, row) in enumerate(pieces)
        for i in range(len(arrays))
    ]
    n_t = len(parts)
    n_w, n_e, n_o = len(weights), len(extras), len(outs)
    places = []
    out_shapes = []
    for cols, dtype, apart in list(outs) + ([(wide, kind, False)] if keep else []):
        places.append(len(out_shapes))
        shape = jax.ShapeDtypeStruct((TILE if apart else count * TILE, cols), dtype)
        out_shapes += [shape] * (count if apart else 1)
    n_out = len(out_shapes)

    def kernel(*refs):
        tile_refs = refs[:n_t]
        w_refs = refs[n_t : n_t + n_w]
        e_refs = refs[n_t + n_w : n_t + n_w + n_e]
        refs = refs[n_t + n_w + n_e :]
        o_refs = refs[:n_out]
        refs = refs[n_out:]
        x_buf, w_bufs, o_bufs = refs[0], refs[1 : 1 + n_w], refs[1 + n_w : 1 + n_w + n_o]
        x_sem, w_sem, o_sem = refs[1 + n_w + n_o :]
        for at in range(n_w):
            _, moves, rows, cols = weights[at]
            for lead, row in moves:
                if isinstance(lead, int):
                    source = w_refs[at].at[lead : lead + rows]
                else:
                    source = w_refs[at].at[lead + (slice(None), slice(0, cols))]
                pltpu.make_async_copy(
                    source,
                    w_bufs[at].at[row : row + rows],
                    w_sem.at[at],
                ).start()
        for i, (place, size, row, at) in enumerate(parts):
            pltpu.make_async_copy(
                tile_refs[i].at[row : row + size], x_buf.at[place : place + size], x_sem.at[at]
            ).start()
        for at in range(n_w):
            pltpu.make_async_copy(w_bufs[at], w_bufs[at], w_sem.at[at]).wait()

        def rows_of(at):
            return pl.ds(pl.multiple_of(at * TILE, TILE), TILE)

        bufs = list(o_bufs) + ([x_buf] if keep else [])

        def step(at, carry):
            rows = rows_of(at)
            pltpu.make_async_copy(x_buf.at[rows], x_buf.at[rows], x_sem.at[at]).wait()
            found = body(x_buf[rows, :], rows, w_bufs, e_refs)
            for i in range(n_o):
                o_bufs[i][rows, :] = found[i]
            for i in range(len(bufs)):
                if i < n_o and outs[i][2]:
                    for own in range(count):

                        @pl.when(at == own)
                        def _():
                            pltpu.make_async_copy(
                                bufs[i].at[rows], o_refs[places[i] + own], o_sem.at[i, at]
                            ).start()

                else:
                    pltpu.make_async_copy(
                        bufs[i].at[rows], o_refs[places[i]].at[rows], o_sem.at[i, at]
                    ).start()
            return carry

        lax.fori_loop(0, count, step, 0)

        def finish(at, carry):
            rows = rows_of(at)
            for i in range(len(bufs)):
                pltpu.make_async_copy(bufs[i].at[rows], bufs[i].at[rows], o_sem.at[i, at]).wait()
            return carry

        lax.fori_loop(0, count, finish, 0)

    any_spec = pl.BlockSpec(memory_space=pltpu.HBM)
    w_shapes = [(len(moves) * rows, cols) for _, moves, rows, cols in weights]
    return pl.pallas_call(
        kernel,
        in_specs=[any_spec] * (n_t + n_w) + [pl.BlockSpec(memory_space=pltpu.VMEM)] * n_e,
        out_specs=[any_spec] * n_out,
        out_shape=out_shapes,
        scratch_shapes=[
            pltpu.VMEM((count * TILE, wide), kind),
            *[pltpu.VMEM(shape, BF) for shape in w_shapes],
            *[pltpu.VMEM((count * TILE, c), t) for c, t, _ in outs],
            pltpu.SemaphoreType.DMA((count,)),
            pltpu.SemaphoreType.DMA((max(n_w, 1),)),
            pltpu.SemaphoreType.DMA((n_o + 1, count)),
        ],
        compiler_params=pltpu.CompilerParams(vmem_limit_bytes=VMEM),
        cost_estimate=cost_of(name),
        name=name,
    )(*[t for p in pieces for t in p[0]], *[w[0] for w in weights], *extras)


def tokens_product(left, right, name, order=None):
    tokens, cols = left.shape
    wide = right.shape[1]
    if order is None:
        block = min(256, cols)
        shape, out_block, place = (cols, wide), (block, wide), lambda i: (i, 0)
    else:
        z_count, x_count, h_count, rows = order
        block = cols // h_count
        shape = (z_count, x_count, h_count, rows, wide)
        out_block, place = (z_count, x_count, 1, rows, wide), lambda i: (0, 0, i, 0, 0)

    def kernel(a_ref, b_ref, o_ref):
        found = lax.dot_general(a_ref[...], b_ref[...], ROWS, preferred_element_type=F32)
        if order is None:
            o_ref[...] = found.astype(BF)
        else:
            for z in range(z_count):
                for x in range(x_count):
                    start = (z * x_count + x) * rows
                    o_ref[z, x, 0] = found[start : start + rows].astype(BF)

    return pl.pallas_call(
        kernel,
        grid=(cols // block,),
        in_specs=[
            pl.BlockSpec((tokens, block), lambda i: (0, i)),
            pl.BlockSpec((tokens, wide), lambda i: (0, 0)),
        ],
        out_specs=pl.BlockSpec(out_block, place),
        out_shape=jax.ShapeDtypeStruct(shape, BF),
        compiler_params=pltpu.CompilerParams(vmem_limit_bytes=VMEM),
        cost_estimate=cost_of(name),
        name=name,
    )(left, right)


def join_grads(x_row, d_q, d_k, d_v, back):
    tiles, _, width = d_q.shape

    def kernel(x_ref, q_ref, k_ref, v_ref, bk_ref, bv_ref, o_ref):
        second = ((pl.program_id(0) >> 1) & 1) != x_ref[0]
        o_ref[0, :, :width] = q_ref[0]
        for at, (own, back) in enumerate(((k_ref, bk_ref), (v_ref, bv_ref))):
            added = own[0] + jnp.where(second, back[0].astype(F32), 0.0)
            o_ref[0, :, (1 + at) * width : (2 + at) * width] = added.astype(BF)

    tile = pl.BlockSpec((1, TILE, width), lambda i, x: (i, 0, 0))
    edge_k = pl.BlockSpec((1, TILE, width), lambda i, x: ((i >> 2) * 2 + (i & 1), 0, 0))
    edge_v = pl.BlockSpec((1, TILE, width), lambda i, x: ((i >> 2) * 2 + (i & 1), 0, 1))
    return pl.pallas_call(
        kernel,
        grid_spec=pltpu.PrefetchScalarGridSpec(
            num_scalar_prefetch=1,
            grid=(tiles,),
            in_specs=[tile, tile, tile, edge_k, edge_v],
            out_specs=pl.BlockSpec((1, TILE, 3 * width), lambda i, x: (i, 0, 0)),
        ),
        out_shape=jax.ShapeDtypeStruct((tiles, TILE, 3 * width), BF),
        compiler_params=pltpu.CompilerParams(vmem_limit_bytes=VMEM),
        cost_estimate=cost_of("join_grads"),
        name="join_grads",
    )(x_row, d_q, d_k, d_v, back, back)


def rows_kernel(array, shape, dtype, moves, name):
    def kernel(a_ref, o_ref):
        for a_lead, a_col, o_lead, o_col, cols in moves:
            source, target = slice(a_col, a_col + cols), slice(o_col, o_col + cols)
            found = a_ref[:, source] if a_lead is None else a_ref[a_lead, :, source]
            if o_lead is None:
                o_ref[:, target] = found.astype(dtype)
            else:
                o_ref[o_lead, :, target] = found.astype(dtype)

    return pl.pallas_call(
        kernel,
        in_specs=[pl.BlockSpec(memory_space=pltpu.VMEM)],
        out_specs=pl.BlockSpec(memory_space=pltpu.VMEM),
        out_shape=jax.ShapeDtypeStruct(shape, dtype),
        compiler_params=pltpu.CompilerParams(vmem_limit_bytes=VMEM),
        cost_estimate=cost_of(name),
        name=name,
    )(array)


def shards(
    layer_input,
    lengths,
    ln1_gain,
    ln1_bias,
    w_qkv,
    bias_query,
    bias_value,
    w_out,
    bias_out,
    ln2_gain,
    ln2_bias,
    w_up,
    bias_up,
    w_down,
    bias_down,
    cotangent,
):
    nh = lax.axis_size("head")
    nb = lax.axis_size("blk")
    nx = 2
    nz = nb // nx
    members = nx * nh
    rows = D // (nh * nb)
    ff_rows = FF // (nh * nb)
    ff_own = nz * ff_rows
    heads = HEADS // members
    width = heads * HEAD_DIM
    head_at = lax.axis_index("head")
    blk_at = lax.axis_index("blk")
    x_at = lax.rem(blk_at, nx)
    z_at = lax.div(blk_at, nx)
    both = ("head", "blk")
    plane = [[h * nb + z * nx + x for x in range(nx) for h in range(nh)] for z in range(nz)]
    column = [[z * nx + x for z in range(nz)] for x in range(nx)]

    def to_core(t):
        return lax.ppermute(t, "head", [(h, h ^ 1) for h in range(nh)])

    def to_y(t):
        return lax.ppermute(t, "head", [(h, h ^ 2) for h in range(nh)])

    def to_x(t):
        return lax.ppermute(t, "blk", [(b, b ^ 1) for b in range(nb)])

    def up_z(t, sources):
        pairs = [(z * nx + x, (z + 1) * nx + x) for z in sources for x in range(nx)]
        return lax.ppermute(t, "blk", pairs)

    def down_z(t, sources):
        pairs = [(z * nx + x, (z - 1) * nx + x) for z in sources for x in range(nx)]
        return lax.ppermute(t, "blk", pairs)

    def to_diag(t):
        return lax.ppermute(
            t, both, [(h * nb + b, (h ^ 2) * nb + (b ^ 1)) for h in range(nh) for b in range(nb)]
        )

    half_tile = TOK_DEV // 2

    def gather_plane(own, relay):
        if relay:
            top, bottom = own[:half_tile], own[half_tile:]
            x_top, y_bottom = to_x(top), to_y(bottom)
            x_bottom, y_top = to_x(bottom), to_y(top)
            diag = (to_y(x_top), to_x(y_bottom))
            same = [(own,), (y_top, y_bottom), (x_top, x_bottom), diag]
        else:
            same = [(own,), (to_y(own),), (to_x(own),), (to_diag(own),)]
        return same + [tuple(to_core(t) for t in arrays) for arrays in same]

    def scatter_start(mine, other, relay):
        swapped = [to_core(other[at]) for at in (3, 1, 2, 0)]
        halves = (slice(0, half_tile), slice(half_tile, TOK_DEV)) if relay else (slice(None),)
        sent = tuple(
            tuple((mine[at][h].astype(F32) + t[h].astype(F32)).astype(BF) for h in halves)
            for at, t in zip((3, 1, 2), swapped)
        )
        return lax.optimization_barrier(sent), mine[0].astype(F32) + swapped[3].astype(F32)

    def scatter_move(sent):
        if len(sent[0]) == 1:
            return to_diag(sent[0][0]), to_y(sent[1][0]), to_x(sent[2][0])

        def added(a, b):
            return (a.astype(F32) + b.astype(F32)).astype(BF)

        diag, y_part, x_part = sent
        from_x, from_y = to_x(diag[0]), to_y(diag[1])
        x_top, y_bottom = to_x(x_part[0]), to_y(y_part[1])
        y_top, x_bottom = to_y(added(y_part[0], from_x)), to_x(added(x_part[1], from_y))
        return x_top, y_top, x_bottom, y_bottom

    def scatter_sum(arrived, kept):
        if len(arrived) == 3:
            return kept + sum(t.astype(F32) for t in arrived)
        top = kept[:half_tile] + arrived[0].astype(F32) + arrived[1].astype(F32)
        bottom = kept[half_tile:] + arrived[2].astype(F32) + arrived[3].astype(F32)
        return jnp.concatenate([top, bottom], axis=0)

    def scatter_end(sent, kept):
        return scatter_sum(scatter_move(sent), kept)

    def plane_a2a(t):
        return lax.all_to_all(
            t, both, split_axis=0, concat_axis=0, tiled=True, axis_index_groups=plane
        )

    def column_a2a(t):
        return lax.all_to_all(
            t, "blk", split_axis=0, concat_axis=0, tiled=True, axis_index_groups=column
        )

    def gather_z(t):
        return lax.all_gather(t, "blk", axis=0, tiled=False, axis_index_groups=column)

    def scatter_z(t):
        return lax.psum_scatter(
            t, "blk", scatter_dimension=0, tiled=False, axis_index_groups=column
        )

    me = x_at * nh + head_at
    slots, halo_slots = [], []
    for tile in range(members):
        diff = jnp.bitwise_xor(me, tile)
        slots.append((diff & 1) * 4 + ((diff >> 2) & 1) * 2 + ((diff >> 1) & 1))
    for tile in range(HALO):
        diff = jnp.bitwise_xor(head_at, tile)
        halo_slots.append((diff & 1) * 2 + ((diff >> 1) & 1))
    slots = jnp.stack(slots).astype(jnp.int32)
    halo_slots = jnp.stack(halo_slots).astype(jnp.int32)
    head_ids = (head_at * nx + x_at) * heads + jnp.arange(heads, dtype=jnp.int32)
    slopes = 2.0 ** (-8.0 * (head_ids.astype(F32) + 1.0) / HEADS)
    scalars = (slots, halo_slots, slopes)
    group_tokens = members * TOK_DEV
    local = jnp.arange(group_tokens, dtype=jnp.int32)
    first = z_at * group_tokens

    def document_at(places):
        positions = first + places
        sequence = lax.div(positions, SEQ_LEN)
        within = positions - sequence * SEQ_LEN
        picked = sequence[:, None] == jnp.arange(lengths.shape[0], dtype=jnp.int32)[None, :]
        row_lengths = jnp.sum(jnp.where(picked[:, :, None], lengths[None, :, :], 0), axis=1)
        ends = jnp.cumsum(row_lengths, axis=1)
        past = ends <= within[:, None]
        valid = (jnp.sum(past.astype(jnp.int32), axis=1) < DOCS).astype(F32)
        return valid, sequence * SEQ_LEN + jnp.sum(jnp.where(past, row_lengths, 0), axis=1)

    valid, doc_start = document_at(local)
    slot = jnp.arange(members, dtype=jnp.int32)
    slot_diff = ((slot >> 1) & 1) * 4 + (slot & 1) * 2 + (slot >> 2)
    slot_tile = jnp.bitwise_xor(me, slot_diff)
    slot_places = (slot_tile[:, None] * TILE + jnp.arange(TILE, dtype=jnp.int32)[None]).reshape(-1)
    valid_slot = document_at(slot_places)[0].reshape(group_tokens, 1)
    low = doc_start - first + WINDOW - lax.div(local, TILE) * TILE
    low = low.reshape(members, 1, TILE)
    valid_tiles = valid.reshape(members, 1, TILE)

    def after(t, *others):
        return lax.optimization_barrier((t,) + others)[0]

    def pin(flag, t, *others):
        return after(t, *others) if flag else t

    x_own = layer_input.reshape(TOK_DEV, D)
    cot_own = cotangent.reshape(TOK_DEV, D)

    small = jnp.concatenate(
        [ln1_gain, ln1_bias, bias_query, bias_value, bias_out, ln2_gain, ln2_bias, bias_down, bias_up]
    )
    small = plane_a2a(jnp.broadcast_to(small, (members,) + small.shape))
    small_all = column_a2a(jnp.broadcast_to(small, (nz,) + small.shape))
    bias_u = lax.dynamic_index_in_dim(small_all, me, 1, keepdims=False)[:, 8 * rows :]
    bias_u = bias_u.reshape(ff_own).astype(F32)
    small_all = small_all[:, :, : 8 * rows]
    vectors = (
        small_all.reshape(nz, nx, nh, 8, rows).transpose(3, 2, 0, 1, 4).reshape(8, D).astype(F32)
    )
    gain_one, shift_one, bias_q, bias_v, bias_o, gain_two, shift_two, bias_d = vectors
    own_cols = (head_at * nx + x_at) * width
    bias_qkv = jnp.concatenate(
        [
            lax.dynamic_slice_in_dim(bias_q, own_cols, width),
            jnp.zeros((width,), F32),
            lax.dynamic_slice_in_dim(bias_v, own_cols, width),
        ]
    )

    near = [(x, h) for x in range(nx) for h in range(nh)]
    qkv_moves = [
        (None, p * D + (h * nx + x) * width, at, p * width, width)
        for at, (x, h) in enumerate(near)
        for p in range(3)
    ]
    up_moves = [
        (None, ((h * nz + z) * nx + x) * ff_rows, at, z * ff_rows, ff_rows)
        for at, (x, h) in enumerate(near)
        for z in range(nz)
    ]
    qkv_col = plane_a2a(
        rows_kernel(w_qkv, (members, rows, 3 * width), BF, qkv_moves, "qkv_split")
    )
    up_col = plane_a2a(
        after(rows_kernel(w_up, (members, rows, ff_own), BF, up_moves, "up_split"), qkv_col)
    )
    out_cols = w_out.reshape(rows, members, D // members).transpose(1, 0, 2)
    if F["split"]:
        first_z = gather_z(qkv_col)
        out_z = gather_z(after(w_out, first_z))
        up_after = out_z
    else:
        first_z = gather_z(jnp.concatenate([qkv_col, out_cols], axis=2))
        up_after = first_z
    if not F["uph"]:
        up_z = gather_z(after(up_col, up_after))
        down_w = gather_z(pin(F["agd"], w_down, up_z)).reshape(ff_own, D)

    by_z = (nz, nx, nh, rows)

    order = column_rows(nz, nx, nh, rows)
    half_z = nz // 2
    if F["split"]:
        halves = out_z.reshape(2, half_z, rows, D)
    else:
        halves = first_z[:, :, :, 3 * width :].transpose(0, 2, 1, 3).reshape(2, half_z, rows, D)
    mine = jnp.where(x_at == 0, halves[0], halves[1])
    theirs = to_x(jnp.where(x_at == 0, halves[1], halves[0]))
    low_half = jnp.where(x_at == 0, mine, theirs)
    high_half = jnp.where(x_at == 0, theirs, mine)
    out_w = jnp.stack([low_half, high_half], axis=1).reshape(width, D)

    rows_in = x_own.astype(F32)
    normed_in, inv_in = normalize(rows_in)

    def whole(arrays):
        return [(t, 0) for t in arrays]

    def in_plane(array, weights, body, name, relay):
        def side(at):
            first = at * members // 2
            return token_kernel(
                [((array,), (first + i) * TILE) for i in range(members // 2)],
                [weights],
                [],
                [(D, BF, True)],
                body,
                name=name,
            )

        other = side(1)
        return scatter_start(side(0), other, relay)

    def times(x, at, w, e):
        return (jnp.dot(x, w[0][...], preferred_element_type=F32).astype(BF),)

    def times_t(x, at, w, e):
        return (lax.dot_general(x, w[0][...], COLS, preferred_element_type=F32).astype(BF),)

    def qkv_body(x, at, w, e):
        normed = normalize(x.astype(F32))[0]
        lowered = (normed * e[0][...] + e[1][...]).astype(BF)
        return (jnp.dot(lowered, w[0][...], preferred_element_type=F32) + e[2][...]).astype(BF), lowered

    x_tiles = gather_plane(pin(F['x1'], x_own, small), F['g2x'])
    if F['cot'] == 0:
        cot_tiles = gather_plane(after(cot_own, *x_tiles[:4]), F['g2c'])
    if F['cot'] == 3:
        cot_tiles = gather_plane(cot_own, F['g2c'])
    if F['cotk'] and F['cot'] in (0, 3):
        x_tiles = list(after(tuple(x_tiles), *(cot_tiles if F['cotk'] == 2 else cot_tiles[:4])))
    x_tiles = list(pin(F['upc'], tuple(x_tiles), up_col))
    qkv, ln1 = token_kernel(
        whole(x_tiles),
        [(first_z, order, rows, 3 * width)],
        [
            gain_one.reshape(1, D),
            shift_one.reshape(1, D),
            bias_qkv.reshape(1, -1),
        ],
        [(3 * width, BF, False), (D, BF, False)],
        qkv_body,
        name="qkv_fwd",
    )
    qkv = qkv.reshape(members, TILE, 3 * width)
    kv = qkv[:, :, width:].reshape(2, 2, 2, TILE, 2 * width)
    kv = jnp.where(x_at == 0, kv[:, 1], kv[:, 0]).reshape(HALO, TILE, 2 * width)
    halo = lax.ppermute(kv, "blk", [(b, b + nx) for b in range(nb - nx)])
    if F["cot"] in (1, 2):
        cot_tiles = gather_plane(after(cot_own, qkv if F["cot"] == 1 else halo), F["g2c"])
    halo = pin(F["cotb"], halo, *cot_tiles[:4])
    if F["uph"]:
        up_z = gather_z(after(up_col, up_after, halo))
        down_w = gather_z(pin(F["agd"], w_down, up_z)).reshape(ff_own, D)
    ctx, lse_high = attention_call(
        attn_fwd_kernel, False, scalars, qkv, None, [low, valid_tiles], heads, None
    )
    ctx, lse_low = attention_call(
        attn_fwd_kernel, True, scalars, qkv, halo, [low, valid_tiles], heads, ctx
    )
    ctx = ctx.reshape(group_tokens, width)
    ctx = pin(F['cotctx'], ctx, *cot_tiles[:4])
    half = group_tokens // 2
    attn_sent, attn_kept = in_plane(ctx, (out_w, [(0, 0)], width, D), times, "out_fwd", F["s2a"])

    def collected(tiles):
        kept = token_kernel(whole(tiles), [], [], [], lambda *_: (), keep=True, name="collect")
        return kept[0]

    if F["gdp"]:
        cot = collected(pin(F["colp"], tuple(cot_tiles), *attn_sent))
    attn_sum = scatter_end(attn_sent, attn_kept)
    if F["gdp"] and F["colp"]:
        attn_sum = after(attn_sum, cot)
    middle = rows_in + (attn_sum + bias_o)
    normed_mid, inv_mid = normalize(middle)
    ln2_own = (normed_mid * gain_two + shift_two).astype(BF)

    def up_body(x, at, w, e):
        v = jnp.dot(x, w[0][...], preferred_element_type=F32) + e[0][...]
        squared = v * v
        t = jnp.tanh(v * (0.7978845608028654 + 0.7978845608028654 * 0.044715 * squared))
        half_up = 0.5 + 0.5 * t
        slope = half_up + (0.5 * v) * (1.0 - t * t) * (
            0.7978845608028654 + 3.0 * 0.7978845608028654 * 0.044715 * squared
        )
        return (v * half_up).astype(BF), slope.astype(BF)

    active, up_slope, ln2 = token_kernel(
        whole(gather_plane(ln2_own, F['g2l'])),
        [(up_z, order, rows, ff_own)],
        [bias_u.reshape(1, ff_own)],
        [(ff_own, BF, False), (ff_own, BF, False)],
        up_body,
        keep=True,
        name="up_fwd",
    )

    cot_full = cot_own.astype(F32)
    def down_body(x, at, w, e):
        d_act = lax.dot_general(x, w[0][...], COLS, preferred_element_type=F32)
        d_pre = (d_act * w[2][at, :].astype(F32)).astype(BF)
        part = lax.dot_general(d_pre, w[1][...], COLS, preferred_element_type=F32)
        return d_pre, part.astype(BF)

    def down_back(side):
        return token_kernel(
            whole(cot_tiles[side * members // 2 : (side + 1) * members // 2]),
            [
                (down_w, [(0, 0)], ff_own, D),
                (up_z, order, rows, ff_own),
                (up_slope, [(side * half, 0)], half, ff_own),
            ],
            [],
            [(ff_own, BF, False), (D, BF, True)],
            down_body,
            name="down_back",
        )

    if F["gdp"]:
        g_down = tokens_product(active, cot, "down_grad")
        up_slope = after(up_slope, g_down)
    d_up_other, *ln2_other = down_back(1)
    d_up_mine, *ln2_mine = down_back(0)
    ln2_sent, ln2_kept = scatter_start(ln2_mine, ln2_other, F['s2l'])
    d_ln2 = scatter_end(ln2_sent, ln2_kept)
    if not F["gdp"]:
        cot = collected(pin(F["gd_lo"], tuple(cot_tiles), *ln2_sent))
        g_down = tokens_product(active, cot, "down_grad")
    grad_w_down = scatter_z(g_down.reshape(nz, ff_rows, D)).astype(F32)
    d_up = jnp.concatenate([d_up_mine, d_up_other], axis=0)
    if F["gu_lo"] != 2:
        d_up = pin(F["gu_lo"] == 3, pin(F["gu_lo"] == 1, d_up, g_down), *ln2_sent)
        g_up = tokens_product(ln2, d_up, "up_grad", by_z)
        d_ln2 = pin(F["gu_hi"] == 1, d_ln2, g_up)
    d_ln2 = pin(F["gd_hi"] == 1, d_ln2, g_down)
    d_middle = cot_full + norm_back(d_ln2 * gain_two, normed_mid, inv_mid)
    d_attn_own = d_middle.astype(BF)
    if F["gu_lo"] == 2:
        g_up = tokens_product(ln2, after(d_up, d_attn_own), "up_grad", by_z)
    up_part = g_up
    up_sum = scatter_z(g_up.reshape(nz, members, rows, ff_own))
    g_up = plane_a2a(up_sum)
    grad_w_up = rows_kernel(
        g_up, (rows, FF), F32, [(m[2], m[3], m[0], m[1], m[4]) for m in up_moves], "up_join"
    )
    grad_b_up = jnp.sum(d_up.astype(F32), axis=0)
    down_sent, down_kept = in_plane(
        pin(F['df_lo'] == 1, pin(F['df_lo'] == 2, active, *ln2_sent), d_attn_own), (down_w, [(0, 0)], ff_own, D), times, "down_fwd", F["s2o"]
    )

    d_attn_tiles = gather_plane(d_attn_own, F['g2a'])
    d_attn_tiles = list(pin(F['df_hi'] == 1, pin(F['rsd'] == 1, pin(F['gd_hi'] == 2, pin(F['gu_hi'] == 2, tuple(d_attn_tiles), up_part), g_down), grad_w_down), *down_sent))

    def ctx_body(x, at, w, e):
        found = lax.dot_general(x, w[0][...], COLS, preferred_element_type=F32)
        return ((found * e[0][at, :]).astype(BF),)

    d_ctx, d_attn = token_kernel(
        whole(d_attn_tiles),
        [(out_w, [(0, 0)], width, D)],
        [valid_slot],
        [(width, BF, False)],
        ctx_body,
        keep=True,
        name="ctx_back",
    )
    down_sent = pin(F['lo_lo'], down_sent, *d_attn_tiles)
    down_moved = scatter_move(down_sent)
    down_sum = scatter_sum(down_moved, down_kept)
    output = (middle + (down_sum + bias_d)).astype(BF)
    d_ctx = d_ctx.reshape(members, TILE, width)
    d_q, d_hk, d_hv, d_k, d_v = attention_call(
        attn_bwd_kernel, True, scalars, qkv, halo, [low, d_ctx, lse_low], heads, None
    )
    def step_back(t):
        return lax.ppermute(t, "blk", [(b + nx, b) for b in range(nb - nx)])

    back = step_back(jnp.concatenate([d_hk, d_hv], axis=-1))
    g_out = tokens_product(ctx, pin(F['go_lo'], d_attn, d_hk), "out_grad")
    g_out_part = g_out
    g_out = pin(F["lo_hi"] == 4, g_out, output)
    g_out = g_out.reshape(half_z, nx, rows, D)
    g_mine = jnp.where(x_at == 0, g_out[:, 0], g_out[:, 1])
    g_theirs = to_x(jnp.where(x_at == 0, g_out[:, 1], g_out[:, 0]))
    g_out = jnp.concatenate(
        [jnp.where(x_at == 0, g_mine, g_theirs), jnp.where(x_at == 0, g_theirs, g_mine)], axis=0
    )
    grad_w_out = scatter_z(pin(F['outh'], g_out, back)).astype(F32)
    d_q = pin(F["go_hi"], d_q, g_out_part)
    d_q = pin(F["lo_hi"] == 1, d_q, output)
    d_q = pin(F["df_hi"] == 2, d_q, *down_sent)
    d_q = pin(F["rsd"] == 2, d_q, grad_w_down)
    d_q = pin(F["rsu"] == 2, d_q, up_sum)
    d_q, d_k, d_v = attention_call(
        attn_bwd_kernel, False, scalars, qkv, None, [low, d_ctx, lse_high, d_k, d_v], heads, d_q
    )
    d_k = pin(F["gkv"], d_k, g_out)
    d_k = pin(F["lo_hi"] == 2, d_k, output)
    x_row = x_at.reshape(1).astype(jnp.int32)
    d_proj = join_grads(x_row, d_q, d_k, d_v, back).reshape(group_tokens, 3 * width)
    d_proj = pin(F["rso"] == 2, d_proj, grad_w_out)
    d_full = pin(F["rso"] == 3, d_proj, grad_w_out)
    d_full = pin(F["rsd"] == 3, pin(F["rsu"] == 3, d_full, up_sum), grad_w_down)
    d_back = pin(F["lo_hi"] == 3, d_proj, *(down_moved if F["arr"] else (output,)))
    d_back = pin(F["rsd"] == 4, d_back, grad_w_down)
    d_back = pin(F["rsu"] == 4, d_back, up_sum)
    d_back = pin(F["rso"] == 4, d_back, grad_w_out)
    d_back = pin(F["upj"], d_back, grad_w_up)
    qkv_weight = (first_z, order, rows, 3 * width)
    if F["gqr"]:
        ln1_sent, ln1_kept = in_plane(d_back, qkv_weight, times_t, "qkv_back", F["s2i"])
        d_full = after(d_full, *ln1_sent)
    g_qkv_part = tokens_product(ln1, d_full, "qkv_grad", by_z)
    if not F["gqr"]:
        d_back = pin(F["gq"], d_back, g_qkv_part)
        ln1_sent, ln1_kept = in_plane(d_back, qkv_weight, times_t, "qkv_back", F["s2i"])
    g_qkv = plane_a2a(scatter_z(g_qkv_part.reshape(nz, members, rows, 3 * width)))
    grad_w_qkv = rows_kernel(
        g_qkv, (rows, 3 * D), F32, [(m[2], m[3], m[0], m[1], m[4]) for m in qkv_moves], "qkv_join"
    )
    d_ln1 = scatter_end(ln1_sent, ln1_kept)
    grad_input = d_middle + norm_back(d_ln1 * gain_one, normed_in, inv_in)

    def placed(t):
        return lax.dynamic_update_slice_in_dim(jnp.zeros((D,), F32), t, own_cols, 0)

    sums = jnp.stack(
        [
            jnp.sum(d_ln1 * normed_in, axis=0),
            jnp.sum(d_ln1, axis=0),
            placed(jnp.sum(d_proj[:, :width].astype(F32), axis=0)),
            placed(jnp.sum(d_proj[:, 2 * width :].astype(F32), axis=0)),
            jnp.sum(d_attn_own.astype(F32), axis=0),
            jnp.sum(d_ln2 * normed_mid, axis=0),
            jnp.sum(d_ln2, axis=0),
            jnp.sum(cot_full, axis=0),
        ]
    )
    sums = sums.reshape(8, nh, nz, nx, rows).transpose(3, 1, 2, 0, 4)
    sums = pin(F["suml"] == 1, sums, g_qkv)
    sums = jnp.sum(plane_a2a(sums.reshape(members, nz, 8 * rows)), axis=0)
    sums = jnp.concatenate([sums, grad_b_up.reshape(nz, ff_rows)], axis=1)
    sums = jnp.sum(
        column_a2a(pin(F["suml"] == 2, sums, grad_w_qkv)),
        axis=0,
    )
    vec = sums[: 8 * rows].reshape(8, rows)
    return (
        output.reshape(1, TOK_DEV, D),
        grad_input.reshape(1, TOK_DEV, D),
        vec[0],
        vec[1],
        grad_w_qkv,
        vec[2],
        vec[3],
        grad_w_out,
        vec[4],
        vec[5],
        vec[6],
        grad_w_up,
        sums[8 * rows :],
        grad_w_down,
        vec[7],
    )


def solution(mesh):
    split = P(("head", "blk"))
    wide = P(("head", "blk"), None)
    tokens = P("blk", "head", None)
    return jax.shard_map(
        shards,
        mesh=mesh,
        in_specs=(
            tokens, P(), split, split, wide, split, split, wide, split, split, split, wide, split, wide, split, tokens,
        ),
        out_specs=(
            tokens, tokens, split, split, wide, split, split, wide, split, split, split, wide, split, wide, split,
        ),
        check_vma=False,
    )
```

```python
import functools

import jax
import jax.numpy as jnp
from jax import lax
from jax.experimental import pallas as pl
from jax.experimental.pallas import tpu as pltpu
from jax.sharding import PartitionSpec as P

D = 2048
HEADS = 16
HEAD_DIM = 128
FF = 8192
TOK_DEV = 256
WINDOW = 1024
SEQ_LEN = 8192
DOCS = 4

EPS = 1e-05
NEG = -1e30
BF = jnp.bfloat16
F32 = jnp.float32
ROWS = (((0,), (0,)), ((), ()))
COLS = (((1,), (1,)), ((), ()))

TILE = 256
HALO = WINDOW // TILE
SPAN = WINDOW + TILE
VMEM = 48 * 1024 * 1024
F = dict(x1=0, cot=1, cotk=1, cotctx=1, cotb=0, gd_lo=1, gd_hi=2, gu_lo=1, gu_hi=0, rsd=1, rsu=4, rso=0, df_lo=0, df_hi=2, lo_lo=1, lo_hi=3, go_lo=1, go_hi=1, gkv=1, hsplit=1, gq=0, agd=1, upc=1, g2x=0, g2c=1, g2l=1, g2a=0, s2a=1, s2l=0, s2o=0, s2i=1, suml=2, split=0, gqr=0, upj=1, gdp=1, colp=0, uph=0, outh=0, arr=0)
COST = dict(qkv_fwd=20, out_fwd=3, up_fwd=0, down_back=0, collect=20, down_grad=20, up_grad=1, down_fwd=0, ctx_back=20, out_grad=0, qkv_grad=8, qkv_back=20, attn_fwd_low=1, attn_fwd_high=20, attn_bwd_low=20, attn_bwd_high=8, qkv_split=8, up_split=3, up_join=3, qkv_join=0, join_grads=0)


def cost_of(name):
    flops = int(COST[name] * 1e9)
    return pl.CostEstimate(flops=flops, bytes_accessed=4096, transcendentals=0)


def normalize(values):
    center = values - jnp.mean(values, axis=-1, keepdims=True)
    inv_scale = lax.rsqrt(jnp.mean(center * center, axis=-1, keepdims=True) + EPS)
    return (center * inv_scale, inv_scale)


def norm_back(d_hat, normed, inv_scale):
    return inv_scale * (
        d_hat
        - jnp.mean(d_hat, axis=-1, keepdims=True)
        - normed * jnp.mean(d_hat * normed, axis=-1, keepdims=True)
    )


def gelu_tanh(values):
    return (
        0.5
        * values
        * (1.0 + jnp.tanh(0.7978845608028654 * (values + 0.044715 * values * values * values)))
    )


def fill_tiles(buffer, halo_ref, own_ref, halo_slots, slots):
    if halo_ref is None:
        sources = [(own_ref, slots, tile) for tile in range(own_ref.shape[0])]
    else:
        sources = [(halo_ref, halo_slots, tile) for tile in range(HALO)]
        sources += [(own_ref, slots, tile) for tile in range(own_ref.shape[0] - HALO)]
    for at, (ref, order, tile) in enumerate(sources):
        buffer[at * TILE : (at + 1) * TILE, :] = ref[order[tile]]


def fill_bias(bias, slope):
    key = lax.broadcasted_iota(jnp.int32, (SPAN, TILE), 0)
    query = lax.broadcasted_iota(jnp.int32, (SPAN, TILE), 1)
    rel = key - WINDOW - query
    bias[...] = jnp.where((rel <= 0) & (rel > -WINDOW), slope * rel.astype(F32), NEG)


def masked_scores(q, keys, bias, low_row):
    scores = lax.dot_general(keys, q, COLS, preferred_element_type=F32)
    scores = scores * HEAD_DIM ** (-0.5) + bias
    key = lax.broadcasted_iota(jnp.int32, (SPAN, TILE), 0)
    return jnp.where(key >= low_row, scores, NEG)


def attn_fwd_kernel(first, slots, halo_slots, slopes, q_ref, k_ref, v_ref, *refs):
    hk_ref, hv_ref, refs = (refs[0], refs[1], refs[3:]) if first else (None, None, refs)
    low_ref, valid_ref, ctx_ref, lse_ref, kbuf, vbuf, bias = refs
    head = pl.program_id(0)
    tile = pl.program_id(1)

    @pl.when(tile == 0)
    def _():
        fill_tiles(kbuf, hk_ref, k_ref, halo_slots, slots)
        fill_tiles(vbuf, hv_ref, v_ref, halo_slots, slots)
        fill_bias(bias, slopes[head])

    start = pl.multiple_of(tile * TILE, TILE)
    scores = masked_scores(q_ref[0], kbuf[pl.ds(start, SPAN), :], bias[...], low_ref[0])
    highest = jnp.max(scores, axis=0, keepdims=True)
    expo = jnp.exp(scores - highest)
    summed = jnp.sum(expo, axis=0, keepdims=True)
    lse_ref[0, 0] = highest + jnp.log(summed)
    context = lax.dot_general(
        vbuf[pl.ds(start, SPAN), :], expo.astype(BF), ROWS, preferred_element_type=F32
    )
    context = context * (valid_ref[0] / summed)
    ctx_ref[0] = context.T.astype(BF)


def attn_bwd_kernel(first, slots, halo_slots, slopes, q_ref, k_ref, v_ref, *refs):
    hk_ref, hv_ref, refs = (refs[0], refs[1], refs[2:]) if first else (None, None, refs)
    low_ref, dctx_ref, lse_ref = refs[:3]
    if first:
        dq_ref, dhk_ref, dhv_ref, dk_ref, dv_ref = refs[3:8]
    else:
        dk_in, dv_in, _, dq_ref, dk_ref, dv_ref = refs[3:9]
    kbuf, vbuf, bias, dkbuf, dvbuf = refs[-5:]
    head = pl.program_id(0)
    tile = pl.program_id(1)
    tiles = k_ref.shape[0]
    own = tiles - HALO
    kept = own * TILE

    @pl.when(tile == 0)
    def _():
        fill_tiles(kbuf, hk_ref, k_ref, halo_slots, slots)
        fill_tiles(vbuf, hv_ref, v_ref, halo_slots, slots)
        fill_bias(bias, slopes[head])
        if first:
            dkbuf[...] = jnp.zeros_like(dkbuf)
            dvbuf[...] = jnp.zeros_like(dvbuf)
        else:
            for buffer, start in ((dkbuf, dk_in), (dvbuf, dv_in)):
                buffer[:kept, :] = start[0]
                buffer[kept:, :] = jnp.zeros((buffer.shape[0] - kept, HEAD_DIM), F32)

    start = pl.multiple_of(tile * TILE, TILE)
    rows = pl.ds(start, SPAN)
    q = q_ref[0]
    d_ctx = dctx_ref[0]
    keys = kbuf[rows, :]
    scores = masked_scores(q, keys, bias[...], low_ref[0])
    probs = jnp.exp(scores - lse_ref[0, 0])
    d_probs = lax.dot_general(vbuf[rows, :], d_ctx, COLS, preferred_element_type=F32)
    delta = jnp.sum(probs * d_probs, axis=0, keepdims=True)
    d_scores = (probs * (d_probs - delta)).astype(BF)
    scale = HEAD_DIM ** (-0.5)
    d_query = lax.dot_general(d_scores, keys, ROWS, preferred_element_type=F32)
    dq_ref[0] = (d_query * scale).astype(BF)
    dkbuf[rows, :] += jnp.dot(d_scores, q, preferred_element_type=F32)
    dvbuf[rows, :] += jnp.dot(probs.astype(BF), d_ctx, preferred_element_type=F32)

    @pl.when(tile == pl.num_programs(1) - 1)
    def _():
        if first:
            for at in range(HALO):
                piece = slice(at * TILE, (at + 1) * TILE)
                dhk_ref[halo_slots[at]] = (dkbuf[piece, :] * scale).astype(BF)
                dhv_ref[halo_slots[at]] = dvbuf[piece, :].astype(BF)
            dk_ref[0] = dkbuf[HALO * TILE :, :]
            dv_ref[0] = dvbuf[HALO * TILE :, :]
        else:
            for at in range(tiles):
                piece = slice(at * TILE, (at + 1) * TILE)
                dk_ref[slots[at]] = dkbuf[piece, :] * scale
                dv_ref[slots[at]] = dvbuf[piece, :]


def attention_call(kernel, first, scalars, qkv, halo, rows, heads, grads):
    tiles = qkv.shape[0]
    queries = HALO if first else tiles - HALO
    base = 0 if first else HALO
    width = heads * HEAD_DIM
    block = (1, TILE, HEAD_DIM)
    whole = (tiles, TILE, HEAD_DIM)
    edge = (HALO, TILE, HEAD_DIM)
    q_s = pl.BlockSpec(block, lambda h, t, s, hs, sl: (s[t + base], 0, h))
    own_s = pl.BlockSpec(whole, lambda h, t, s, hs, sl: (0, 0, h))
    k_s = pl.BlockSpec(whole, lambda h, t, s, hs, sl: (0, 0, heads + h))
    v_s = pl.BlockSpec(whole, lambda h, t, s, hs, sl: (0, 0, 2 * heads + h))
    hk_s = pl.BlockSpec(edge, lambda h, t, s, hs, sl: (0, 0, h))
    hv_s = pl.BlockSpec(edge, lambda h, t, s, hs, sl: (0, 0, heads + h))
    row_s = pl.BlockSpec((1, 1, TILE), lambda h, t, s, hs, sl: (t + base, 0, 0))
    lse_s = pl.BlockSpec((1, 1, 1, TILE), lambda h, t, s, hs, sl: (h, t, 0, 0))
    part_s = pl.BlockSpec(
        (1, (tiles - HALO) * TILE, HEAD_DIM), lambda h, t, s, hs, sl: (h, 0, 0)
    )
    any_s = pl.BlockSpec(memory_space=pl.ANY)
    out = jax.ShapeDtypeStruct
    in_specs, args = [q_s, k_s, v_s], [qkv, qkv, qkv]
    if first:
        in_specs += [hk_s, hv_s]
        args += [halo, halo]
    forward = kernel is attn_fwd_kernel
    aliases = {}
    length = tiles * TILE
    scratch = [
        pltpu.VMEM((length, HEAD_DIM), BF),
        pltpu.VMEM((length, HEAD_DIM), BF),
        pltpu.VMEM((SPAN, TILE), F32),
    ]
    part = (heads, (tiles - HALO) * TILE, HEAD_DIM)
    if forward:
        if first:
            aliases = {3 + len(args): 0}
            in_specs += [any_s]
            args += [grads]
        in_specs += [row_s, row_s]
        out_specs = [q_s, lse_s]
        shapes = [out((tiles, TILE, width), BF), out((heads, queries, 1, TILE), F32)]
    else:
        in_specs += [row_s, q_s, lse_s]
        scratch += [pltpu.VMEM((length, HEAD_DIM), F32), pltpu.VMEM((length, HEAD_DIM), F32)]
        if first:
            out_specs = [q_s, hk_s, hk_s, part_s, part_s]
            shapes = [out((tiles, TILE, width), BF)] + [out((HALO, TILE, width), BF)] * 2
            shapes += [out(part, F32)] * 2
        else:
            in_specs += [part_s, part_s, any_s]
            aliases = {3 + len(args) + len(rows): 0}
            out_specs = [q_s, own_s, own_s]
            shapes = [out((tiles, TILE, width), BF)] + [out((tiles, TILE, width), F32)] * 2
            rows = list(rows) + [grads]
    return pl.pallas_call(
        functools.partial(kernel, first),
        grid_spec=pltpu.PrefetchScalarGridSpec(
            num_scalar_prefetch=3,
            grid=(heads, queries),
            in_specs=in_specs,
            out_specs=out_specs,
            scratch_shapes=scratch,
        ),
        out_shape=shapes,
        input_output_aliases=aliases,
        compiler_params=pltpu.CompilerParams(vmem_limit_bytes=VMEM),
        cost_estimate=cost_of(("attn_fwd" if forward else "attn_bwd") + ("_low" if first else "_high")),
        name=("attn_fwd" if forward else "attn_bwd") + ("_low" if first else "_high"),
    )(*scalars, *args, *rows)


def column_rows(z_count, x_count, h_count, rows):
    return [
        ((z, x * h_count + h), ((h * z_count + z) * x_count + x) * rows)
        for z in range(z_count)
        for x in range(x_count)
        for h in range(h_count)
    ]


def token_kernel(pieces, weights, extras, outs, body, keep=False, name=None):
    count = len(pieces)
    wide, kind = pieces[0][0][0].shape[1], pieces[0][0][0].dtype
    parts = [
        (at * TILE + i * (TILE // len(arrays)), TILE // len(arrays), row, at)
        for at, (arrays, row) in enumerate(pieces)
        for i in range(len(arrays))
    ]
    n_t = len(parts)
    n_w, n_e, n_o = len(weights), len(extras), len(outs)
    places = []
    out_shapes = []
    for cols, dtype, apart in list(outs) + ([(wide, kind, False)] if keep else []):
        places.append(len(out_shapes))
        shape = jax.ShapeDtypeStruct((TILE if apart else count * TILE, cols), dtype)
        out_shapes += [shape] * (count if apart else 1)
    n_out = len(out_shapes)

    def kernel(*refs):
        tile_refs = refs[:n_t]
        w_refs = refs[n_t : n_t + n_w]
        e_refs = refs[n_t + n_w : n_t + n_w + n_e]
        refs = refs[n_t + n_w + n_e :]
        o_refs = refs[:n_out]
        refs = refs[n_out:]
        x_buf, w_bufs, o_bufs = refs[0], refs[1 : 1 + n_w], refs[1 + n_w : 1 + n_w + n_o]
        x_sem, w_sem, o_sem = refs[1 + n_w + n_o :]
        for at in range(n_w):
            _, moves, rows, cols = weights[at]
            for lead, row in moves:
                if isinstance(lead, int):
                    source = w_refs[at].at[lead : lead + rows]
                else:
                    source = w_refs[at].at[lead + (slice(None), slice(0, cols))]
                pltpu.make_async_copy(
                    source,
                    w_bufs[at].at[row : row + rows],
                    w_sem.at[at],
                ).start()
        for i, (place, size, row, at) in enumerate(parts):
            pltpu.make_async_copy(
                tile_refs[i].at[row : row + size], x_buf.at[place : place + size], x_sem.at[at]
            ).start()
        for at in range(n_w):
            pltpu.make_async_copy(w_bufs[at], w_bufs[at], w_sem.at[at]).wait()

        def rows_of(at):
            return pl.ds(pl.multiple_of(at * TILE, TILE), TILE)

        bufs = list(o_bufs) + ([x_buf] if keep else [])

        def step(at, carry):
            rows = rows_of(at)
            pltpu.make_async_copy(x_buf.at[rows], x_buf.at[rows], x_sem.at[at]).wait()
            found = body(x_buf[rows, :], rows, w_bufs, e_refs)
            for i in range(n_o):
                o_bufs[i][rows, :] = found[i]
            for i in range(len(bufs)):
                if i < n_o and outs[i][2]:
                    for own in range(count):

                        @pl.when(at == own)
                        def _():
                            pltpu.make_async_copy(
                                bufs[i].at[rows], o_refs[places[i] + own], o_sem.at[i, at]
                            ).start()

                else:
                    pltpu.make_async_copy(
                        bufs[i].at[rows], o_refs[places[i]].at[rows], o_sem.at[i, at]
                    ).start()
            return carry

        lax.fori_loop(0, count, step, 0)

        def finish(at, carry):
            rows = rows_of(at)
            for i in range(len(bufs)):
                pltpu.make_async_copy(bufs[i].at[rows], bufs[i].at[rows], o_sem.at[i, at]).wait()
            return carry

        lax.fori_loop(0, count, finish, 0)

    any_spec = pl.BlockSpec(memory_space=pltpu.HBM)
    w_shapes = [(len(moves) * rows, cols) for _, moves, rows, cols in weights]
    return pl.pallas_call(
        kernel,
        in_specs=[any_spec] * (n_t + n_w) + [pl.BlockSpec(memory_space=pltpu.VMEM)] * n_e,
        out_specs=[any_spec] * n_out,
        out_shape=out_shapes,
        scratch_shapes=[
            pltpu.VMEM((count * TILE, wide), kind),
            *[pltpu.VMEM(shape, BF) for shape in w_shapes],
            *[pltpu.VMEM((count * TILE, c), t) for c, t, _ in outs],
            pltpu.SemaphoreType.DMA((count,)),
            pltpu.SemaphoreType.DMA((max(n_w, 1),)),
            pltpu.SemaphoreType.DMA((n_o + 1, count)),
        ],
        compiler_params=pltpu.CompilerParams(vmem_limit_bytes=VMEM),
        cost_estimate=cost_of(name),
        name=name,
    )(*[t for p in pieces for t in p[0]], *[w[0] for w in weights], *extras)


def tokens_product(left, right, name, order=None):
    tokens, cols = left.shape
    wide = right.shape[1]
    if order is None:
        block = min(256, cols)
        shape, out_block, place = (cols, wide), (block, wide), lambda i: (i, 0)
    else:
        z_count, x_count, h_count, rows = order
        block = cols // h_count
        shape = (z_count, x_count, h_count, rows, wide)
        out_block, place = (z_count, x_count, 1, rows, wide), lambda i: (0, 0, i, 0, 0)

    def kernel(a_ref, b_ref, o_ref):
        found = lax.dot_general(a_ref[...], b_ref[...], ROWS, preferred_element_type=F32)
        if order is None:
            o_ref[...] = found.astype(BF)
        else:
            for z in range(z_count):
                for x in range(x_count):
                    start = (z * x_count + x) * rows
                    o_ref[z, x, 0] = found[start : start + rows].astype(BF)

    return pl.pallas_call(
        kernel,
        grid=(cols // block,),
        in_specs=[
            pl.BlockSpec((tokens, block), lambda i: (0, i)),
            pl.BlockSpec((tokens, wide), lambda i: (0, 0)),
        ],
        out_specs=pl.BlockSpec(out_block, place),
        out_shape=jax.ShapeDtypeStruct(shape, BF),
        compiler_params=pltpu.CompilerParams(vmem_limit_bytes=VMEM),
        cost_estimate=cost_of(name),
        name=name,
    )(left, right)


def join_grads(x_row, d_q, d_k, d_v, back):
    tiles, _, width = d_q.shape

    def kernel(x_ref, q_ref, k_ref, v_ref, bk_ref, bv_ref, o_ref):
        second = ((pl.program_id(0) >> 1) & 1) != x_ref[0]
        o_ref[0, :, :width] = q_ref[0]
        for at, (own, back) in enumerate(((k_ref, bk_ref), (v_ref, bv_ref))):
            added = own[0] + jnp.where(second, back[0].astype(F32), 0.0)
            o_ref[0, :, (1 + at) * width : (2 + at) * width] = added.astype(BF)

    tile = pl.BlockSpec((1, TILE, width), lambda i, x: (i, 0, 0))
    edge_k = pl.BlockSpec((1, TILE, width), lambda i, x: ((i >> 2) * 2 + (i & 1), 0, 0))
    edge_v = pl.BlockSpec((1, TILE, width), lambda i, x: ((i >> 2) * 2 + (i & 1), 0, 1))
    return pl.pallas_call(
        kernel,
        grid_spec=pltpu.PrefetchScalarGridSpec(
            num_scalar_prefetch=1,
            grid=(tiles,),
            in_specs=[tile, tile, tile, edge_k, edge_v],
            out_specs=pl.BlockSpec((1, TILE, 3 * width), lambda i, x: (i, 0, 0)),
        ),
        out_shape=jax.ShapeDtypeStruct((tiles, TILE, 3 * width), BF),
        compiler_params=pltpu.CompilerParams(vmem_limit_bytes=VMEM),
        cost_estimate=cost_of("join_grads"),
        name="join_grads",
    )(x_row, d_q, d_k, d_v, back, back)


def rows_kernel(array, shape, dtype, moves, name):
    def kernel(a_ref, o_ref):
        for a_lead, a_col, o_lead, o_col, cols in moves:
            source, target = slice(a_col, a_col + cols), slice(o_col, o_col + cols)
            found = a_ref[:, source] if a_lead is None else a_ref[a_lead, :, source]
            if o_lead is None:
                o_ref[:, target] = found.astype(dtype)
            else:
                o_ref[o_lead, :, target] = found.astype(dtype)

    return pl.pallas_call(
        kernel,
        in_specs=[pl.BlockSpec(memory_space=pltpu.VMEM)],
        out_specs=pl.BlockSpec(memory_space=pltpu.VMEM),
        out_shape=jax.ShapeDtypeStruct(shape, dtype),
        compiler_params=pltpu.CompilerParams(vmem_limit_bytes=VMEM),
        cost_estimate=cost_of(name),
        name=name,
    )(array)


def shards(
    layer_input,
    lengths,
    ln1_gain,
    ln1_bias,
    w_qkv,
    bias_query,
    bias_value,
    w_out,
    bias_out,
    ln2_gain,
    ln2_bias,
    w_up,
    bias_up,
    w_down,
    bias_down,
    cotangent,
):
    nh = lax.axis_size("head")
    nb = lax.axis_size("blk")
    nx = 2
    nz = nb // nx
    members = nx * nh
    rows = D // (nh * nb)
    ff_rows = FF // (nh * nb)
    ff_own = nz * ff_rows
    heads = HEADS // members
    width = heads * HEAD_DIM
    head_at = lax.axis_index("head")
    blk_at = lax.axis_index("blk")
    x_at = lax.rem(blk_at, nx)
    z_at = lax.div(blk_at, nx)
    both = ("head", "blk")
    plane = [[h * nb + z * nx + x for x in range(nx) for h in range(nh)] for z in range(nz)]
    column = [[z * nx + x for z in range(nz)] for x in range(nx)]

    def to_core(t):
        return lax.ppermute(t, "head", [(h, h ^ 1) for h in range(nh)])

    def to_y(t):
        return lax.ppermute(t, "head", [(h, h ^ 2) for h in range(nh)])

    def to_x(t):
        return lax.ppermute(t, "blk", [(b, b ^ 1) for b in range(nb)])

    def up_z(t, sources):
        pairs = [(z * nx + x, (z + 1) * nx + x) for z in sources for x in range(nx)]
        return lax.ppermute(t, "blk", pairs)

    def down_z(t, sources):
        pairs = [(z * nx + x, (z - 1) * nx + x) for z in sources for x in range(nx)]
        return lax.ppermute(t, "blk", pairs)

    def to_diag(t):
        return lax.ppermute(
            t, both, [(h * nb + b, (h ^ 2) * nb + (b ^ 1)) for h in range(nh) for b in range(nb)]
        )

    half_tile = TOK_DEV // 2

    def gather_plane(own, relay):
        if relay:
            top, bottom = own[:half_tile], own[half_tile:]
            x_top, y_bottom = to_x(top), to_y(bottom)
            x_bottom, y_top = to_x(bottom), to_y(top)
            diag = (to_y(x_top), to_x(y_bottom))
            same = [(own,), (y_top, y_bottom), (x_top, x_bottom), diag]
        else:
            same = [(own,), (to_y(own),), (to_x(own),), (to_diag(own),)]
        return same + [tuple(to_core(t) for t in arrays) for arrays in same]

    def scatter_start(mine, other, relay):
        swapped = [to_core(other[at]) for at in (3, 1, 2, 0)]
        halves = (slice(0, half_tile), slice(half_tile, TOK_DEV)) if relay else (slice(None),)
        sent = tuple(
            tuple((mine[at][h].astype(F32) + t[h].astype(F32)).astype(BF) for h in halves)
            for at, t in zip((3, 1, 2), swapped)
        )
        return lax.optimization_barrier(sent), mine[0].astype(F32) + swapped[3].astype(F32)

    def scatter_move(sent):
        if len(sent[0]) == 1:
            return to_diag(sent[0][0]), to_y(sent[1][0]), to_x(sent[2][0])

        def added(a, b):
            return (a.astype(F32) + b.astype(F32)).astype(BF)

        diag, y_part, x_part = sent
        from_x, from_y = to_x(diag[0]), to_y(diag[1])
        x_top, y_bottom = to_x(x_part[0]), to_y(y_part[1])
        y_top, x_bottom = to_y(added(y_part[0], from_x)), to_x(added(x_part[1], from_y))
        return x_top, y_top, x_bottom, y_bottom

    def scatter_sum(arrived, kept):
        if len(arrived) == 3:
            return kept + sum(t.astype(F32) for t in arrived)
        top = kept[:half_tile] + arrived[0].astype(F32) + arrived[1].astype(F32)
        bottom = kept[half_tile:] + arrived[2].astype(F32) + arrived[3].astype(F32)
        return jnp.concatenate([top, bottom], axis=0)

    def scatter_end(sent, kept):
        return scatter_sum(scatter_move(sent), kept)

    def plane_a2a(t):
        return lax.all_to_all(
            t, both, split_axis=0, concat_axis=0, tiled=True, axis_index_groups=plane
        )

    def column_a2a(t):
        return lax.all_to_all(
            t, "blk", split_axis=0, concat_axis=0, tiled=True, axis_index_groups=column
        )

    def gather_z(t):
        return lax.all_gather(t, "blk", axis=0, tiled=False, axis_index_groups=column)

    def scatter_z(t):
        return lax.psum_scatter(
            t, "blk", scatter_dimension=0, tiled=False, axis_index_groups=column
        )

    me = x_at * nh + head_at
    slots, halo_slots = [], []
    for tile in range(members):
        diff = jnp.bitwise_xor(me, tile)
        slots.append((diff & 1) * 4 + ((diff >> 2) & 1) * 2 + ((diff >> 1) & 1))
    for tile in range(HALO):
        diff = jnp.bitwise_xor(head_at, tile)
        halo_slots.append((diff & 1) * 2 + ((diff >> 1) & 1))
    slots = jnp.stack(slots).astype(jnp.int32)
    halo_slots = jnp.stack(halo_slots).astype(jnp.int32)
    head_ids = (head_at * nx + x_at) * heads + jnp.arange(heads, dtype=jnp.int32)
    slopes = 2.0 ** (-8.0 * (head_ids.astype(F32) + 1.0) / HEADS)
    scalars = (slots, halo_slots, slopes)
    group_tokens = members * TOK_DEV
    local = jnp.arange(group_tokens, dtype=jnp.int32)
    first = z_at * group_tokens

    def document_at(places):
        positions = first + places
        sequence = lax.div(positions, SEQ_LEN)
        within = positions - sequence * SEQ_LEN
        picked = sequence[:, None] == jnp.arange(lengths.shape[0], dtype=jnp.int32)[None, :]
        row_lengths = jnp.sum(jnp.where(picked[:, :, None], lengths[None, :, :], 0), axis=1)
        ends = jnp.cumsum(row_lengths, axis=1)
        past = ends <= within[:, None]
        valid = (jnp.sum(past.astype(jnp.int32), axis=1) < DOCS).astype(F32)
        return valid, sequence * SEQ_LEN + jnp.sum(jnp.where(past, row_lengths, 0), axis=1)

    valid, doc_start = document_at(local)
    slot = jnp.arange(members, dtype=jnp.int32)
    slot_diff = ((slot >> 1) & 1) * 4 + (slot & 1) * 2 + (slot >> 2)
    slot_tile = jnp.bitwise_xor(me, slot_diff)
    slot_places = (slot_tile[:, None] * TILE + jnp.arange(TILE, dtype=jnp.int32)[None]).reshape(-1)
    valid_slot = document_at(slot_places)[0].reshape(group_tokens, 1)
    low = doc_start - first + WINDOW - lax.div(local, TILE) * TILE
    low = low.reshape(members, 1, TILE)
    valid_tiles = valid.reshape(members, 1, TILE)

    def after(t, *others):
        return lax.optimization_barrier((t,) + others)[0]

    def pin(flag, t, *others):
        return after(t, *others) if flag else t

    x_own = layer_input.reshape(TOK_DEV, D)
    cot_own = cotangent.reshape(TOK_DEV, D)

    small = jnp.concatenate(
        [ln1_gain, ln1_bias, bias_query, bias_value, bias_out, ln2_gain, ln2_bias, bias_down, bias_up]
    )
    small = plane_a2a(jnp.broadcast_to(small, (members,) + small.shape))
    small_all = column_a2a(jnp.broadcast_to(small, (nz,) + small.shape))
    bias_u = lax.dynamic_index_in_dim(small_all, me, 1, keepdims=False)[:, 8 * rows :]
    bias_u = bias_u.reshape(ff_own).astype(F32)
    small_all = small_all[:, :, : 8 * rows]
    vectors = (
        small_all.reshape(nz, nx, nh, 8, rows).transpose(3, 2, 0, 1, 4).reshape(8, D).astype(F32)
    )
    gain_one, shift_one, bias_q, bias_v, bias_o, gain_two, shift_two, bias_d = vectors
    own_cols = (head_at * nx + x_at) * width
    bias_qkv = jnp.concatenate(
        [
            lax.dynamic_slice_in_dim(bias_q, own_cols, width),
            jnp.zeros((width,), F32),
            lax.dynamic_slice_in_dim(bias_v, own_cols, width),
        ]
    )

    near = [(x, h) for x in range(nx) for h in range(nh)]
    qkv_moves = [
        (None, p * D + (h * nx + x) * width, at, p * width, width)
        for at, (x, h) in enumerate(near)
        for p in range(3)
    ]
    up_moves = [
        (None, ((h * nz + z) * nx + x) * ff_rows, at, z * ff_rows, ff_rows)
        for at, (x, h) in enumerate(near)
        for z in range(nz)
    ]
    qkv_col = plane_a2a(
        rows_kernel(w_qkv, (members, rows, 3 * width), BF, qkv_moves, "qkv_split")
    )
    up_col = plane_a2a(
        after(rows_kernel(w_up, (members, rows, ff_own), BF, up_moves, "up_split"), qkv_col)
    )
    out_cols = w_out.reshape(rows, members, D // members).transpose(1, 0, 2)
    if F["split"]:
        first_z = gather_z(qkv_col)
        out_z = gather_z(after(w_out, first_z))
        up_after = out_z
    else:
        first_z = gather_z(jnp.concatenate([qkv_col, out_cols], axis=2))
        up_after = first_z
    if not F["uph"]:
        up_z = gather_z(after(up_col, up_after))
        down_w = gather_z(pin(F["agd"], w_down, up_z)).reshape(ff_own, D)

    by_z = (nz, nx, nh, rows)

    order = column_rows(nz, nx, nh, rows)
    half_z = nz // 2
    if F["split"]:
        halves = out_z.reshape(2, half_z, rows, D)
    else:
        halves = first_z[:, :, :, 3 * width :].transpose(0, 2, 1, 3).reshape(2, half_z, rows, D)
    mine = jnp.where(x_at == 0, halves[0], halves[1])
    theirs = to_x(jnp.where(x_at == 0, halves[1], halves[0]))
    low_half = jnp.where(x_at == 0, mine, theirs)
    high_half = jnp.where(x_at == 0, theirs, mine)
    out_w = jnp.stack([low_half, high_half], axis=1).reshape(width, D)

    rows_in = x_own.astype(F32)
    normed_in, inv_in = normalize(rows_in)

    def whole(arrays):
        return [(t, 0) for t in arrays]

    def in_plane(array, weights, body, name, relay):
        def side(at):
            first = at * members // 2
            return token_kernel(
                [((array,), (first + i) * TILE) for i in range(members // 2)],
                [weights],
                [],
                [(D, BF, True)],
                body,
                name=name,
            )

        other = side(1)
        return scatter_start(side(0), other, relay)

    def times(x, at, w, e):
        return (jnp.dot(x, w[0][...], preferred_element_type=F32).astype(BF),)

    def times_t(x, at, w, e):
        return (lax.dot_general(x, w[0][...], COLS, preferred_element_type=F32).astype(BF),)

    def qkv_body(x, at, w, e):
        normed = normalize(x.astype(F32))[0]
        lowered = (normed * e[0][...] + e[1][...]).astype(BF)
        return (jnp.dot(lowered, w[0][...], preferred_element_type=F32) + e[2][...]).astype(BF), lowered

    x_tiles = gather_plane(pin(F['x1'], x_own, small), F['g2x'])
    if F['cot'] == 0:
        cot_tiles = gather_plane(after(cot_own, *x_tiles[:4]), F['g2c'])
    if F['cot'] == 3:
        cot_tiles = gather_plane(cot_own, F['g2c'])
    if F['cotk'] and F['cot'] in (0, 3):
        x_tiles = list(after(tuple(x_tiles), *(cot_tiles if F['cotk'] == 2 else cot_tiles[:4])))
    x_tiles = list(pin(F['upc'], tuple(x_tiles), up_col))
    qkv, ln1 = token_kernel(
        whole(x_tiles),
        [(first_z, order, rows, 3 * width)],
        [
            gain_one.reshape(1, D),
            shift_one.reshape(1, D),
            bias_qkv.reshape(1, -1),
        ],
        [(3 * width, BF, False), (D, BF, False)],
        qkv_body,
        name="qkv_fwd",
    )
    qkv = qkv.reshape(members, TILE, 3 * width)
    kv = qkv[:, :, width:].reshape(2, 2, 2, TILE, 2 * width)
    kv = jnp.where(x_at == 0, kv[:, 1], kv[:, 0]).reshape(HALO, TILE, 2 * width)
    halo = lax.ppermute(kv, "blk", [(b, b + nx) for b in range(nb - nx)])
    if F["cot"] in (1, 2):
        cot_tiles = gather_plane(after(cot_own, qkv if F["cot"] == 1 else halo), F["g2c"])
    halo = pin(F["cotb"], halo, *cot_tiles[:4])
    if F["uph"]:
        up_z = gather_z(after(up_col, up_after, halo))
        down_w = gather_z(pin(F["agd"], w_down, up_z)).reshape(ff_own, D)
    ctx, lse_high = attention_call(
        attn_fwd_kernel, False, scalars, qkv, None, [low, valid_tiles], heads, None
    )
    ctx, lse_low = attention_call(
        attn_fwd_kernel, True, scalars, qkv, halo, [low, valid_tiles], heads, ctx
    )
    ctx = ctx.reshape(group_tokens, width)
    ctx = pin(F['cotctx'], ctx, *cot_tiles[:4])
    half = group_tokens // 2
    attn_sent, attn_kept = in_plane(ctx, (out_w, [(0, 0)], width, D), times, "out_fwd", F["s2a"])

    def collected(tiles):
        kept = token_kernel(whole(tiles), [], [], [], lambda *_: (), keep=True, name="collect")
        return kept[0]

    if F["gdp"]:
        cot = collected(pin(F["colp"], tuple(cot_tiles), *attn_sent))
    attn_sum = scatter_end(attn_sent, attn_kept)
    if F["gdp"] and F["colp"]:
        attn_sum = after(attn_sum, cot)
    middle = rows_in + (attn_sum + bias_o)
    normed_mid, inv_mid = normalize(middle)
    ln2_own = (normed_mid * gain_two + shift_two).astype(BF)

    def up_body(x, at, w, e):
        v = jnp.dot(x, w[0][...], preferred_element_type=F32) + e[0][...]
        squared = v * v
        t = jnp.tanh(v * (0.7978845608028654 + 0.7978845608028654 * 0.044715 * squared))
        half_up = 0.5 + 0.5 * t
        slope = half_up + (0.5 * v) * (1.0 - t * t) * (
            0.7978845608028654 + 3.0 * 0.7978845608028654 * 0.044715 * squared
        )
        return (v * half_up).astype(BF), slope.astype(BF)

    active, up_slope, ln2 = token_kernel(
        whole(gather_plane(ln2_own, F['g2l'])),
        [(up_z, order, rows, ff_own)],
        [bias_u.reshape(1, ff_own)],
        [(ff_own, BF, False), (ff_own, BF, False)],
        up_body,
        keep=True,
        name="up_fwd",
    )

    cot_full = cot_own.astype(F32)
    def down_body(x, at, w, e):
        d_act = lax.dot_general(x, w[0][...], COLS, preferred_element_type=F32)
        d_pre = (d_act * w[2][at, :].astype(F32)).astype(BF)
        part = lax.dot_general(d_pre, w[1][...], COLS, preferred_element_type=F32)
        return d_pre, part.astype(BF)

    def down_back(side):
        return token_kernel(
            whole(cot_tiles[side * members // 2 : (side + 1) * members // 2]),
            [
                (down_w, [(0, 0)], ff_own, D),
                (up_z, order, rows, ff_own),
                (up_slope, [(side * half, 0)], half, ff_own),
            ],
            [],
            [(ff_own, BF, False), (D, BF, True)],
            down_body,
            name="down_back",
        )

    if F["gdp"]:
        g_down = tokens_product(active, cot, "down_grad")
        up_slope = after(up_slope, g_down)
    d_up_other, *ln2_other = down_back(1)
    d_up_mine, *ln2_mine = down_back(0)
    ln2_sent, ln2_kept = scatter_start(ln2_mine, ln2_other, F['s2l'])
    d_ln2 = scatter_end(ln2_sent, ln2_kept)
    if not F["gdp"]:
        cot = collected(pin(F["gd_lo"], tuple(cot_tiles), *ln2_sent))
        g_down = tokens_product(active, cot, "down_grad")
    grad_w_down = scatter_z(g_down.reshape(nz, ff_rows, D)).astype(F32)
    d_up = jnp.concatenate([d_up_mine, d_up_other], axis=0)
    if F["gu_lo"] != 2:
        d_up = pin(F["gu_lo"] == 3, pin(F["gu_lo"] == 1, d_up, g_down), *ln2_sent)
        g_up = tokens_product(ln2, d_up, "up_grad", by_z)
        d_ln2 = pin(F["gu_hi"] == 1, d_ln2, g_up)
    d_ln2 = pin(F["gd_hi"] == 1, d_ln2, g_down)
    d_middle = cot_full + norm_back(d_ln2 * gain_two, normed_mid, inv_mid)
    d_attn_own = d_middle.astype(BF)
    if F["gu_lo"] == 2:
        g_up = tokens_product(ln2, after(d_up, d_attn_own), "up_grad", by_z)
    up_part = g_up
    up_sum = scatter_z(g_up.reshape(nz, members, rows, ff_own))
    g_up = plane_a2a(up_sum)
    grad_w_up = rows_kernel(
        g_up, (rows, FF), F32, [(m[2], m[3], m[0], m[1], m[4]) for m in up_moves], "up_join"
    )
    grad_b_up = jnp.sum(d_up.astype(F32), axis=0)
    down_sent, down_kept = in_plane(
        pin(F['df_lo'] == 1, pin(F['df_lo'] == 2, active, *ln2_sent), d_attn_own), (down_w, [(0, 0)], ff_own, D), times, "down_fwd", F["s2o"]
    )

    d_attn_tiles = gather_plane(d_attn_own, F['g2a'])
    d_attn_tiles = list(pin(F['df_hi'] == 1, pin(F['rsd'] == 1, pin(F['gd_hi'] == 2, pin(F['gu_hi'] == 2, tuple(d_attn_tiles), up_part), g_down), grad_w_down), *down_sent))

    def ctx_body(x, at, w, e):
        found = lax.dot_general(x, w[0][...], COLS, preferred_element_type=F32)
        return ((found * e[0][at, :]).astype(BF),)

    d_ctx, d_attn = token_kernel(
        whole(d_attn_tiles),
        [(out_w, [(0, 0)], width, D)],
        [valid_slot],
        [(width, BF, False)],
        ctx_body,
        keep=True,
        name="ctx_back",
    )
    down_sent = pin(F['lo_lo'], down_sent, *d_attn_tiles)
    down_moved = scatter_move(down_sent)
    down_sum = scatter_sum(down_moved, down_kept)
    output = (middle + (down_sum + bias_d)).astype(BF)
    d_ctx = d_ctx.reshape(members, TILE, width)
    d_q, d_hk, d_hv, d_k, d_v = attention_call(
        attn_bwd_kernel, True, scalars, qkv, halo, [low, d_ctx, lse_low], heads, None
    )
    def step_back(t):
        return lax.ppermute(t, "blk", [(b + nx, b) for b in range(nb - nx)])

    back = step_back(jnp.concatenate([d_hk, d_hv], axis=-1))
    g_out = tokens_product(ctx, pin(F['go_lo'], d_attn, d_hk), "out_grad")
    g_out_part = g_out
    g_out = pin(F["lo_hi"] == 4, g_out, output)
    g_out = g_out.reshape(half_z, nx, rows, D)
    g_mine = jnp.where(x_at == 0, g_out[:, 0], g_out[:, 1])
    g_theirs = to_x(jnp.where(x_at == 0, g_out[:, 1], g_out[:, 0]))
    g_out = jnp.concatenate(
        [jnp.where(x_at == 0, g_mine, g_theirs), jnp.where(x_at == 0, g_theirs, g_mine)], axis=0
    )
    grad_w_out = scatter_z(pin(F['outh'], g_out, back)).astype(F32)
    d_q = pin(F["go_hi"], d_q, g_out_part)
    d_q = pin(F["lo_hi"] == 1, d_q, output)
    d_q = pin(F["df_hi"] == 2, d_q, *down_sent)
    d_q = pin(F["rsd"] == 2, d_q, grad_w_down)
    d_q = pin(F["rsu"] == 2, d_q, up_sum)
    d_q, d_k, d_v = attention_call(
        attn_bwd_kernel, False, scalars, qkv, None, [low, d_ctx, lse_high, d_k, d_v], heads, d_q
    )
    d_k = pin(F["gkv"], d_k, g_out)
    d_k = pin(F["lo_hi"] == 2, d_k, output)
    x_row = x_at.reshape(1).astype(jnp.int32)
    d_proj = join_grads(x_row, d_q, d_k, d_v, back).reshape(group_tokens, 3 * width)
    d_proj = pin(F["rso"] == 2, d_proj, grad_w_out)
    d_full = pin(F["rso"] == 3, d_proj, grad_w_out)
    d_full = pin(F["rsd"] == 3, pin(F["rsu"] == 3, d_full, up_sum), grad_w_down)
    d_back = pin(F["lo_hi"] == 3, d_proj, *(down_moved if F["arr"] else (output,)))
    d_back = pin(F["rsd"] == 4, d_back, grad_w_down)
    d_back = pin(F["rsu"] == 4, d_back, up_sum)
    d_back = pin(F["rso"] == 4, d_back, grad_w_out)
    d_back = pin(F["upj"], d_back, grad_w_up)
    qkv_weight = (first_z, order, rows, 3 * width)
    if F["gqr"]:
        ln1_sent, ln1_kept = in_plane(d_back, qkv_weight, times_t, "qkv_back", F["s2i"])
        d_full = after(d_full, *ln1_sent)
    g_qkv_part = tokens_product(ln1, d_full, "qkv_grad", by_z)
    if not F["gqr"]:
        d_back = pin(F["gq"], d_back, g_qkv_part)
        ln1_sent, ln1_kept = in_plane(d_back, qkv_weight, times_t, "qkv_back", F["s2i"])
    g_qkv = plane_a2a(scatter_z(g_qkv_part.reshape(nz, members, rows, 3 * width)))
    grad_w_qkv = rows_kernel(
        g_qkv, (rows, 3 * D), F32, [(m[2], m[3], m[0], m[1], m[4]) for m in qkv_moves], "qkv_join"
    )
    d_ln1 = scatter_end(ln1_sent, ln1_kept)
    grad_input = d_middle + norm_back(d_ln1 * gain_one, normed_in, inv_in)

    def placed(t):
        return lax.dynamic_update_slice_in_dim(jnp.zeros((D,), F32), t, own_cols, 0)

    sums = jnp.stack(
        [
            jnp.sum(d_ln1 * normed_in, axis=0),
            jnp.sum(d_ln1, axis=0),
            placed(jnp.sum(d_proj[:, :width].astype(F32), axis=0)),
            placed(jnp.sum(d_proj[:, 2 * width :].astype(F32), axis=0)),
            jnp.sum(d_attn_own.astype(F32), axis=0),
            jnp.sum(d_ln2 * normed_mid, axis=0),
            jnp.sum(d_ln2, axis=0),
            jnp.sum(cot_full, axis=0),
        ]
    )
    sums = sums.reshape(8, nh, nz, nx, rows).transpose(3, 1, 2, 0, 4)
    sums = pin(F["suml"] == 1, sums, g_qkv)
    sums = jnp.sum(plane_a2a(sums.reshape(members, nz, 8 * rows)), axis=0)
    sums = jnp.concatenate([sums, grad_b_up.reshape(nz, ff_rows)], axis=1)
    sums = jnp.sum(
        column_a2a(pin(F["suml"] == 2, sums, grad_w_qkv)),
        axis=0,
    )
    vec = sums[: 8 * rows].reshape(8, rows)
    return (
        output.reshape(1, TOK_DEV, D),
        grad_input.reshape(1, TOK_DEV, D),
        vec[0],
        vec[1],
        grad_w_qkv,
        vec[2],
        vec[3],
        grad_w_out,
        vec[4],
        vec[5],
        vec[6],
        grad_w_up,
        sums[8 * rows :],
        grad_w_down,
        vec[7],
    )


def solution(mesh):
    split = P(("head", "blk"))
    wide = P(("head", "blk"), None)
    tokens = P("blk", "head", None)
    return jax.shard_map(
        shards,
        mesh=mesh,
        in_specs=(
            tokens, P(), split, split, wide, split, split, wide, split, split, split, wide, split, wide, split, tokens,
        ),
        out_specs=(
            tokens, tokens, split, split, wide, split, split, wide, split, split, split, wide, split, wide, split,
        ),
        check_vma=False,
    )
```
